32 devices in a mesh: band: 2 (over x), ingest: 16 (over z, y, core).
Axes of the slice: x: 2, y: 2, z: 4, core: 2. Of those that a mesh axis runs over, the one named last changes fastest.
Arguments:
- voltages: int32 [1024, 2, 2, 45056], P(('band', 'ingest')), parts along dimension 0, may hold values from -127 to 127
- taps: float32 [4, 4096], replicated, may hold values from -3 to 3
- station_gain: float32 [512], P('ingest'), may hold values from 0.5 to 2
- station_order: int32 [512], replicated, may hold values from 0 to 511, each once
Outputs:
- visibilities: bfloat16 [64, 36, 2, 128, 128], P(('band', 'ingest')), parts along dimension 0
The draws below stay inside these ranges and needn't reach their ends.
There are 2 independent parts, one for each index of `band`. The reference program is written for one: setup_inputs(seed, part) draws one part's arguments, and reference() takes and returns one part's arrays. A program takes and returns all parts, laid end to end along the dimension named above; an argument that names none is the same for every part. Nothing has to cross between parts.
Inputs may be any that keep to these rules, and one draw needn't show every extreme that they name: `station_order`: a permutation of the stations.
All inputs are finite; a program needn't handle non-finite values.
Results may differ from the reference program's by a relative error of at most 0.0052.
Values may be sent and summed in bfloat16 or wider, within the bound.
No kernel may reach another device: no remote copies, remote signals or barrier semaphores. Data moves between devices by JAX's collectives and lax.ppermute only.
A program may use at most 128 MiB of HBM per device.

```python
import math
import jax
import jax.numpy as jnp
from jax import lax

STATIONS = 512
NCHAN = 4096
BLOCK = 64
TAPS = 4
SPECTRA = 8
AVG = 32
OUT = 32
NB = 8
SAMPLES = 45056


def with_ends(entries, stream_key, smallest, high):
    place = [jax.random.randint(jax.random.fold_in(stream_key, axis), (), 0, length) for axis, length in enumerate(entries.shape)]
    longest = entries.shape.index(max(entries.shape))
    beside = place[:longest] + [(place[longest] + 1) % entries.shape[longest]] + place[longest + 1:]
    return entries.at[tuple(place)].set(smallest).at[tuple(beside)].set(high)


def steps_of(rng, shape, split, smallest, top_value):
    gain = 1.0
    for dim, shards_of in split:
        steps = jax.random.uniform(jax.random.fold_in(jax.random.fold_in(rng, 6), dim), (shards_of,), jnp.float32, smallest / len(split), top_value / len(split))
        gain = gain * jnp.repeat(jnp.exp(steps), shape[dim] // shards_of).reshape((-1,) + (1,) * (len(shape) - 1 - dim))
    return gain


def centred(own_key, shape, deviation, bound, kind=jnp.bfloat16):
    values = jax.random.normal(own_key, shape, jnp.float32) * deviation
    return jnp.minimum(jnp.maximum(values, -bound), bound).astype(kind)


def setup_inputs(seed: int = 0, part: int = 0) -> dict:
    splits = jax.random.split(jax.random.key(seed), 5)
    part_keys = jax.random.split(jax.random.fold_in(splits[4], part), 5)
    return {
        "voltages": with_ends(jax.random.randint(part_keys[0], (STATIONS, 2, 2, SAMPLES), -127, 128), jax.random.fold_in(part_keys[0], 1), -127, 127).astype(jnp.int32),
        "taps": centred(splits[1], (TAPS, NCHAN), 0.5, 3.0, jnp.float32),
        "station_gain": jnp.clip(jnp.exp(math.log(2.0) - 1.3862944 * jax.random.uniform(splits[2], (STATIONS,), jnp.float32) ** steps_of(splits[2], (STATIONS,), ((0, 16),), -0.2, 0.2)), 0.5, 2.0),
        "station_order": jax.random.permutation(splits[3], STATIONS).astype(jnp.int32),
    }


def reference(voltages, taps, station_gain, station_order):
    samples = voltages.astype(jnp.float32).reshape(STATIONS, 2, 2, SPECTRA + TAPS - 1, NCHAN)
    filtered = jnp.zeros((STATIONS, 2, 2, SPECTRA, NCHAN), jnp.float32)
    for tap_index in range(TAPS):
        filtered = filtered + taps[tap_index] * samples[:, :, :, tap_index:tap_index + SPECTRA, :]
    spectrum = jnp.fft.fft(filtered[:, :, 0] + 1j * filtered[:, :, 1], axis=-1)
    factor = station_gain[:, None, None, None] / (64.0 * math.sqrt(NCHAN))
    spectrum = spectrum * factor
    first = (NCHAN - OUT * AVG) // 2
    real_part = jnp.real(spectrum).astype(jnp.bfloat16)[..., first:first + OUT * AVG]
    imag_part = jnp.imag(spectrum).astype(jnp.bfloat16)[..., first:first + OUT * AVG]
    stacked = jnp.stack([real_part, imag_part], axis=2).astype(jnp.float32)
    stacked = stacked.reshape(STATIONS, 2, 2, SPECTRA, OUT, AVG)
    power = lax.optimization_barrier(jnp.mean(lax.optimization_barrier(jnp.sum(stacked * stacked, axis=2)), axis=(0, 1, 2, 4)))
    arranged = jnp.transpose(stacked, (4, 0, 1, 2, 3, 5)).reshape(OUT, STATIONS, 2, 2, SPECTRA * AVG)
    arranged = jnp.take(arranged, station_order.astype(jnp.int32), axis=1)
    inner_len = SPECTRA * AVG
    right_rows = arranged.reshape(OUT, NB, 2 * BLOCK, 2 * inner_len)
    imag_rows = jnp.concatenate([right_rows[..., inner_len:], -right_rows[..., :inner_len]], axis=-1)
    pieces = []
    for row_block in range(NB):
        lefts = jnp.stack([right_rows[:, row_block], imag_rows[:, row_block]], axis=1)
        pieces.append(jnp.einsum('oxrk,ojsk->ojxrs', lefts, right_rows[:, :row_block + 1]))
    summed = jnp.concatenate(pieces, axis=1)
    scaled = summed / (SPECTRA * AVG * power)[:, None, None, None, None]
    return scaled.astype(jnp.bfloat16)
```

```python
import functools
import math

import jax
import jax.numpy as jnp
import ml_dtypes
import numpy as np
from jax import lax
from jax.experimental import pallas as pl
from jax.experimental.pallas import tpu as pltpu
from jax.sharding import PartitionSpec as P

STATIONS = 512
NCHAN = 4096
BLOCK = 64
TAPS = 4
SPECTRA = 8
AVG = 32
OUT_DEV = 2
LANES = 128
CHUNKS = ((0, 4), (4, 4))
GROUP = 4
ROWS = 16
BF16 = jnp.bfloat16
F32 = jnp.float32
NT = (((1,), (1,)), ((), ()))


def split(values):
    high = values.astype(ml_dtypes.bfloat16)
    low = (values - high.astype(np.float64)).astype(ml_dtypes.bfloat16)
    return high, low


def tables(all_out):
    blocks = NCHAN // LANES
    angle = 2.0 * math.pi * (np.outer(np.arange(AVG), np.arange(blocks)) % blocks) / blocks
    cos, sin = np.cos(angle), np.sin(angle)
    stage = np.zeros((2, AVG, blocks, 2))
    stage[0, :, :, 0], stage[0, :, :, 1] = cos, sin
    stage[1, :, :, 0], stage[1, :, :, 1] = -sin, cos
    stage = stage.reshape(2 * AVG, 2 * blocks)
    stage = np.kron(np.eye(GROUP), stage)
    angle = 2.0 * math.pi * np.outer(np.arange(AVG), np.arange(LANES)) / NCHAN
    turn = np.stack([np.cos(angle), -np.sin(angle)]).astype(np.float32)
    first = (NCHAN - all_out * AVG) // 2
    bins = first // AVG + np.arange(all_out)
    angle = 2.0 * math.pi * (np.outer(bins, np.arange(LANES)) % LANES) / LANES
    cos, sin = np.cos(angle), np.sin(angle)
    last = np.zeros((all_out, 2, 2, LANES))
    last[:, 0, 0], last[:, 0, 1] = cos, sin
    last[:, 1, 0], last[:, 1, 1] = -sin, cos
    last = last.reshape(2 * all_out, 2 * LANES)
    return np.concatenate(split(stage)), turn, np.concatenate(split(last))


def halves(values):
    high = values.astype(BF16)
    return high, (values - high.astype(F32)).astype(BF16)


def spectra_kernel(count, gain_ref, *refs):
    frames = refs[: count + TAPS - 1]
    taps_ref, stage_ref, turn_ref, last_ref, out_ref, high_ref, low_ref, zhigh_ref, zlow_ref, held_ref = refs[count + TAPS - 1 :]
    outer, inner = pl.program_id(0), pl.program_id(1)
    wide = 2 * AVG
    for u in range(GROUP):
        for r in range(0, wide, 16):
            rows = slice(r, r + 16)
            coeffs = [taps_ref[j, rows, :] for j in range(TAPS)]
            samples = [ref[u, 0, rows, :].astype(F32) for ref in frames]
            for m in range(count):
                value = coeffs[0] * samples[m]
                for j in range(1, TAPS):
                    value = value + coeffs[j] * samples[m + j]
                high, low = halves(value)
                place = (slice(u * wide + r, u * wide + r + 16), slice(m * LANES, (m + 1) * LANES))
                high_ref[place] = high
                low_ref[place] = low
    size = GROUP * wide
    for start in range(0, count, 2):
        lanes = slice(start * LANES, (start + 2) * LANES)
        both = jnp.dot(stage_ref[...], high_ref[:, lanes], preferred_element_type=F32)
        rest = jnp.dot(stage_ref[:size, :], low_ref[:, lanes], preferred_element_type=F32)
        section = both[:size] + (both[size:] + rest)
        for u in range(GROUP):
            for m in range(start, start + 2):
                at = slice((m - start) * LANES, (m - start + 1) * LANES)
                real = section[u * wide : u * wide + AVG, at]
                imag = section[u * wide + AVG : (u + 1) * wide, at]
                turn_real, turn_imag = turn_ref[0], turn_ref[1]
                row = slice((u * count + m) * AVG, (u * count + m + 1) * AVG)
                high, low = halves(real * turn_real - imag * turn_imag)
                zhigh_ref[row, :LANES] = high
                zlow_ref[row, :LANES] = low
                high, low = halves(real * turn_imag + imag * turn_real)
                zhigh_ref[row, LANES:] = high
                zlow_ref[row, LANES:] = low
    outs = last_ref.shape[0] // 2
    width = count * AVG
    for pair in range(GROUP // 2):
        rows = slice(pair * 2 * width, (pair + 1) * 2 * width)
        both = lax.dot_general(last_ref[...], zhigh_ref[rows, :], NT, preferred_element_type=F32)
        rest = lax.dot_general(last_ref[:outs, :], zlow_ref[rows, :], NT, preferred_element_type=F32)
        found = both[:outs] + (both[outs:] + rest)
        for p in range(2):
            factor = gain_ref[(outer * ROWS + inner * GROUP + pair * 2) // 2] * (1.0 / (64.0 * math.sqrt(NCHAN)))
            at = pl.multiple_of((inner * GROUP + pair * 2 + p) * outs, outs)
            held_ref[pl.ds(at, outs), :] = found[:, p * width : (p + 1) * width] * factor

    @pl.when(inner == ROWS // GROUP - 1)
    def _():
        for row in range(outs):
            out_ref[row] = held_ref[pl.ds(row, ROWS, stride=outs), :].astype(BF16)


def spectra(voltages, taps, station_gain, consts, start, count):
    streams = voltages.shape[0]
    stage, turn, last = consts
    outs = last.shape[0] // 2
    steps = ROWS // GROUP
    wide = 2 * AVG
    width = count * AVG
    frame_spec = [
        pl.BlockSpec((GROUP, 1, wide, LANES), functools.partial(lambda j, a, b: (a * steps + b, j, 0, 0), start + j))
        for j in range(count + TAPS - 1)
    ]
    whole = lambda shape: pl.BlockSpec(shape, lambda a, b: (0,) * len(shape))
    return pl.pallas_call(
        functools.partial(spectra_kernel, count),
        out_shape=jax.ShapeDtypeStruct((outs, streams, width), BF16),
        grid=(streams // ROWS, steps),
        in_specs=[pl.BlockSpec(memory_space=pltpu.SMEM)]
        + frame_spec
        + [whole(taps.shape), whole(stage.shape), whole(turn.shape), whole(last.shape)],
        out_specs=pl.BlockSpec((outs, ROWS, width), lambda a, b: (0, a, 0)),
        scratch_shapes=[
            pltpu.VMEM((GROUP * wide, count * LANES), BF16),
            pltpu.VMEM((GROUP * wide, count * LANES), BF16),
            pltpu.VMEM((GROUP * width, 2 * LANES), BF16),
            pltpu.VMEM((GROUP * width, 2 * LANES), BF16),
            pltpu.VMEM((ROWS * outs, width), F32),
        ],
        compiler_params=pltpu.CompilerParams(vmem_limit_bytes=40 * 2**20),
        cost_estimate=pl.CostEstimate(
            flops=streams * count * 12_000_000,
            bytes_accessed=streams * (count + TAPS - 1) * wide * LANES * 4,
            transcendentals=0,
        ),
        name="spectra",
    )(station_gain, *([voltages] * (count + TAPS - 1)), taps, stage, turn, last)


def tiles_kernel(pick_ref, *refs):
    count = len(CHUNKS)
    parts, (out_ref, held_ref) = refs[:count], refs[count:]
    rows = 2 * STATIONS
    pieces = [part[:, ri].reshape(rows, part.shape[-1]) for ri in range(2) for part in parts]
    total = jnp.zeros((8, LANES), F32)
    for piece in pieces:
        wide = piece.astype(F32)
        total = total + jnp.sum((wide * wide).reshape(rows // 8, 8, LANES), axis=0)
    power = jnp.sum(total) / (STATIONS * 2 * SPECTRA * AVG)
    scale = 1.0 / jnp.full((1, LANES), SPECTRA * AVG * power, F32)
    data = jnp.concatenate(pieces, axis=1)
    half = data.shape[1] // 2
    side = 2 * BLOCK
    tile = 0
    for b in range(STATIONS // BLOCK):
        own = slice(b * side, (b + 1) * side)
        held_ref[own, :] = jnp.dot(pick_ref[own, :], data, preferred_element_type=F32).astype(BF16)
        mine = held_ref[own, :]
        left = jnp.concatenate([mine, jnp.concatenate([mine[:, half:], -mine[:, :half]], axis=1)], axis=0)
        for c in range(b + 1):
            product = lax.dot_general(left, held_ref[c * side : (c + 1) * side, :], NT, preferred_element_type=F32)
            scaled = (product * scale).astype(BF16)
            out_ref[0, tile, 0] = scaled[:side]
            out_ref[0, tile, 1] = scaled[side:]
            tile += 1


def tiles(pick, parts):
    devices, _, own, width = parts[0].shape
    blocks = STATIONS // BLOCK
    pairs = blocks * (blocks + 1) // 2
    side = 2 * BLOCK
    part_spec = pl.BlockSpec((devices, 2, own, width), lambda o: (0, o, 0, 0))
    return pl.pallas_call(
        tiles_kernel,
        out_shape=jax.ShapeDtypeStruct((OUT_DEV, pairs, 2, side, side), BF16),
        grid=(OUT_DEV,),
        in_specs=[pl.BlockSpec(pick.shape, lambda o: (0, 0))] + [part_spec] * len(parts),
        out_specs=pl.BlockSpec((1, pairs, 2, side, side), lambda o: (o, 0, 0, 0, 0)),
        scratch_shapes=[pltpu.VMEM((2 * STATIONS, 2 * SPECTRA * AVG), BF16)],
        compiler_params=pltpu.CompilerParams(vmem_limit_bytes=40 * 2**20),
        cost_estimate=pl.CostEstimate(flops=4_500_000_000, bytes_accessed=9_000_000, transcendentals=0),
        name="tiles",
    )(pick, *parts)


def body(voltages, taps, station_gain, station_order):
    devices = lax.axis_size("ingest")
    streams = 2 * voltages.shape[0]
    blocks = NCHAN // LANES
    all_out = OUT_DEV * devices
    consts = tables(all_out)
    frames = SPECTRA + TAPS - 1
    samples = voltages.reshape(streams, 2, frames * blocks, LANES).transpose(0, 2, 1, 3)
    samples = samples.reshape(streams, frames, 2 * blocks, LANES)
    coeffs = jnp.repeat(taps.reshape(TAPS, blocks, LANES), 2, axis=1)
    parts = []
    for start, count in CHUNKS:
        packed = spectra(samples, coeffs, station_gain, consts, start, count)
        packed = packed.reshape(devices, 2 * OUT_DEV, streams, count * AVG)
        parts.append(lax.all_to_all(packed, "ingest", split_axis=0, concat_axis=0, tiled=True))
    wanted = (2 * station_order[:, None] + jnp.arange(2, dtype=jnp.int32)).reshape(-1, 1)
    pick = (wanted == jnp.arange(2 * STATIONS, dtype=jnp.int32)).astype(BF16)
    return tiles(pick, parts)


def solution(mesh):
    return jax.shard_map(
        body,
        mesh=mesh,
        in_specs=(P(("band", "ingest"), None, None, None), P(), P("ingest"), P()),
        out_specs=P(("band", "ingest"), None, None, None, None),
        check_vma=False,
    )
```

```python
import functools
import math

import jax
import jax.numpy as jnp
import ml_dtypes
import numpy as np
from jax import lax
from jax.experimental import pallas as pl
from jax.experimental.pallas import tpu as pltpu
from jax.sharding import PartitionSpec as P

STATIONS = 512
NCHAN = 4096
BLOCK = 64
TAPS = 4
SPECTRA = 8
AVG = 32
OUT_DEV = 2
LANES = 128
CHUNKS = ((0, 4), (4, 4))
GROUP = 4
ROWS = 16
BF16 = jnp.bfloat16
F32 = jnp.float32
NT = (((1,), (1,)), ((), ()))


def split(values):
    high = values.astype(ml_dtypes.bfloat16)
    low = (values - high.astype(np.float64)).astype(ml_dtypes.bfloat16)
    return high, low


def tables(all_out):
    blocks = NCHAN // LANES
    angle = 2.0 * math.pi * (np.outer(np.arange(AVG), np.arange(blocks)) % blocks) / blocks
    cos, sin = np.cos(angle), np.sin(angle)
    stage = np.zeros((2, AVG, blocks, 2))
    stage[0, :, :, 0], stage[0, :, :, 1] = cos, sin
    stage[1, :, :, 0], stage[1, :, :, 1] = -sin, cos
    stage = stage.reshape(2 * AVG, 2 * blocks)
    stage = np.kron(np.eye(GROUP), stage)
    angle = 2.0 * math.pi * np.outer(np.arange(AVG), np.arange(LANES)) / NCHAN
    turn = np.stack([np.cos(angle), -np.sin(angle)]).astype(np.float32)
    first = (NCHAN - all_out * AVG) // 2
    bins = first // AVG + np.arange(all_out)
    angle = 2.0 * math.pi * (np.outer(bins, np.arange(LANES)) % LANES) / LANES
    cos, sin = np.cos(angle), np.sin(angle)
    last = np.zeros((all_out, 2, 2, LANES))
    last[:, 0, 0], last[:, 0, 1] = cos, sin
    last[:, 1, 0], last[:, 1, 1] = -sin, cos
    last = last.reshape(2 * all_out, 2 * LANES)
    return np.concatenate(split(stage)), turn, np.concatenate(split(last))


def halves(values):
    high = values.astype(BF16)
    return high, (values - high.astype(F32)).astype(BF16)


def spectra_kernel(count, gain_ref, *refs):
    frames = refs[: count + TAPS - 1]
    taps_ref, stage_ref, turn_ref, last_ref, out_ref, coeff_ref, high_ref, low_ref, zhigh_ref, zlow_ref, held_ref = refs[count + TAPS - 1 :]
    step = pl.program_id(0)
    wide = 2 * AVG
    size = GROUP * wide
    outs = last_ref.shape[0] // 2
    width = count * AVG

    @pl.when(step == 0)
    def _():
        for j in range(TAPS):
            rows = taps_ref[pl.ds(j, AVG, stride=TAPS), :]
            for ri in range(2):
                coeff_ref[j, pl.ds(ri, AVG, stride=2), :] = rows

    def filter_group(g):
        for u in range(GROUP):
            for r in range(0, wide, 16):
                rows = slice(r, r + 16)
                coeffs = [coeff_ref[j, rows, :] for j in range(TAPS)]
                samples = [ref[g * GROUP + u, 0, rows, :].astype(F32) for ref in frames]
                for m in range(count):
                    value = coeffs[0] * samples[m]
                    for j in range(1, TAPS):
                        value = value + coeffs[j] * samples[m + j]
                    high, low = halves(value)
                    place = (g, slice(u * wide + r, u * wide + r + 16), slice(m * LANES, (m + 1) * LANES))
                    high_ref[place] = high
                    low_ref[place] = low

    def first_group(g):
        for start in range(0, count, 2):
            lanes = slice(start * LANES, (start + 2) * LANES)
            both = jnp.dot(stage_ref[...], high_ref[g, :, lanes], preferred_element_type=F32)
            rest = jnp.dot(stage_ref[:size, :], low_ref[g, :, lanes], preferred_element_type=F32)
            section = both[:size] + (both[size:] + rest)
            for u in range(GROUP):
                for m in range(start, start + 2):
                    at = slice((m - start) * LANES, (m - start + 1) * LANES)
                    real = section[u * wide : u * wide + AVG, at]
                    imag = section[u * wide + AVG : (u + 1) * wide, at]
                    turn_real, turn_imag = turn_ref[0], turn_ref[1]
                    row = slice((u * count + m) * AVG, (u * count + m + 1) * AVG)
                    high, low = halves(real * turn_real - imag * turn_imag)
                    zhigh_ref[g, row, :LANES] = high
                    zlow_ref[g, row, :LANES] = low
                    high, low = halves(real * turn_imag + imag * turn_real)
                    zhigh_ref[g, row, LANES:] = high
                    zlow_ref[g, row, LANES:] = low

    def last_group(g):
        for pair in range(GROUP // 2):
            rows = slice(pair * 2 * width, (pair + 1) * 2 * width)
            both = lax.dot_general(last_ref[...], zhigh_ref[g, rows, :], NT, preferred_element_type=F32)
            rest = lax.dot_general(last_ref[:outs, :], zlow_ref[g, rows, :], NT, preferred_element_type=F32)
            found = both[:outs] + (both[outs:] + rest)
            stream = g * GROUP + pair * 2
            factor = gain_ref[(step * ROWS + stream) // 2] * (1.0 / (64.0 * math.sqrt(NCHAN)))
            for p in range(2):
                held_ref[(stream + p) * outs : (stream + p + 1) * outs, :] = found[:, p * width : (p + 1) * width] * factor

    groups = ROWS // GROUP
    for g in range(groups + 2):
        if g < groups:
            filter_group(g)
        if 1 <= g <= groups:
            first_group(g - 1)
        if g >= 2:
            last_group(g - 2)
    for row in range(outs):
        out_ref[row] = held_ref[pl.ds(row, ROWS, stride=outs), :].astype(BF16)


def spectra(voltages, taps, station_gain, consts, start, count):
    streams = voltages.shape[0]
    stage, turn, last = consts
    outs = last.shape[0] // 2
    groups = ROWS // GROUP
    wide = 2 * AVG
    width = count * AVG
    frame_spec = [
        pl.BlockSpec((ROWS, 1, wide, LANES), functools.partial(lambda j, a: (a, j, 0, 0), start + j))
        for j in range(count + TAPS - 1)
    ]
    whole = lambda shape: pl.BlockSpec(shape, lambda a: (0,) * len(shape))
    return pl.pallas_call(
        functools.partial(spectra_kernel, count),
        out_shape=jax.ShapeDtypeStruct((outs, streams, width), BF16),
        grid=(streams // ROWS,),
        in_specs=[pl.BlockSpec(memory_space=pltpu.SMEM)]
        + frame_spec
        + [whole(taps.shape), whole(stage.shape), whole(turn.shape), whole(last.shape)],
        out_specs=pl.BlockSpec((outs, ROWS, width), lambda a: (0, a, 0)),
        scratch_shapes=[
            pltpu.VMEM((TAPS, wide, LANES), F32),
            pltpu.VMEM((groups, GROUP * wide, count * LANES), BF16),
            pltpu.VMEM((groups, GROUP * wide, count * LANES), BF16),
            pltpu.VMEM((groups, GROUP * width, 2 * LANES), BF16),
            pltpu.VMEM((groups, GROUP * width, 2 * LANES), BF16),
            pltpu.VMEM((ROWS * outs, width), F32),
        ],
        compiler_params=pltpu.CompilerParams(vmem_limit_bytes=60_000_000),
        cost_estimate=pl.CostEstimate(
            flops=streams * count * 12_000_000,
            bytes_accessed=streams * (count + TAPS - 1) * wide * LANES * 4,
            transcendentals=0,
        ),
        name="spectra",
    )(station_gain, *([voltages] * (count + TAPS - 1)), taps, stage, turn, last)


def squares(pieces):
    total = jnp.zeros((8, LANES), F32)
    for piece in pieces:
        values = piece.astype(F32)
        total = total + jnp.sum((values * values).reshape(-1, 8, LANES), axis=0)
    return total


def arrange_kernel(pick_ref, part_ref, out_ref, power_ref):
    rows = 2 * STATIONS
    pieces = [part_ref[:, ri].reshape(rows, LANES) for ri in range(2)]
    power_ref[0] = squares(pieces)
    data = jnp.concatenate(pieces, axis=1)
    for r in range(0, rows, 2 * LANES):
        own = slice(r, r + 2 * LANES)
        out_ref[0, own, :] = jnp.dot(pick_ref[own, :], data, preferred_element_type=F32).astype(BF16)


def arrange(pick, part):
    devices, _, own, width = part.shape
    rows = 2 * STATIONS
    return pl.pallas_call(
        arrange_kernel,
        out_shape=(
            jax.ShapeDtypeStruct((OUT_DEV, rows, 2 * width), BF16),
            jax.ShapeDtypeStruct((OUT_DEV, 8, LANES), F32),
        ),
        grid=(OUT_DEV,),
        in_specs=[
            pl.BlockSpec(pick.shape, lambda o: (0, 0)),
            pl.BlockSpec((devices, 2, own, width), lambda o: (0, o, 0, 0)),
        ],
        out_specs=(
            pl.BlockSpec((1, rows, 2 * width), lambda o: (o, 0, 0)),
            pl.BlockSpec((1, 8, LANES), lambda o: (o, 0, 0)),
        ),
        compiler_params=pltpu.CompilerParams(vmem_limit_bytes=40 * 2**20),
        cost_estimate=pl.CostEstimate(flops=1_100_000_000, bytes_accessed=4_000_000, transcendentals=0),
        name="arrange",
    )(pick, part)


def turned(values):
    return jnp.concatenate([values[:, LANES:], -values[:, :LANES]], axis=1)


def tiles_kernel(pick_ref, part_ref, early_ref, power_ref, out_ref, left_ref, right_ref):
    rows = 2 * STATIONS
    side = 2 * BLOCK
    blocks = STATIONS // BLOCK
    pieces = [part_ref[:, ri].reshape(rows, LANES) for ri in range(2)]
    power = jnp.sum(squares(pieces) + power_ref[0]) / (STATIONS * 2 * SPECTRA * AVG)
    scale = 1.0 / jnp.full((1, LANES), SPECTRA * AVG * power, F32)
    data = jnp.concatenate(pieces, axis=1)
    half = data.shape[1]
    for r in range(0, rows, 2 * side):
        found = jnp.dot(pick_ref[r : r + 2 * side, :], data, preferred_element_type=F32).astype(BF16)
        early = early_ref[0, r : r + 2 * side, :]
        right_ref[r : r + 2 * side, :half] = early
        right_ref[r : r + 2 * side, half:] = found
        for p in range(2):
            own = slice(p * side, (p + 1) * side)
            at = 2 * r + p * 2 * side
            left_ref[at : at + side, :half] = early[own]
            left_ref[at : at + side, half:] = found[own]
            left_ref[at + side : at + 2 * side, :half] = turned(early[own])
            left_ref[at + side : at + 2 * side, half:] = turned(found[own])
    for c in range(0, blocks, 2):
        right = right_ref[c * side : (c + 2) * side, :]
        for b in range(c, blocks):
            left = left_ref[b * 2 * side : (b + 1) * 2 * side, :]
            product = lax.dot_general(left, right, NT, preferred_element_type=F32)
            for p in range(2):
                if c + p <= b:
                    tile = b * (b + 1) // 2 + c + p
                    scaled = (product[:, p * side : (p + 1) * side] * scale).astype(BF16)
                    out_ref[0, tile, 0] = scaled[:side]
                    out_ref[0, tile, 1] = scaled[side:]


def tiles(pick, part, early, power):
    devices, _, own, width = part.shape
    blocks = STATIONS // BLOCK
    pairs = blocks * (blocks + 1) // 2
    side = 2 * BLOCK
    rows = 2 * STATIONS
    return pl.pallas_call(
        tiles_kernel,
        out_shape=jax.ShapeDtypeStruct((OUT_DEV, pairs, 2, side, side), BF16),
        grid=(OUT_DEV,),
        in_specs=[
            pl.BlockSpec(pick.shape, lambda o: (0, 0)),
            pl.BlockSpec((devices, 2, own, width), lambda o: (0, o, 0, 0)),
            pl.BlockSpec((1, rows, 2 * width), lambda o: (o, 0, 0)),
            pl.BlockSpec((1, 8, LANES), lambda o: (o, 0, 0)),
        ],
        out_specs=pl.BlockSpec((1, pairs, 2, side, side), lambda o: (o, 0, 0, 0, 0)),
        scratch_shapes=[
            pltpu.VMEM((2 * rows, 4 * width), BF16),
            pltpu.VMEM((rows, 4 * width), BF16),
        ],
        compiler_params=pltpu.CompilerParams(vmem_limit_bytes=40 * 2**20),
        cost_estimate=pl.CostEstimate(flops=4_500_000_000, bytes_accessed=9_000_000, transcendentals=0),
        name="tiles",
    )(pick, part, early, power)


def body(voltages, taps, station_gain, station_order):
    devices = lax.axis_size("ingest")
    streams = 2 * voltages.shape[0]
    blocks = NCHAN // LANES
    all_out = OUT_DEV * devices
    consts = tables(all_out)
    frames = SPECTRA + TAPS - 1
    samples = voltages.reshape(streams, 2, frames * blocks, LANES).transpose(0, 2, 1, 3)
    samples = samples.reshape(streams, frames, 2 * blocks, LANES)
    coeffs = taps.reshape(TAPS, blocks, LANES).transpose(1, 0, 2).reshape(TAPS * blocks, LANES)
    parts = []
    for start, count in CHUNKS:
        packed = spectra(samples, coeffs, station_gain, consts, start, count)
        packed = packed.reshape(devices, 2 * OUT_DEV, streams, count * AVG)
        parts.append(lax.all_to_all(packed, "ingest", split_axis=0, concat_axis=0, tiled=True))
    wanted = (2 * station_order[:, None] + jnp.arange(2, dtype=jnp.int32)).reshape(-1, 1)
    pick = (wanted == jnp.arange(2 * STATIONS, dtype=jnp.int32)).astype(BF16)
    early, power = arrange(pick, parts[0])
    return tiles(pick, parts[1], early, power)


def solution(mesh):
    return jax.shard_map(
        body,
        mesh=mesh,
        in_specs=(P(("band", "ingest"), None, None, None), P(), P("ingest"), P()),
        out_specs=P(("band", "ingest"), None, None, None, None),
        check_vma=False,
    )
```

```python
import functools
import math

import jax
import jax.numpy as jnp
import ml_dtypes
import numpy as np
from jax import lax
from jax.experimental import pallas as pl
from jax.experimental.pallas import tpu as pltpu
from jax.sharding import PartitionSpec as P

STATIONS = 512
NCHAN = 4096
BLOCK = 64
TAPS = 4
SPECTRA = 8
AVG = 32
OUT_DEV = 2
LANES = 128
CHUNKS = ((0, 4), (4, 4))
GROUP = 4
ROWS = 16
BF16 = jnp.bfloat16
F32 = jnp.float32
NT = (((1,), (1,)), ((), ()))


def split(values):
    high = values.astype(ml_dtypes.bfloat16)
    low = (values - high.astype(np.float64)).astype(ml_dtypes.bfloat16)
    return high, low


def tables(all_out):
    blocks = NCHAN // LANES
    angle = 2.0 * math.pi * (np.outer(np.arange(AVG), np.arange(blocks)) % blocks) / blocks
    cos, sin = np.cos(angle), np.sin(angle)
    stage = np.zeros((2, AVG, blocks, 2))
    stage[0, :, :, 0], stage[0, :, :, 1] = cos, sin
    stage[1, :, :, 0], stage[1, :, :, 1] = -sin, cos
    stage = stage.reshape(2 * AVG, 2 * blocks)
    stage = np.kron(np.eye(GROUP), stage)
    angle = 2.0 * math.pi * np.outer(np.arange(AVG), np.arange(LANES)) / NCHAN
    turn = np.stack([np.cos(angle), -np.sin(angle)]).astype(np.float32)
    first = (NCHAN - all_out * AVG) // 2
    bins = first // AVG + np.arange(all_out)
    angle = 2.0 * math.pi * (np.outer(bins, np.arange(LANES)) % LANES) / LANES
    cos, sin = np.cos(angle), np.sin(angle)
    last = np.zeros((all_out, 2, 2, LANES))
    last[:, 0, 0], last[:, 0, 1] = cos, sin
    last[:, 1, 0], last[:, 1, 1] = -sin, cos
    last = last.reshape(2 * all_out, 2 * LANES)
    return np.concatenate(split(stage)), turn, np.concatenate(split(last))


def halves(values):
    high = values.astype(BF16)
    return high, (values - high.astype(F32)).astype(BF16)


def spectra_kernel(count, partners, gain_ref, *refs):
    frames, refs = refs[: count + TAPS - 1], refs[count + TAPS - 1 :]
    (taps_ref, stage_ref, turn_ref, last_ref), refs = refs[:4], refs[4:]
    out_refs = refs[: max(partners, 1)]
    coeff_ref, high_ref, low_ref, zhigh_ref, zlow_ref, held_ref = refs[len(out_refs) :]
    step = pl.program_id(0)
    wide = 2 * AVG
    size = GROUP * wide
    outs = last_ref.shape[0] // 2
    width = count * AVG

    @pl.when(step == 0)
    def _():
        for j in range(TAPS):
            rows = taps_ref[pl.ds(j, AVG, stride=TAPS), :]
            for ri in range(2):
                coeff_ref[j, pl.ds(ri, AVG, stride=2), :] = rows

    def filter_group(g):
        for u in range(GROUP):
            for r in range(0, wide, 16):
                rows = slice(r, r + 16)
                coeffs = [coeff_ref[j, rows, :] for j in range(TAPS)]
                samples = [ref[g * GROUP + u, 0, rows, :].astype(F32) for ref in frames]
                for m in range(count):
                    value = coeffs[0] * samples[m]
                    for j in range(1, TAPS):
                        value = value + coeffs[j] * samples[m + j]
                    high, low = halves(value)
                    place = (g, slice(u * wide + r, u * wide + r + 16), slice(m * LANES, (m + 1) * LANES))
                    high_ref[place] = high
                    low_ref[place] = low

    def first_group(g):
        for start in range(0, count, 2):
            lanes = slice(start * LANES, (start + 2) * LANES)
            both = jnp.dot(stage_ref[...], high_ref[g, :, lanes], preferred_element_type=F32)
            rest = jnp.dot(stage_ref[:size, :], low_ref[g, :, lanes], preferred_element_type=F32)
            section = both[:size] + (both[size:] + rest)
            for u in range(GROUP):
                for m in range(start, start + 2):
                    at = slice((m - start) * LANES, (m - start + 1) * LANES)
                    real = section[u * wide : u * wide + AVG, at]
                    imag = section[u * wide + AVG : (u + 1) * wide, at]
                    turn_real, turn_imag = turn_ref[0], turn_ref[1]
                    row = slice((u * count + m) * AVG, (u * count + m + 1) * AVG)
                    high, low = halves(real * turn_real - imag * turn_imag)
                    zhigh_ref[g, row, :LANES] = high
                    zlow_ref[g, row, :LANES] = low
                    high, low = halves(real * turn_imag + imag * turn_real)
                    zhigh_ref[g, row, LANES:] = high
                    zlow_ref[g, row, LANES:] = low

    def last_group(g):
        for pair in range(GROUP // 2):
            rows = slice(pair * 2 * width, (pair + 1) * 2 * width)
            both = lax.dot_general(last_ref[...], zhigh_ref[g, rows, :], NT, preferred_element_type=F32)
            rest = lax.dot_general(last_ref[:outs, :], zlow_ref[g, rows, :], NT, preferred_element_type=F32)
            found = both[:outs] + (both[outs:] + rest)
            stream = g * GROUP + pair * 2
            factor = gain_ref[(step * ROWS + stream) // 2] * (1.0 / (64.0 * math.sqrt(NCHAN)))
            for p in range(2):
                held_ref[(stream + p) * outs : (stream + p + 1) * outs, :] = found[:, p * width : (p + 1) * width] * factor

    groups = ROWS // GROUP
    for g in range(groups + 2):
        if g < groups:
            filter_group(g)
        if 1 <= g <= groups:
            first_group(g - 1)
        if g >= 2:
            last_group(g - 2)
    if partners:
        me = lax.axis_index("ingest")
        each = outs // partners
        for k in range(partners):
            target = jnp.bitwise_xor(me, k) * each
            for q in range(each):
                out_refs[k][q] = held_ref[pl.ds(target + q, ROWS, stride=outs), :].astype(BF16)
    else:
        for row in range(outs):
            out_refs[0][row] = held_ref[pl.ds(row, ROWS, stride=outs), :].astype(BF16)


def spectra(voltages, taps, station_gain, consts, start, count, partners=0):
    streams = voltages.shape[0]
    stage, turn, last = consts
    outs = last.shape[0] // 2
    groups = ROWS // GROUP
    wide = 2 * AVG
    width = count * AVG
    frame_spec = [
        pl.BlockSpec((ROWS, 1, wide, LANES), functools.partial(lambda j, a: (a, j, 0, 0), start + j))
        for j in range(count + TAPS - 1)
    ]
    whole = lambda shape: pl.BlockSpec(shape, lambda a: (0,) * len(shape))
    pieces = max(partners, 1)
    return pl.pallas_call(
        functools.partial(spectra_kernel, count, partners),
        out_shape=[jax.ShapeDtypeStruct((outs // pieces, streams, width), BF16)] * pieces,
        grid=(streams // ROWS,),
        in_specs=[pl.BlockSpec(memory_space=pltpu.SMEM)]
        + frame_spec
        + [whole(taps.shape), whole(stage.shape), whole(turn.shape), whole(last.shape)],
        out_specs=[pl.BlockSpec((outs // pieces, ROWS, width), lambda a: (0, a, 0))] * pieces,
        scratch_shapes=[
            pltpu.VMEM((TAPS, wide, LANES), F32),
            pltpu.VMEM((groups, GROUP * wide, count * LANES), BF16),
            pltpu.VMEM((groups, GROUP * wide, count * LANES), BF16),
            pltpu.VMEM((groups, GROUP * width, 2 * LANES), BF16),
            pltpu.VMEM((groups, GROUP * width, 2 * LANES), BF16),
            pltpu.VMEM((ROWS * outs, width), F32),
        ],
        compiler_params=pltpu.CompilerParams(vmem_limit_bytes=60_000_000),
        cost_estimate=pl.CostEstimate(
            flops=streams * count * 12_000_000,
            bytes_accessed=streams * (count + TAPS - 1) * wide * LANES * 4,
            transcendentals=0,
        ),
        name="spectra",
    )(station_gain, *([voltages] * (count + TAPS - 1)), taps, stage, turn, last)


def squares(pieces):
    total = jnp.zeros((8, LANES), F32)
    for piece in pieces:
        values = piece.astype(F32)
        total = total + jnp.sum((values * values).reshape(-1, 8, LANES), axis=0)
    return total


def arrange_kernel(pick_ref, *refs):
    part_refs, (out_ref, power_ref) = refs[:-2], refs[-2:]
    rows = 2 * STATIONS
    pieces = [jnp.concatenate([part_ref[ri] for part_ref in part_refs], axis=0) for ri in range(2)]
    power_ref[0] = squares(pieces)
    data = jnp.concatenate(pieces, axis=1)
    for r in range(0, rows, 2 * LANES):
        own = slice(r, r + 2 * LANES)
        out_ref[0, own, :] = jnp.dot(pick_ref[own, :], data, preferred_element_type=F32).astype(BF16)


def arrange(pick, parts):
    _, own, width = parts[0].shape
    rows = 2 * STATIONS
    return pl.pallas_call(
        arrange_kernel,
        out_shape=(
            jax.ShapeDtypeStruct((OUT_DEV, rows, 2 * width), BF16),
            jax.ShapeDtypeStruct((OUT_DEV, 8, LANES), F32),
        ),
        grid=(OUT_DEV,),
        in_specs=[
            pl.BlockSpec(pick.shape, lambda o: (0, 0)),
        ]
        + [pl.BlockSpec((2, own, width), lambda o: (o, 0, 0))] * len(parts),
        out_specs=(
            pl.BlockSpec((1, rows, 2 * width), lambda o: (o, 0, 0)),
            pl.BlockSpec((1, 8, LANES), lambda o: (o, 0, 0)),
        ),
        compiler_params=pltpu.CompilerParams(vmem_limit_bytes=40 * 2**20),
        cost_estimate=pl.CostEstimate(flops=1_100_000_000, bytes_accessed=4_000_000, transcendentals=0),
        name="arrange",
    )(pick, *parts)


def turned(values):
    return jnp.concatenate([values[:, LANES:], -values[:, :LANES]], axis=1)


def tiles_kernel(pick_ref, part_ref, early_ref, power_ref, out_ref, left_ref, right_ref):
    rows = 2 * STATIONS
    side = 2 * BLOCK
    blocks = STATIONS // BLOCK
    pieces = [part_ref[:, ri].reshape(rows, LANES) for ri in range(2)]
    power = jnp.sum(squares(pieces) + power_ref[0]) / (STATIONS * 2 * SPECTRA * AVG)
    scale = 1.0 / jnp.full((1, LANES), SPECTRA * AVG * power, F32)
    data = jnp.concatenate(pieces, axis=1)
    half = data.shape[1]
    for r in range(0, rows, 2 * side):
        found = jnp.dot(pick_ref[r : r + 2 * side, :], data, preferred_element_type=F32).astype(BF16)
        early = early_ref[0, r : r + 2 * side, :]
        right_ref[r : r + 2 * side, :half] = early
        right_ref[r : r + 2 * side, half:] = found
        for p in range(2):
            own = slice(p * side, (p + 1) * side)
            at = 2 * r + p * 2 * side
            left_ref[at : at + side, :half] = early[own]
            left_ref[at : at + side, half:] = found[own]
            left_ref[at + side : at + 2 * side, :half] = turned(early[own])
            left_ref[at + side : at + 2 * side, half:] = turned(found[own])
    for c in range(0, blocks, 2):
        right = right_ref[c * side : (c + 2) * side, :]
        for b in range(c, blocks):
            left = left_ref[b * 2 * side : (b + 1) * 2 * side, :]
            product = lax.dot_general(left, right, NT, preferred_element_type=F32)
            for p in range(2):
                if c + p <= b:
                    tile = b * (b + 1) // 2 + c + p
                    scaled = (product[:, p * side : (p + 1) * side] * scale).astype(BF16)
                    out_ref[0, tile, 0] = scaled[:side]
                    out_ref[0, tile, 1] = scaled[side:]


def tiles(pick, part, early, power):
    devices, _, own, width = part.shape
    blocks = STATIONS // BLOCK
    pairs = blocks * (blocks + 1) // 2
    side = 2 * BLOCK
    rows = 2 * STATIONS
    return pl.pallas_call(
        tiles_kernel,
        out_shape=jax.ShapeDtypeStruct((OUT_DEV, pairs, 2, side, side), BF16),
        grid=(OUT_DEV,),
        in_specs=[
            pl.BlockSpec(pick.shape, lambda o: (0, 0)),
            pl.BlockSpec((devices, 2, own, width), lambda o: (0, o, 0, 0)),
            pl.BlockSpec((1, rows, 2 * width), lambda o: (o, 0, 0)),
            pl.BlockSpec((1, 8, LANES), lambda o: (o, 0, 0)),
        ],
        out_specs=pl.BlockSpec((1, pairs, 2, side, side), lambda o: (o, 0, 0, 0, 0)),
        scratch_shapes=[
            pltpu.VMEM((2 * rows, 4 * width), BF16),
            pltpu.VMEM((rows, 4 * width), BF16),
        ],
        compiler_params=pltpu.CompilerParams(vmem_limit_bytes=40 * 2**20),
        cost_estimate=pl.CostEstimate(flops=4_500_000_000, bytes_accessed=9_000_000, transcendentals=0),
        name="tiles",
    )(pick, part, early, power)


def body(voltages, taps, station_gain, station_order):
    devices = lax.axis_size("ingest")
    streams = 2 * voltages.shape[0]
    blocks = NCHAN // LANES
    all_out = OUT_DEV * devices
    consts = tables(all_out)
    frames = SPECTRA + TAPS - 1
    samples = voltages.reshape(streams, 2, frames * blocks, LANES).transpose(0, 2, 1, 3)
    samples = samples.reshape(streams, frames, 2 * blocks, LANES)
    coeffs = taps.reshape(TAPS, blocks, LANES).transpose(1, 0, 2).reshape(TAPS * blocks, LANES)
    (start, count), (later, rest) = CHUNKS
    sent = spectra(samples, coeffs, station_gain, consts, start, count, devices)
    early = [sent[0]] + [
        lax.ppermute(sent[k], "ingest", [(i, i ^ k) for i in range(devices)]) for k in range(1, devices)
    ]
    packed = spectra(samples, coeffs, station_gain, consts, later, rest)[0]
    packed = packed.reshape(devices, 2 * OUT_DEV, streams, rest * AVG)
    late = lax.all_to_all(packed, "ingest", split_axis=0, concat_axis=0, tiled=True)
    wanted = (2 * station_order[:, None] + jnp.arange(2, dtype=jnp.int32)).reshape(-1, 1)
    column = jnp.arange(2 * STATIONS, dtype=jnp.int32)
    pick = (wanted == column).astype(BF16)
    mixed = (wanted == jnp.bitwise_xor(column, lax.axis_index("ingest") * streams)).astype(BF16)
    held, power = arrange(mixed, early)
    return tiles(pick, late, held, power)


def solution(mesh):
    return jax.shard_map(
        body,
        mesh=mesh,
        in_specs=(P(("band", "ingest"), None, None, None), P(), P("ingest"), P()),
        out_specs=P(("band", "ingest"), None, None, None, None),
        check_vma=False,
    )
```

```python
import functools
import math

import jax
import jax.numpy as jnp
import ml_dtypes
import numpy as np
from jax import lax
from jax.experimental import pallas as pl
from jax.experimental.pallas import tpu as pltpu
from jax.sharding import PartitionSpec as P

STATIONS = 512
NCHAN = 4096
BLOCK = 64
TAPS = 4
SPECTRA = 8
AVG = 32
OUT_DEV = 2
LANES = 128
CHUNKS = ((0, 4), (4, 4))
GROUP = 4
FIRST_SENT = 5
WINDOW = 5
ROWS = 16
BF16 = jnp.bfloat16
F32 = jnp.float32
NT = (((1,), (1,)), ((), ()))


def split(values):
    high = values.astype(ml_dtypes.bfloat16)
    low = (values - high.astype(np.float64)).astype(ml_dtypes.bfloat16)
    return high, low


def tables(all_out):
    blocks = NCHAN // LANES
    angle = 2.0 * math.pi * (np.outer(np.arange(AVG), np.arange(blocks)) % blocks) / blocks
    cos, sin = np.cos(angle), np.sin(angle)
    stage = np.zeros((2, AVG, blocks, 2))
    stage[0, :, :, 0], stage[0, :, :, 1] = cos, sin
    stage[1, :, :, 0], stage[1, :, :, 1] = -sin, cos
    stage = stage.reshape(2 * AVG, 2 * blocks)
    stage = np.kron(np.eye(GROUP), stage)
    angle = 2.0 * math.pi * np.outer(np.arange(AVG), np.arange(LANES)) / NCHAN
    turn = np.stack([np.cos(angle), -np.sin(angle)]).astype(np.float32)
    first = (NCHAN - all_out * AVG) // 2
    bins = first // AVG + np.arange(all_out)
    angle = 2.0 * math.pi * (np.outer(bins, np.arange(LANES)) % LANES) / LANES
    cos, sin = np.cos(angle), np.sin(angle)
    last = np.zeros((all_out, 2, 2, LANES))
    last[:, 0, 0], last[:, 0, 1] = cos, sin
    last[:, 1, 0], last[:, 1, 1] = -sin, cos
    last = last.reshape(2 * all_out, 2 * LANES)
    return np.concatenate(split(stage)), turn, np.concatenate(split(last))


def halves(values):
    high = values.astype(BF16)
    return high, (values - high.astype(F32)).astype(BF16)


def spectra_kernel(count, partners, gain_ref, *refs):
    frames, refs = refs[: count + TAPS - 1], refs[count + TAPS - 1 :]
    (taps_ref, stage_ref, turn_ref, last_ref), refs = refs[:4], refs[4:]
    out_refs = refs[: max(partners, 1)]
    coeff_ref, high_ref, low_ref, zhigh_ref, zlow_ref, held_ref = refs[len(out_refs) :]
    step = pl.program_id(0)
    wide = 2 * AVG
    size = GROUP * wide
    outs = last_ref.shape[0] // 2
    width = count * AVG

    @pl.when(step == 0)
    def _():
        for j in range(TAPS):
            rows = taps_ref[pl.ds(j, AVG, stride=TAPS), :]
            for ri in range(2):
                coeff_ref[j, pl.ds(ri, AVG, stride=2), :] = rows

    def filter_group(g):
        for u in range(GROUP):
            for r in range(0, wide, 16):
                rows = slice(r, r + 16)
                coeffs = [coeff_ref[j, rows, :] for j in range(TAPS)]
                samples = [ref[g * GROUP + u, 0, rows, :].astype(F32) for ref in frames]
                for m in range(count):
                    value = coeffs[0] * samples[m]
                    for j in range(1, TAPS):
                        value = value + coeffs[j] * samples[m + j]
                    high, low = halves(value)
                    place = (g, slice(u * wide + r, u * wide + r + 16), slice(m * LANES, (m + 1) * LANES))
                    high_ref[place] = high
                    low_ref[place] = low

    def first_group(g):
        for start in range(0, count, 2):
            lanes = slice(start * LANES, (start + 2) * LANES)
            both = jnp.dot(stage_ref[...], high_ref[g, :, lanes], preferred_element_type=F32)
            rest = jnp.dot(stage_ref[:size, :], low_ref[g, :, lanes], preferred_element_type=F32)
            section = both[:size] + (both[size:] + rest)
            for u in range(GROUP):
                for m in range(start, start + 2):
                    at = slice((m - start) * LANES, (m - start + 1) * LANES)
                    real = section[u * wide : u * wide + AVG, at]
                    imag = section[u * wide + AVG : (u + 1) * wide, at]
                    turn_real, turn_imag = turn_ref[0], turn_ref[1]
                    row = slice((u * count + m) * AVG, (u * count + m + 1) * AVG)
                    high, low = halves(real * turn_real - imag * turn_imag)
                    zhigh_ref[g, row, :LANES] = high
                    zlow_ref[g, row, :LANES] = low
                    high, low = halves(real * turn_imag + imag * turn_real)
                    zhigh_ref[g, row, LANES:] = high
                    zlow_ref[g, row, LANES:] = low

    def last_group(g):
        for pair in range(GROUP // 2):
            rows = slice(pair * 2 * width, (pair + 1) * 2 * width)
            both = lax.dot_general(last_ref[...], zhigh_ref[g, rows, :], NT, preferred_element_type=F32)
            rest = lax.dot_general(last_ref[:outs, :], zlow_ref[g, rows, :], NT, preferred_element_type=F32)
            found = both[:outs] + (both[outs:] + rest)
            stream = g * GROUP + pair * 2
            factor = gain_ref[(step * ROWS + stream) // 2] * (1.0 / (64.0 * math.sqrt(NCHAN)))
            for p in range(2):
                held_ref[(stream + p) * outs : (stream + p + 1) * outs, :] = found[:, p * width : (p + 1) * width] * factor

    groups = ROWS // GROUP
    for g in range(groups + 2):
        if g < groups:
            filter_group(g)
        if 1 <= g <= groups:
            first_group(g - 1)
        if g >= 2:
            last_group(g - 2)
    if partners:
        me = lax.axis_index("ingest")
        each = outs // partners
        for k in range(partners):
            target = jnp.bitwise_xor(me, k) * each
            for q in range(each):
                out_refs[k][q] = held_ref[pl.ds(target + q, ROWS, stride=outs), :].astype(BF16)
    else:
        for row in range(outs):
            out_refs[0][row] = held_ref[pl.ds(row, ROWS, stride=outs), :].astype(BF16)


def spectra(voltages, taps, station_gain, consts, start, count, partners=0):
    streams = voltages.shape[0]
    stage, turn, last = consts
    outs = last.shape[0] // 2
    groups = ROWS // GROUP
    wide = 2 * AVG
    width = count * AVG
    frame_spec = [
        pl.BlockSpec((ROWS, 1, wide, LANES), functools.partial(lambda j, a: (a, j, 0, 0), start + j))
        for j in range(count + TAPS - 1)
    ]
    whole = lambda shape: pl.BlockSpec(shape, lambda a: (0,) * len(shape))
    pieces = max(partners, 1)
    return pl.pallas_call(
        functools.partial(spectra_kernel, count, partners),
        out_shape=[jax.ShapeDtypeStruct((outs // pieces, streams, width), BF16)] * pieces,
        grid=(streams // ROWS,),
        in_specs=[pl.BlockSpec(memory_space=pltpu.SMEM)]
        + frame_spec
        + [whole(taps.shape), whole(stage.shape), whole(turn.shape), whole(last.shape)],
        out_specs=[pl.BlockSpec((outs // pieces, ROWS, width), lambda a: (0, a, 0))] * pieces,
        scratch_shapes=[
            pltpu.VMEM((TAPS, wide, LANES), F32),
            pltpu.VMEM((groups, GROUP * wide, count * LANES), BF16),
            pltpu.VMEM((groups, GROUP * wide, count * LANES), BF16),
            pltpu.VMEM((groups, GROUP * width, 2 * LANES), BF16),
            pltpu.VMEM((groups, GROUP * width, 2 * LANES), BF16),
            pltpu.VMEM((ROWS * outs, width), F32),
        ],
        compiler_params=pltpu.CompilerParams(vmem_limit_bytes=60_000_000),
        cost_estimate=pl.CostEstimate(
            flops=streams * count * 12_000_000,
            bytes_accessed=streams * (count + TAPS - 1) * wide * LANES * 4,
            transcendentals=0,
        ),
        name="spectra",
    )(station_gain, *([voltages] * (count + TAPS - 1)), taps, stage, turn, last)


def squares(pieces):
    total = jnp.zeros((8, LANES), F32)
    for piece in pieces:
        values = piece.astype(F32)
        total = total + jnp.sum((values * values).reshape(-1, 8, LANES), axis=0)
    return total


def arrange_kernel(pick_ref, *refs):
    part_refs, (out_ref, power_ref) = refs[:-2], refs[-2:]
    rows = 2 * STATIONS
    pieces = [jnp.concatenate([part_ref[ri] for part_ref in part_refs], axis=0) for ri in range(2)]
    power_ref[0] = squares(pieces)
    data = jnp.concatenate(pieces, axis=1)
    for r in range(0, rows, 2 * LANES):
        own = slice(r, r + 2 * LANES)
        out_ref[0, own, :] = jnp.dot(pick_ref[own, :], data, preferred_element_type=F32).astype(BF16)


def arrange(pick, parts):
    _, own, width = parts[0].shape
    rows = 2 * STATIONS
    return pl.pallas_call(
        arrange_kernel,
        out_shape=(
            jax.ShapeDtypeStruct((OUT_DEV, rows, 2 * width), BF16),
            jax.ShapeDtypeStruct((OUT_DEV, 8, LANES), F32),
        ),
        grid=(OUT_DEV,),
        in_specs=[
            pl.BlockSpec(pick.shape, lambda o: (0, 0)),
        ]
        + [pl.BlockSpec((2, own, width), lambda o: (o, 0, 0))] * len(parts),
        out_specs=(
            pl.BlockSpec((1, rows, 2 * width), lambda o: (o, 0, 0)),
            pl.BlockSpec((1, 8, LANES), lambda o: (o, 0, 0)),
        ),
        compiler_params=pltpu.CompilerParams(vmem_limit_bytes=16 * 2**20),
        cost_estimate=pl.CostEstimate(flops=1_100_000_000, bytes_accessed=4_000_000, transcendentals=0),
        name="arrange",
    )(pick, *parts)


def turned(values):
    return jnp.concatenate([values[:, LANES:], -values[:, :LANES]], axis=1)


def tiles_kernel(pick_ref, early_ref, power_ref, *refs):
    part_refs, (out_ref, left_ref, right_ref) = refs[:-3], refs[-3:]
    rows = 2 * STATIONS
    side = 2 * BLOCK
    blocks = STATIONS // BLOCK
    pieces = [jnp.concatenate([part_ref[ri] for part_ref in part_refs], axis=0) for ri in range(2)]
    power = jnp.sum(squares(pieces) + power_ref[0]) / (STATIONS * 2 * SPECTRA * AVG)
    scale = 1.0 / jnp.full((1, LANES), SPECTRA * AVG * power, F32)
    data = jnp.concatenate(pieces, axis=1)
    half = data.shape[1]
    for r in range(0, rows, 2 * side):
        found = jnp.dot(pick_ref[r : r + 2 * side, :], data, preferred_element_type=F32).astype(BF16)
        early = early_ref[0, r : r + 2 * side, :]
        right_ref[r : r + 2 * side, :half] = early
        right_ref[r : r + 2 * side, half:] = found
        for p in range(2):
            own = slice(p * side, (p + 1) * side)
            at = 2 * r + p * 2 * side
            left_ref[at : at + side, :half] = early[own]
            left_ref[at : at + side, half:] = found[own]
            left_ref[at + side : at + 2 * side, :half] = turned(early[own])
            left_ref[at + side : at + 2 * side, half:] = turned(found[own])
    for c in range(0, blocks, 2):
        right = right_ref[c * side : (c + 2) * side, :]
        for b in range(c, blocks):
            left = left_ref[b * 2 * side : (b + 1) * 2 * side, :]
            product = lax.dot_general(left, right, NT, preferred_element_type=F32)
            for p in range(2):
                if c + p <= b:
                    tile = b * (b + 1) // 2 + c + p
                    scaled = (product[:, p * side : (p + 1) * side] * scale).astype(BF16)
                    out_ref[0, tile, 0] = scaled[:side]
                    out_ref[0, tile, 1] = scaled[side:]


def tiles(pick, parts, early, power):
    _, own, width = parts[0].shape
    blocks = STATIONS // BLOCK
    pairs = blocks * (blocks + 1) // 2
    side = 2 * BLOCK
    rows = 2 * STATIONS
    return pl.pallas_call(
        tiles_kernel,
        out_shape=jax.ShapeDtypeStruct((OUT_DEV, pairs, 2, side, side), BF16),
        grid=(OUT_DEV,),
        in_specs=[
            pl.BlockSpec(pick.shape, lambda o: (0, 0)),
            pl.BlockSpec((1, rows, 2 * width), lambda o: (o, 0, 0)),
            pl.BlockSpec((1, 8, LANES), lambda o: (o, 0, 0)),
        ]
        + [pl.BlockSpec((2, own, width), lambda o: (o, 0, 0))] * len(parts),
        out_specs=pl.BlockSpec((1, pairs, 2, side, side), lambda o: (o, 0, 0, 0, 0)),
        scratch_shapes=[
            pltpu.VMEM((2 * rows, 4 * width), BF16),
            pltpu.VMEM((rows, 4 * width), BF16),
        ],
        compiler_params=pltpu.CompilerParams(vmem_limit_bytes=24 * 2**20),
        cost_estimate=pl.CostEstimate(flops=4_500_000_000, bytes_accessed=9_000_000, transcendentals=0),
        name="tiles",
    )(pick, early, power, *parts)


def sending_order(devices):
    far = [(piece, k) for piece in range(2) for k in range(devices // 2, devices)]
    near = [(piece, k) for piece in range(2) for k in range(1, devices // 2)]
    order, far = far[:FIRST_SENT], far[FIRST_SENT:]
    while far or near:
        order += far[:1] + near[:1]
        far, near = far[1:], near[1:]
    return order


def body(voltages, taps, station_gain, station_order):
    devices = lax.axis_size("ingest")
    streams = 2 * voltages.shape[0]
    blocks = NCHAN // LANES
    all_out = OUT_DEV * devices
    consts = tables(all_out)
    frames = SPECTRA + TAPS - 1
    samples = voltages.reshape(streams, 2, frames * blocks, LANES).transpose(0, 2, 1, 3)
    samples = samples.reshape(streams, frames, 2 * blocks, LANES)
    coeffs = taps.reshape(TAPS, blocks, LANES).transpose(1, 0, 2).reshape(TAPS * blocks, LANES)
    sent = [spectra(samples, coeffs, station_gain, consts, start, count, devices) for start, count in CHUNKS]
    held = [{0: pieces[0]} for pieces in sent]
    order = sending_order(devices)
    for place, (piece, k) in enumerate(order):
        ready = sent[piece][k]
        if place >= WINDOW:
            before, past = order[place - WINDOW]
            ready, held[before][past] = lax.optimization_barrier((ready, held[before][past]))
        held[piece][k] = lax.ppermute(ready, "ingest", [(i, i ^ k) for i in range(devices)])
    early, late = [[pieces[k] for k in range(devices)] for pieces in held]
    wanted = (2 * station_order[:, None] + jnp.arange(2, dtype=jnp.int32)).reshape(-1, 1)
    column = jnp.bitwise_xor(jnp.arange(2 * STATIONS, dtype=jnp.int32), lax.axis_index("ingest") * streams)
    pick = (wanted == column).astype(BF16)
    rows, power = arrange(pick, early)
    return tiles(pick, late, rows, power)


def solution(mesh):
    return jax.shard_map(
        body,
        mesh=mesh,
        in_specs=(P(("band", "ingest"), None, None, None), P(), P("ingest"), P()),
        out_specs=P(("band", "ingest"), None, None, None, None),
        check_vma=False,
    )
```

```python
import functools
import math

import jax
import jax.numpy as jnp
import ml_dtypes
import numpy as np
from jax import lax
from jax.experimental import pallas as pl
from jax.experimental.pallas import tpu as pltpu
from jax.sharding import PartitionSpec as P

STATIONS = 512
NCHAN = 4096
BLOCK = 64
TAPS = 4
SPECTRA = 8
AVG = 32
OUT_DEV = 2
LANES = 128
CHUNKS = ((0, 4), (4, 4))
GROUP = 4
WINDOW = 5
ROWS = 16
BF16 = jnp.bfloat16
F32 = jnp.float32
NT = (((1,), (1,)), ((), ()))


def split(values):
    high = values.astype(ml_dtypes.bfloat16)
    low = (values - high.astype(np.float64)).astype(ml_dtypes.bfloat16)
    return high, low


def tables(all_out):
    blocks = NCHAN // LANES
    angle = 2.0 * math.pi * (np.outer(np.arange(AVG), np.arange(blocks)) % blocks) / blocks
    cos, sin = np.cos(angle), np.sin(angle)
    stage = np.zeros((2, AVG, blocks, 2))
    stage[0, :, :, 0], stage[0, :, :, 1] = cos, sin
    stage[1, :, :, 0], stage[1, :, :, 1] = -sin, cos
    stage = stage.reshape(2 * AVG, 2 * blocks)
    stage = np.kron(np.eye(GROUP), stage)
    angle = 2.0 * math.pi * np.outer(np.arange(AVG), np.arange(LANES)) / NCHAN
    turn = np.stack([np.cos(angle), -np.sin(angle)]).astype(np.float32)
    first = (NCHAN - all_out * AVG) // 2
    bins = first // AVG + np.arange(all_out)
    angle = 2.0 * math.pi * (np.outer(bins, np.arange(LANES)) % LANES) / LANES
    cos, sin = np.cos(angle), np.sin(angle)
    last = np.zeros((all_out, 2, 2, LANES))
    last[:, 0, 0], last[:, 0, 1] = cos, sin
    last[:, 1, 0], last[:, 1, 1] = -sin, cos
    last = last.reshape(2 * all_out, 2 * LANES)
    return np.concatenate(split(stage)), turn, np.concatenate(split(last))


def halves(values):
    high = values.astype(BF16)
    return high, (values - high.astype(F32)).astype(BF16)


def spectra_kernel(count, partners, gain_ref, *refs):
    frames, refs = refs[: count + TAPS - 1], refs[count + TAPS - 1 :]
    (taps_ref, stage_ref, turn_ref, last_ref), refs = refs[:4], refs[4:]
    out_refs = refs[: max(partners, 1)]
    (coeff_ref, held_ref), refs = refs[len(out_refs) : len(out_refs) + 2], refs[len(out_refs) + 2 :]
    groups = ROWS // GROUP
    high_refs, low_refs, zhigh_refs, zlow_refs = [refs[i * groups : (i + 1) * groups] for i in range(4)]
    step = pl.program_id(0)
    wide = 2 * AVG
    size = GROUP * wide
    outs = last_ref.shape[0] // 2
    width = count * AVG

    @pl.when(step == 0)
    def _():
        for j in range(TAPS):
            rows = taps_ref[pl.ds(j, AVG, stride=TAPS), :]
            for ri in range(2):
                coeff_ref[j, pl.ds(ri, AVG, stride=2), :] = rows

    def filter_rows(g, u, r):
        rows = slice(r, r + 16)
        coeffs = [coeff_ref[j, rows, :] for j in range(TAPS)]
        samples = [ref[g * GROUP + u, 0, rows, :].astype(F32) for ref in frames]
        for m in range(count):
            value = coeffs[0] * samples[m]
            for j in range(1, TAPS):
                value = value + coeffs[j] * samples[m + j]
            high, low = halves(value)
            place = (slice(u * wide + r, u * wide + r + 16), slice(m * LANES, (m + 1) * LANES))
            high_refs[g][place] = high
            low_refs[g][place] = low

    def first_part(g, start):
        lanes = slice(start * LANES, (start + 2) * LANES)
        both = jnp.dot(stage_ref[...], high_refs[g][:, lanes], preferred_element_type=F32)
        rest = jnp.dot(stage_ref[:size, :], low_refs[g][:, lanes], preferred_element_type=F32)
        section = both[:size] + (both[size:] + rest)
        for u in range(GROUP):
            for m in range(start, start + 2):
                at = slice((m - start) * LANES, (m - start + 1) * LANES)
                real = section[u * wide : u * wide + AVG, at]
                imag = section[u * wide + AVG : (u + 1) * wide, at]
                turn_real, turn_imag = turn_ref[0], turn_ref[1]
                row = slice((u * count + m) * AVG, (u * count + m + 1) * AVG)
                high, low = halves(real * turn_real - imag * turn_imag)
                zhigh_refs[g][row, :LANES] = high
                zlow_refs[g][row, :LANES] = low
                high, low = halves(real * turn_imag + imag * turn_real)
                zhigh_refs[g][row, LANES:] = high
                zlow_refs[g][row, LANES:] = low

    def last_part(g, pair):
        rows = slice(pair * 2 * width, (pair + 1) * 2 * width)
        both = lax.dot_general(last_ref[...], zhigh_refs[g][rows, :], NT, preferred_element_type=F32)
        rest = lax.dot_general(last_ref[:outs, :], zlow_refs[g][rows, :], NT, preferred_element_type=F32)
        found = both[:outs] + (both[outs:] + rest)
        stream = g * GROUP + pair * 2
        factor = gain_ref[(step * ROWS + stream) // 2] * (1.0 / (64.0 * math.sqrt(NCHAN)))
        for p in range(2):
            held_ref[(stream + p) * outs : (stream + p + 1) * outs, :] = found[:, p * width : (p + 1) * width] * factor

    for g in range(groups + 2):
        filters = [(g, u, r) for u in range(GROUP) for r in range(0, wide, 16)] if g < groups else []
        firsts = [(g - 1, start) for start in range(0, count, 2)] if 1 <= g <= groups else []
        lasts = [(g - 2, pair) for pair in range(GROUP // 2)] if g >= 2 else []
        while filters or firsts or lasts:
            for work, jobs, most in ((first_part, firsts, 1), (filter_rows, filters, 4), (last_part, lasts, 1), (filter_rows, filters, 4)):
                for job in jobs[:most]:
                    work(*job)
                del jobs[:most]
    if partners:
        me = lax.axis_index("ingest")
        each = outs // partners
        for k in range(partners):
            target = jnp.bitwise_xor(me, k) * each
            for q in range(each):
                out_refs[k][q] = held_ref[pl.ds(target + q, ROWS, stride=outs), :].astype(BF16)
    else:
        for row in range(outs):
            out_refs[0][row] = held_ref[pl.ds(row, ROWS, stride=outs), :].astype(BF16)


def spectra(voltages, taps, station_gain, consts, start, count, partners=0):
    streams = voltages.shape[0]
    stage, turn, last = consts
    outs = last.shape[0] // 2
    groups = ROWS // GROUP
    wide = 2 * AVG
    width = count * AVG
    frame_spec = [
        pl.BlockSpec((ROWS, 1, wide, LANES), functools.partial(lambda j, a: (a, j, 0, 0), start + j))
        for j in range(count + TAPS - 1)
    ]
    whole = lambda shape: pl.BlockSpec(shape, lambda a: (0,) * len(shape))
    pieces = max(partners, 1)
    return pl.pallas_call(
        functools.partial(spectra_kernel, count, partners),
        out_shape=[jax.ShapeDtypeStruct((outs // pieces, streams, width), BF16)] * pieces,
        grid=(streams // ROWS,),
        in_specs=[pl.BlockSpec(memory_space=pltpu.SMEM)]
        + frame_spec
        + [whole(taps.shape), whole(stage.shape), whole(turn.shape), whole(last.shape)],
        out_specs=[pl.BlockSpec((outs // pieces, ROWS, width), lambda a: (0, a, 0))] * pieces,
        scratch_shapes=[
            pltpu.VMEM((TAPS, wide, LANES), F32),
            pltpu.VMEM((ROWS * outs, width), F32),
        ]
        + [pltpu.VMEM((GROUP * wide, count * LANES), BF16)] * (2 * groups)
        + [pltpu.VMEM((GROUP * width, 2 * LANES), BF16)] * (2 * groups),
        compiler_params=pltpu.CompilerParams(vmem_limit_bytes=60_000_000),
        cost_estimate=pl.CostEstimate(
            flops=streams * count * 12_000_000,
            bytes_accessed=streams * (count + TAPS - 1) * wide * LANES * 4,
            transcendentals=0,
        ),
        name="spectra",
    )(station_gain, *([voltages] * (count + TAPS - 1)), taps, stage, turn, last)


def squares(pieces):
    total = jnp.zeros((8, LANES), F32)
    for piece in pieces:
        values = piece.astype(F32)
        total = total + jnp.sum((values * values).reshape(-1, 8, LANES), axis=0)
    return total


def arrange_kernel(pick_ref, part_ref, out_ref, power_ref):
    rows = 2 * STATIONS
    pieces = [part_ref[:, ri].reshape(rows, LANES) for ri in range(2)]
    power_ref[0] = squares(pieces)
    data = jnp.concatenate(pieces, axis=1)
    for r in range(0, rows, 2 * LANES):
        own = slice(r, r + 2 * LANES)
        out_ref[0, own, :] = jnp.dot(pick_ref[own, :], data, preferred_element_type=F32).astype(BF16)


def arrange(pick, part):
    devices, _, own, width = part.shape
    rows = 2 * STATIONS
    return pl.pallas_call(
        arrange_kernel,
        out_shape=(
            jax.ShapeDtypeStruct((OUT_DEV, rows, 2 * width), BF16),
            jax.ShapeDtypeStruct((OUT_DEV, 8, LANES), F32),
        ),
        grid=(OUT_DEV,),
        in_specs=[
            pl.BlockSpec(pick.shape, lambda o: (0, 0)),
            pl.BlockSpec((devices, 2, own, width), lambda o: (0, o, 0, 0)),
        ],
        out_specs=(
            pl.BlockSpec((1, rows, 2 * width), lambda o: (o, 0, 0)),
            pl.BlockSpec((1, 8, LANES), lambda o: (o, 0, 0)),
        ),
        compiler_params=pltpu.CompilerParams(vmem_limit_bytes=16 * 2**20),
        cost_estimate=pl.CostEstimate(flops=1_100_000_000, bytes_accessed=4_000_000, transcendentals=0),
        name="arrange",
    )(pick, part)


def turned(values):
    return jnp.concatenate([values[:, LANES:], -values[:, :LANES]], axis=1)


def tiles_kernel(pick_ref, early_ref, power_ref, *refs):
    part_refs, (out_ref, left_ref, right_ref) = refs[:-3], refs[-3:]
    rows = 2 * STATIONS
    side = 2 * BLOCK
    blocks = STATIONS // BLOCK
    pieces = [jnp.concatenate([part_ref[ri] for part_ref in part_refs], axis=0) for ri in range(2)]
    power = jnp.sum(squares(pieces) + power_ref[0]) / (STATIONS * 2 * SPECTRA * AVG)
    scale = 1.0 / jnp.full((1, LANES), SPECTRA * AVG * power, F32)
    data = jnp.concatenate(pieces, axis=1)
    half = data.shape[1]
    for r in range(0, rows, 2 * side):
        found = jnp.dot(pick_ref[r : r + 2 * side, :], data, preferred_element_type=F32).astype(BF16)
        early = early_ref[0, r : r + 2 * side, :]
        right_ref[r : r + 2 * side, :half] = early
        right_ref[r : r + 2 * side, half:] = found
        for p in range(2):
            own = slice(p * side, (p + 1) * side)
            at = 2 * r + p * 2 * side
            left_ref[at : at + side, :half] = early[own]
            left_ref[at : at + side, half:] = found[own]
            left_ref[at + side : at + 2 * side, :half] = turned(early[own])
            left_ref[at + side : at + 2 * side, half:] = turned(found[own])
    for c in range(0, blocks, 2):
        right = right_ref[c * side : (c + 2) * side, :]
        for b in range(c, blocks):
            left = left_ref[b * 2 * side : (b + 1) * 2 * side, :]
            product = lax.dot_general(left, right, NT, preferred_element_type=F32)
            for p in range(2):
                if c + p <= b:
                    tile = b * (b + 1) // 2 + c + p
                    scaled = (product[:, p * side : (p + 1) * side] * scale).astype(BF16)
                    out_ref[0, tile, 0] = scaled[:side]
                    out_ref[0, tile, 1] = scaled[side:]


def tiles(pick, parts, early, power):
    _, own, width = parts[0].shape
    blocks = STATIONS // BLOCK
    pairs = blocks * (blocks + 1) // 2
    side = 2 * BLOCK
    rows = 2 * STATIONS
    return pl.pallas_call(
        tiles_kernel,
        out_shape=jax.ShapeDtypeStruct((OUT_DEV, pairs, 2, side, side), BF16),
        grid=(OUT_DEV,),
        in_specs=[
            pl.BlockSpec(pick.shape, lambda o: (0, 0)),
            pl.BlockSpec((1, rows, 2 * width), lambda o: (o, 0, 0)),
            pl.BlockSpec((1, 8, LANES), lambda o: (o, 0, 0)),
        ]
        + [pl.BlockSpec((2, own, width), lambda o: (o, 0, 0))] * len(parts),
        out_specs=pl.BlockSpec((1, pairs, 2, side, side), lambda o: (o, 0, 0, 0, 0)),
        scratch_shapes=[
            pltpu.VMEM((2 * rows, 4 * width), BF16),
            pltpu.VMEM((rows, 4 * width), BF16),
        ],
        compiler_params=pltpu.CompilerParams(vmem_limit_bytes=24 * 2**20),
        cost_estimate=pl.CostEstimate(flops=4_500_000_000, bytes_accessed=9_000_000, transcendentals=0),
        name="tiles",
    )(pick, early, power, *parts)


def sending_order(devices):
    far, near = list(range(devices // 2, devices)), list(range(1, devices // 2))
    order, far = far[:1], far[1:]
    while far or near:
        order += far[:1] + near[:1]
        far, near = far[1:], near[1:]
    return order


def body(voltages, taps, station_gain, station_order):
    devices = lax.axis_size("ingest")
    streams = 2 * voltages.shape[0]
    blocks = NCHAN // LANES
    all_out = OUT_DEV * devices
    consts = tables(all_out)
    frames = SPECTRA + TAPS - 1
    samples = voltages.reshape(streams, 2, frames * blocks, LANES).transpose(0, 2, 1, 3)
    samples = samples.reshape(streams, frames, 2 * blocks, LANES)
    coeffs = taps.reshape(TAPS, blocks, LANES).transpose(1, 0, 2).reshape(TAPS * blocks, LANES)
    (start, count), (later, rest) = CHUNKS
    packed = spectra(samples, coeffs, station_gain, consts, start, count)[0]
    packed = packed.reshape(devices, 2 * OUT_DEV, streams, count * AVG)
    packed, station_gain = lax.optimization_barrier((packed, station_gain))
    early = lax.all_to_all(packed, "ingest", split_axis=0, concat_axis=0, tiled=True)
    sent = spectra(samples, coeffs, station_gain, consts, later, rest, devices)
    late = {0: sent[0]}
    order = sending_order(devices)
    for place, k in enumerate(order):
        ready = sent[k]
        if place >= WINDOW:
            past = order[place - WINDOW]
            ready, late[past] = lax.optimization_barrier((ready, late[past]))
        late[k] = lax.ppermute(ready, "ingest", [(i, i ^ k) for i in range(devices)])
    wanted = (2 * station_order[:, None] + jnp.arange(2, dtype=jnp.int32)).reshape(-1, 1)
    column = jnp.arange(2 * STATIONS, dtype=jnp.int32)
    pick = (wanted == column).astype(BF16)
    mixed = (wanted == jnp.bitwise_xor(column, lax.axis_index("ingest") * streams)).astype(BF16)
    rows, power = arrange(pick, early)
    return tiles(mixed, [late[k] for k in range(devices)], rows, power)


def solution(mesh):
    return jax.shard_map(
        body,
        mesh=mesh,
        in_specs=(P(("band", "ingest"), None, None, None), P(), P("ingest"), P()),
        out_specs=P(("band", "ingest"), None, None, None, None),
        check_vma=False,
    )
```

```python
import functools
import math

import jax
import jax.numpy as jnp
import ml_dtypes
import numpy as np
from jax import lax
from jax.experimental import pallas as pl
from jax.experimental.pallas import tpu as pltpu
from jax.sharding import PartitionSpec as P

STATIONS = 512
NCHAN = 4096
BLOCK = 64
TAPS = 4
SPECTRA = 8
FRAMES = SPECTRA + TAPS - 1
AVG = 32
OUT_DEV = 2
LANES = 128
WIDE = 2 * AVG
WIDTH = SPECTRA * AVG
GROUP = 4
STEP = 8
ROWS = 16
WINDOW = 5
VMEM_LIMIT = 60_000_000
BF16 = jnp.bfloat16
F32 = jnp.float32
NT = (((1,), (1,)), ((), ()))


def split(values):
    high = values.astype(ml_dtypes.bfloat16)
    low = (values - high.astype(np.float64)).astype(ml_dtypes.bfloat16)
    return high, low


def tables(all_out):
    blocks = NCHAN // LANES
    angle = 2.0 * math.pi * (np.outer(np.arange(AVG), np.arange(blocks)) % blocks) / blocks
    cos, sin = np.cos(angle), np.sin(angle)
    stage = np.zeros((2, AVG, blocks, 2))
    stage[0, :, :, 0], stage[0, :, :, 1] = cos, sin
    stage[1, :, :, 0], stage[1, :, :, 1] = -sin, cos
    stage = np.kron(np.eye(GROUP), stage.reshape(2 * AVG, 2 * blocks))
    angle = 2.0 * math.pi * np.outer(np.arange(AVG), np.arange(LANES)) / NCHAN
    turn = np.stack([np.cos(angle), -np.sin(angle)]).astype(np.float32)
    first = (NCHAN - all_out * AVG) // 2
    bins = first // AVG + np.arange(all_out)
    angle = 2.0 * math.pi * (np.outer(np.arange(LANES), bins) % LANES) / LANES
    cos, sin = np.cos(angle), np.sin(angle)
    last = np.zeros((2, LANES, all_out, 2))
    last[0, :, :, 0], last[0, :, :, 1] = cos, -sin
    last[1, :, :, 0], last[1, :, :, 1] = sin, cos
    beside = max(1, LANES // (2 * all_out))
    last = np.kron(np.eye(beside), last.reshape(2 * LANES, 2 * all_out))
    return np.concatenate(split(stage)), turn, np.concatenate(split(last), axis=1)


def halves(values):
    high = values.astype(BF16)
    return high, (values - high.astype(F32)).astype(BF16)


def spectra_kernel(first_stream, partners, outs, gain_ref, *refs):
    frames, refs = refs[:FRAMES], refs[FRAMES:]
    (taps_ref, stage_ref, turn_ref, last_ref), refs = refs[:4], refs[4:]
    out_refs, refs = refs[: max(partners, 1)], refs[max(partners, 1) :]
    (coeff_ref, held_ref), refs = refs[:2], refs[2:]
    groups = STEP // GROUP
    high_refs, low_refs, turned_refs = [refs[i * groups : (i + 1) * groups] for i in range(3)]
    outer, inner = pl.program_id(0), pl.program_id(1)
    size = GROUP * WIDE
    beside = last_ref.shape[0] // (2 * LANES)
    columns = beside * outs

    @pl.when((outer == 0) & (inner == 0))
    def _():
        for j in range(TAPS):
            rows = taps_ref[pl.ds(j, AVG, stride=TAPS), :]
            for ri in range(2):
                coeff_ref[j, pl.ds(ri, AVG, stride=2), :] = rows

    def filter_rows(g, u, r):
        rows = slice(r, r + 16)
        coeffs = [coeff_ref[j, rows, :] for j in range(TAPS)]
        samples = [ref[g * GROUP + u, 0, rows, :].astype(F32) for ref in frames]
        for m in range(SPECTRA):
            value = coeffs[0] * samples[m]
            for j in range(1, TAPS):
                value = value + coeffs[j] * samples[m + j]
            high, low = halves(value)
            place = (slice(u * WIDE + r, u * WIDE + r + 16), slice(m * LANES, (m + 1) * LANES))
            high_refs[g][place] = high
            low_refs[g][place] = low

    def first_part(g, start):
        lanes = slice(start * LANES, (start + 2) * LANES)
        both = jnp.dot(stage_ref[...], high_refs[g][:, lanes], preferred_element_type=F32)
        rest = jnp.dot(stage_ref[:size, :], low_refs[g][:, lanes], preferred_element_type=F32)
        section = both[:size] + (both[size:] + rest)
        turn_real, turn_imag = turn_ref[0], turn_ref[1]
        for u in range(GROUP):
            pair, place = divmod(u, beside)
            for m in range(start, start + 2):
                at = slice((m - start) * LANES, (m - start + 1) * LANES)
                real = section[u * WIDE : u * WIDE + AVG, at]
                imag = section[u * WIDE + AVG : (u + 1) * WIDE, at]
                for ri, value in enumerate((real * turn_real - imag * turn_imag, real * turn_imag + imag * turn_real)):
                    where = slice((2 * place + ri) * LANES, (2 * place + ri + 1) * LANES)
                    for part, kept in enumerate(halves(value)):
                        row = (2 * pair + part) * WIDTH + m * AVG
                        turned_refs[g][row : row + AVG, where] = kept

    def last_part(g, pair):
        rows = slice(2 * pair * WIDTH, 2 * (pair + 1) * WIDTH)
        product = jnp.dot(turned_refs[g][rows, :], last_ref[...], preferred_element_type=F32)
        found = product[:WIDTH, :columns] + (product[:WIDTH, columns:] + product[WIDTH:, :columns])
        found = found.T
        for place in range(beside):
            stream = g * GROUP + pair * beside + place
            factor = gain_ref[(first_stream + outer * ROWS + inner * STEP + stream) // 2]
            factor = factor * (1.0 / (64.0 * math.sqrt(NCHAN)))
            at = pl.multiple_of((inner * STEP + stream) * outs, outs)
            mine = found[place * outs : (place + 1) * outs] * factor
            for half in range(WIDTH // LANES):
                held_ref[half, pl.ds(at, outs), :] = mine[:, half * LANES : (half + 1) * LANES]

    for g in range(groups + 2):
        filters = [(g, u, r) for u in range(GROUP) for r in range(0, WIDE, 16)] if g < groups else []
        firsts = [(g - 1, start) for start in range(0, SPECTRA, 2)] if 1 <= g <= groups else []
        lasts = [(g - 2, pair) for pair in range(GROUP // beside)] if g >= 2 else []
        while filters or firsts or lasts:
            for work, jobs, most in ((first_part, firsts, 1), (filter_rows, filters, 2), (last_part, lasts, 1), (filter_rows, filters, 2)):
                for job in jobs[:most]:
                    work(*job)
                del jobs[:most]

    @pl.when(inner == ROWS // STEP - 1)
    def _():
        me = lax.axis_index("ingest") if partners else 0
        each = outs // len(out_refs)
        for k, out_ref in enumerate(out_refs):
            target = jnp.bitwise_xor(me, k) * each if partners else 0
            for q in range(each):
                for half in range(WIDTH // LANES):
                    rows = held_ref[half, pl.ds(target + q, ROWS, stride=outs), :]
                    out_ref[q, :, half * LANES : (half + 1) * LANES] = rows.astype(BF16)


def spectra(voltages, taps, station_gain, consts, outs, start, stop, partners=0):
    stage, turn, last = consts
    groups = STEP // GROUP
    inner = ROWS // STEP
    pieces = max(partners, 1)
    frame_spec = [
        pl.BlockSpec((STEP, 1, WIDE, LANES), functools.partial(lambda j, a, b: (start // STEP + a * inner + b, j, 0, 0), j))
        for j in range(FRAMES)
    ]
    whole = lambda shape: pl.BlockSpec(shape, lambda a, b: (0,) * len(shape))
    return pl.pallas_call(
        functools.partial(spectra_kernel, start, partners, outs),
        out_shape=[jax.ShapeDtypeStruct((outs // pieces, stop - start, WIDTH), BF16)] * pieces,
        grid=((stop - start) // ROWS, inner),
        in_specs=[pl.BlockSpec(memory_space=pltpu.SMEM)]
        + frame_spec
        + [whole(taps.shape), whole(stage.shape), whole(turn.shape), whole(last.shape)],
        out_specs=[pl.BlockSpec((outs // pieces, ROWS, WIDTH), lambda a, b: (0, a, 0))] * pieces,
        scratch_shapes=[
            pltpu.VMEM((TAPS, WIDE, LANES), F32),
            pltpu.VMEM((WIDTH // LANES, ROWS * outs, LANES), F32),
        ]
        + [pltpu.VMEM((GROUP * WIDE, SPECTRA * LANES), BF16)] * (2 * groups)
        + [pltpu.VMEM((2 * GROUP * WIDTH * 2 * LANES // last.shape[0], last.shape[0]), BF16)] * groups,
        compiler_params=pltpu.CompilerParams(vmem_limit_bytes=VMEM_LIMIT),
        cost_estimate=pl.CostEstimate(
            flops=(stop - start) * SPECTRA * 12_000_000,
            bytes_accessed=(stop - start) * FRAMES * WIDE * LANES * 4,
            transcendentals=0,
        ),
        name="spectra",
    )(station_gain, *([voltages] * FRAMES), taps, stage, turn, last)


def squares(values):
    values = values.astype(F32)
    values = jnp.sum((values * values).reshape(-1, 8, values.shape[-1]), axis=0)
    return sum(values[:, lane : lane + LANES] for lane in range(0, values.shape[-1], LANES))


def arrange_kernel(pick_ref, part_ref, out_ref, power_ref):
    rows = 2 * STATIONS
    data = jnp.concatenate([part_ref[:, ri].reshape(-1, WIDTH) for ri in range(2)], axis=1)
    power_ref[0] = squares(data)
    for r in range(0, rows, 2 * LANES):
        own = slice(r, r + 2 * LANES)
        out_ref[0, own, :] = jnp.dot(pick_ref[own, :], data, preferred_element_type=F32).astype(BF16)


def arrange(pick, part):
    devices, _, own, width = part.shape
    rows = 2 * STATIONS
    return pl.pallas_call(
        arrange_kernel,
        out_shape=(
            jax.ShapeDtypeStruct((OUT_DEV, rows, 2 * width), BF16),
            jax.ShapeDtypeStruct((OUT_DEV, 8, LANES), F32),
        ),
        grid=(OUT_DEV,),
        in_specs=[
            pl.BlockSpec(pick.shape, lambda o: (0, 0)),
            pl.BlockSpec((devices, 2, own, width), lambda o: (0, o, 0, 0)),
        ],
        out_specs=(
            pl.BlockSpec((1, rows, 2 * width), lambda o: (o, 0, 0)),
            pl.BlockSpec((1, 8, LANES), lambda o: (o, 0, 0)),
        ),
        compiler_params=pltpu.CompilerParams(vmem_limit_bytes=40 * 2**20),
        cost_estimate=pl.CostEstimate(flops=1_100_000_000, bytes_accessed=4_000_000, transcendentals=0),
        name="arrange",
    )(pick, part)


def tiles_kernel(late, early_ref, power_ref, *refs):
    (pick_refs, part_refs), refs = (refs[: min(late, 1)], refs[min(late, 1) :][:late]), refs[-3:]
    out_ref, left_ref, right_ref = refs
    rows = 2 * STATIONS
    side = 2 * BLOCK
    blocks = STATIONS // BLOCK
    total = power_ref[0]
    if late:
        data = [jnp.concatenate([part_ref[ri] for part_ref in part_refs], axis=0) for ri in range(2)]
        data = jnp.concatenate(data, axis=1)
        total = total + squares(data)
    power = jnp.sum(total) / (STATIONS * 2 * SPECTRA * AVG)
    scale = 1.0 / jnp.full((1, LANES), SPECTRA * AVG * power, F32)
    for r in range(0, rows, 2 * side):
        own = slice(r, r + 2 * side)
        found = early_ref[0, own, :]
        if late:
            found = (jnp.dot(pick_refs[0][own, :], data, preferred_element_type=F32) + found.astype(F32)).astype(BF16)
        right_ref[own, :] = found
        for p in range(2):
            mine = found[p * side : (p + 1) * side]
            at = 2 * r + p * 2 * side
            left_ref[at : at + side, :] = mine
            left_ref[at + side : at + 2 * side, :WIDTH] = mine[:, WIDTH:]
            left_ref[at + side : at + 2 * side, WIDTH:] = -mine[:, :WIDTH]
    for c in range(0, blocks, 2):
        right = right_ref[c * side : (c + 2) * side, :]
        for b in range(c, blocks):
            left = left_ref[b * 2 * side : (b + 1) * 2 * side, :]
            product = lax.dot_general(left, right, NT, preferred_element_type=F32)
            for p in range(2):
                if c + p <= b:
                    tile = b * (b + 1) // 2 + c + p
                    scaled = (product[:, p * side : (p + 1) * side] * scale).astype(BF16)
                    out_ref[0, tile, 0] = scaled[:side]
                    out_ref[0, tile, 1] = scaled[side:]


def tiles(early, power, picks, parts):
    blocks = STATIONS // BLOCK
    pairs = blocks * (blocks + 1) // 2
    side = 2 * BLOCK
    rows = 2 * STATIONS
    return pl.pallas_call(
        functools.partial(tiles_kernel, len(parts)),
        out_shape=jax.ShapeDtypeStruct((OUT_DEV, pairs, 2, side, side), BF16),
        grid=(OUT_DEV,),
        in_specs=[
            pl.BlockSpec((1, rows, 2 * WIDTH), lambda o: (o, 0, 0)),
            pl.BlockSpec((1, 8, LANES), lambda o: (o, 0, 0)),
        ]
        + [pl.BlockSpec(pick.shape, lambda o: (0, 0)) for pick in picks]
        + [pl.BlockSpec((2,) + part.shape[1:], lambda o: (o, 0, 0)) for part in parts],
        out_specs=pl.BlockSpec((1, pairs, 2, side, side), lambda o: (o, 0, 0, 0, 0)),
        scratch_shapes=[
            pltpu.VMEM((2 * rows, 2 * WIDTH), BF16),
            pltpu.VMEM((rows, 2 * WIDTH), BF16),
        ],
        compiler_params=pltpu.CompilerParams(vmem_limit_bytes=40 * 2**20),
        cost_estimate=pl.CostEstimate(flops=4_500_000_000, bytes_accessed=9_000_000, transcendentals=0),
        name="tiles",
    )(early, power, *picks, *parts)


def body(voltages, taps, station_gain, station_order):
    devices = lax.axis_size("ingest")
    streams = 2 * voltages.shape[0]
    blocks = NCHAN // LANES
    outs = 2 * OUT_DEV * devices
    consts = tables(OUT_DEV * devices)
    samples = voltages.reshape(streams, 2, FRAMES * blocks, LANES).transpose(0, 2, 1, 3)
    samples = samples.reshape(streams, FRAMES, 2 * blocks, LANES)
    coeffs = taps.reshape(TAPS, blocks, LANES).transpose(1, 0, 2).reshape(TAPS * blocks, LANES)
    cut = streams - streams // (2 * ROWS) * ROWS
    wanted = (2 * station_order[:, None] + jnp.arange(2, dtype=jnp.int32)).reshape(-1, 1)

    def pick(start, stop, first):
        place = np.arange(devices * (stop - start), dtype=np.int32)
        source = jnp.bitwise_xor(place // (stop - start), first) * streams + start + place % (stop - start)
        return (wanted == source).astype(BF16)

    packed = spectra(samples, coeffs, station_gain, consts, outs, 0, cut)[0]
    packed = packed.reshape(devices, 2 * OUT_DEV, cut, WIDTH)
    packed, station_gain = lax.optimization_barrier((packed, station_gain))
    early = lax.all_to_all(packed, "ingest", split_axis=0, concat_axis=0, tiled=True)
    picks, late = [], []
    if cut < streams:
        sent = spectra(samples, coeffs, station_gain, consts, outs, cut, streams, devices)
        late = [sent[0]]
        for k in range(1, devices):
            ready = sent[k]
            if k > WINDOW:
                ready, late[k - WINDOW] = lax.optimization_barrier((ready, late[k - WINDOW]))
            late.append(lax.ppermute(ready, "ingest", [(i, i ^ k) for i in range(devices)]))
        picks = [pick(cut, streams, lax.axis_index("ingest"))]
    rows, power = arrange(pick(0, cut, 0), early)
    return tiles(rows, power, picks, late)


def solution(mesh):
    return jax.shard_map(
        body,
        mesh=mesh,
        in_specs=(P(("band", "ingest"), None, None, None), P(), P("ingest"), P()),
        out_specs=P(("band", "ingest"), None, None, None, None),
        check_vma=False,
    )
```

```python
import functools
import math

import jax
import jax.numpy as jnp
import ml_dtypes
import numpy as np
from jax import lax
from jax.experimental import pallas as pl
from jax.experimental.pallas import tpu as pltpu
from jax.sharding import PartitionSpec as P

STATIONS = 512
NCHAN = 4096
BLOCK = 64
TAPS = 4
SPECTRA = 8
FRAMES = SPECTRA + TAPS - 1
AVG = 32
OUT_DEV = 2
LANES = 128
WIDE = 2 * AVG
WIDTH = SPECTRA * AVG
GROUP = 2
STEP = 8
ROWS = 16
WINDOW = 5
VMEM_LIMIT = 60_000_000
BF16 = jnp.bfloat16
F32 = jnp.float32
NT = (((1,), (1,)), ((), ()))


def split(values):
    high = values.astype(ml_dtypes.bfloat16)
    low = (values - high.astype(np.float64)).astype(ml_dtypes.bfloat16)
    return high, low


def tables(all_out):
    blocks = NCHAN // LANES
    angle = 2.0 * math.pi * (np.outer(np.arange(AVG), np.arange(blocks)) % blocks) / blocks
    cos, sin = np.cos(angle), np.sin(angle)
    stage = np.zeros((2, AVG, blocks, 2))
    stage[0, :, :, 0], stage[0, :, :, 1] = cos, sin
    stage[1, :, :, 0], stage[1, :, :, 1] = -sin, cos
    stage = np.stack(split(stage), axis=1).reshape(4 * AVG, 2 * blocks)
    stage = np.concatenate([np.kron(np.eye(GROUP), stage.astype(np.float32))] * 2, axis=1).astype(ml_dtypes.bfloat16)
    angle = 2.0 * math.pi * np.outer(np.arange(AVG), np.arange(LANES)) / NCHAN
    turn = np.stack([np.cos(angle), -np.sin(angle)]).astype(np.float32)
    first = (NCHAN - all_out * AVG) // 2
    bins = first // AVG + np.arange(all_out)
    angle = 2.0 * math.pi * (np.outer(np.arange(LANES), bins) % LANES) / LANES
    cos, sin = np.cos(angle), np.sin(angle)
    last = np.zeros((2, LANES, all_out, 2))
    last[0, :, :, 0], last[0, :, :, 1] = cos, -sin
    last[1, :, :, 0], last[1, :, :, 1] = sin, cos
    beside = max(1, LANES // (2 * all_out))
    last = np.kron(np.eye(beside), last.reshape(2 * LANES, 2 * all_out))
    last = np.concatenate(split(last), axis=1)
    return stage, turn, np.concatenate([last, last])


def halves(values):
    high = values.astype(BF16)
    return high, (values - high.astype(F32)).astype(BF16)


def spectra_kernel(first_stream, partners, outs, gain_ref, *refs):
    frames, refs = refs[:FRAMES], refs[FRAMES:]
    (taps_ref, stage_ref, turn_ref, last_ref), refs = refs[:4], refs[4:]
    out_refs, refs = refs[: max(partners, 1)], refs[max(partners, 1) :]
    (coeff_ref, held_ref), refs = refs[:2], refs[2:]
    groups = STEP // GROUP
    halves_refs, turned_refs = refs[:groups], refs[groups:]
    outer, inner = pl.program_id(0), pl.program_id(1)
    size = GROUP * WIDE
    beside = last_ref.shape[0] // (4 * LANES)
    columns = beside * outs

    @pl.when((outer == 0) & (inner == 0))
    def _():
        for j in range(TAPS):
            rows = taps_ref[pl.ds(j, AVG, stride=TAPS), :]
            for ri in range(2):
                coeff_ref[j, pl.ds(ri, AVG, stride=2), :] = rows

    def filter_rows(g, u, r):
        rows = slice(r, r + 16)
        coeffs = [coeff_ref[j, rows, :] for j in range(TAPS)]
        samples = [ref[g * GROUP + u, 0, rows, :].astype(F32) for ref in frames]
        for m in range(SPECTRA):
            value = coeffs[0] * samples[m]
            for j in range(1, TAPS):
                value = value + coeffs[j] * samples[m + j]
            for part, kept in enumerate(halves(value)):
                row = part * size + u * WIDE + r
                halves_refs[g][row : row + 16, m * LANES : (m + 1) * LANES] = kept

    def first_part(g, start):
        lanes = slice(start * LANES, (start + 2) * LANES)
        section = jnp.dot(stage_ref[...], halves_refs[g][:, lanes], preferred_element_type=F32)
        turn_real, turn_imag = turn_ref[0], turn_ref[1]
        for u in range(GROUP):
            pair, place = divmod(u, beside)
            for m in range(start, start + 2):
                at = slice((m - start) * LANES, (m - start + 1) * LANES)
                blocks = [section[(4 * u + i) * AVG : (4 * u + i + 1) * AVG, at] for i in range(4)]
                real, imag = blocks[0] + blocks[1], blocks[2] + blocks[3]
                row = pair * WIDTH + m * AVG
                for ri, value in enumerate((real * turn_real - imag * turn_imag, real * turn_imag + imag * turn_real)):
                    for part, kept in enumerate(halves(value)):
                        lane = ((part * beside + place) * 2 + ri) * LANES
                        turned_refs[g][row : row + AVG, lane : lane + LANES] = kept

    def last_part(g, pair):
        rows = slice(pair * WIDTH, (pair + 1) * WIDTH)
        product = jnp.dot(turned_refs[g][rows, :], last_ref[...], preferred_element_type=F32)
        found = (product[:, :columns] + product[:, columns:]).T
        for place in range(beside):
            stream = g * GROUP + pair * beside + place
            factor = gain_ref[(first_stream + outer * ROWS + inner * STEP + stream) // 2]
            factor = factor * (1.0 / (64.0 * math.sqrt(NCHAN)))
            at = pl.multiple_of((inner * STEP + stream) * outs, outs)
            mine = found[place * outs : (place + 1) * outs] * factor
            for half in range(WIDTH // LANES):
                held_ref[half, pl.ds(at, outs), :] = mine[:, half * LANES : (half + 1) * LANES]

    for g in range(groups + 2):
        filters = [(g, u, r) for u in range(GROUP) for r in range(0, WIDE, 16)] if g < groups else []
        firsts = [(g - 1, start) for start in range(0, SPECTRA, 2)] if 1 <= g <= groups else []
        lasts = [(g - 2, pair) for pair in range(GROUP // beside)] if g >= 2 else []
        while filters or firsts or lasts:
            for work, jobs, most in ((first_part, firsts, 1), (filter_rows, filters, 2), (last_part, lasts, 1), (filter_rows, filters, 2)):
                for job in jobs[:most]:
                    work(*job)
                del jobs[:most]

    @pl.when(inner == ROWS // STEP - 1)
    def _():
        me = lax.axis_index("ingest") if partners else 0
        each = outs // len(out_refs)
        for k, out_ref in enumerate(out_refs):
            target = jnp.bitwise_xor(me, k) * each if partners else 0
            for q in range(each):
                for half in range(WIDTH // LANES):
                    rows = held_ref[half, pl.ds(target + q, ROWS, stride=outs), :]
                    out_ref[q, :, half * LANES : (half + 1) * LANES] = rows.astype(BF16)


def spectra(voltages, taps, station_gain, consts, outs, start, stop, partners=0):
    stage, turn, last = consts
    groups = STEP // GROUP
    inner = ROWS // STEP
    pieces = max(partners, 1)
    frame_spec = [
        pl.BlockSpec((STEP, 1, WIDE, LANES), functools.partial(lambda j, a, b: (start // STEP + a * inner + b, j, 0, 0), j))
        for j in range(FRAMES)
    ]
    whole = lambda shape: pl.BlockSpec(shape, lambda a, b: (0,) * len(shape))
    return pl.pallas_call(
        functools.partial(spectra_kernel, start, partners, outs),
        out_shape=[jax.ShapeDtypeStruct((outs // pieces, stop - start, WIDTH), BF16)] * pieces,
        grid=((stop - start) // ROWS, inner),
        in_specs=[pl.BlockSpec(memory_space=pltpu.SMEM)]
        + frame_spec
        + [whole(taps.shape), whole(stage.shape), whole(turn.shape), whole(last.shape)],
        out_specs=[pl.BlockSpec((outs // pieces, ROWS, WIDTH), lambda a, b: (0, a, 0))] * pieces,
        scratch_shapes=[
            pltpu.VMEM((TAPS, WIDE, LANES), F32),
            pltpu.VMEM((WIDTH // LANES, ROWS * outs, LANES), F32),
        ]
        + [pltpu.VMEM((2 * GROUP * WIDE, SPECTRA * LANES), BF16)] * groups
        + [pltpu.VMEM((4 * GROUP * WIDTH * LANES // last.shape[0], last.shape[0]), BF16)] * groups,
        compiler_params=pltpu.CompilerParams(vmem_limit_bytes=VMEM_LIMIT),
        cost_estimate=pl.CostEstimate(
            flops=(stop - start) * SPECTRA * 12_000_000,
            bytes_accessed=(stop - start) * FRAMES * WIDE * LANES * 4,
            transcendentals=0,
        ),
        name="spectra",
    )(station_gain, *([voltages] * FRAMES), taps, stage, turn, last)


def squares(values):
    values = values.astype(F32)
    values = jnp.sum((values * values).reshape(-1, 8, values.shape[-1]), axis=0)
    return sum(values[:, lane : lane + LANES] for lane in range(0, values.shape[-1], LANES))


def arrange_kernel(pick_ref, part_ref, out_ref, power_ref):
    rows = 2 * STATIONS
    data = jnp.concatenate([part_ref[:, ri].reshape(-1, WIDTH) for ri in range(2)], axis=1)
    power_ref[0] = squares(data)
    for r in range(0, rows, 2 * LANES):
        own = slice(r, r + 2 * LANES)
        out_ref[0, own, :] = jnp.dot(pick_ref[own, :], data, preferred_element_type=F32).astype(BF16)


def arrange(pick, part):
    devices, _, own, width = part.shape
    rows = 2 * STATIONS
    return pl.pallas_call(
        arrange_kernel,
        out_shape=(
            jax.ShapeDtypeStruct((OUT_DEV, rows, 2 * width), BF16),
            jax.ShapeDtypeStruct((OUT_DEV, 8, LANES), F32),
        ),
        grid=(OUT_DEV,),
        in_specs=[
            pl.BlockSpec(pick.shape, lambda o: (0, 0)),
            pl.BlockSpec((devices, 2, own, width), lambda o: (0, o, 0, 0)),
        ],
        out_specs=(
            pl.BlockSpec((1, rows, 2 * width), lambda o: (o, 0, 0)),
            pl.BlockSpec((1, 8, LANES), lambda o: (o, 0, 0)),
        ),
        compiler_params=pltpu.CompilerParams(vmem_limit_bytes=40 * 2**20),
        cost_estimate=pl.CostEstimate(flops=1_100_000_000, bytes_accessed=4_000_000, transcendentals=0),
        name="arrange",
    )(pick, part)


def tiles_kernel(late, early_ref, power_ref, *refs):
    (pick_refs, part_refs), refs = (refs[: min(late, 1)], refs[min(late, 1) :][:late]), refs[-3:]
    out_ref, left_ref, right_ref = refs
    rows = 2 * STATIONS
    side = 2 * BLOCK
    blocks = STATIONS // BLOCK
    total = power_ref[0]
    if late:
        data = [jnp.concatenate([part_ref[ri] for part_ref in part_refs], axis=0) for ri in range(2)]
        data = jnp.concatenate(data, axis=1)
        total = total + squares(data)
    power = jnp.sum(total) / (STATIONS * 2 * SPECTRA * AVG)
    scale = 1.0 / jnp.full((1, LANES), SPECTRA * AVG * power, F32)
    for r in range(0, rows, 2 * side):
        own = slice(r, r + 2 * side)
        found = early_ref[0, own, :]
        if late:
            found = (jnp.dot(pick_refs[0][own, :], data, preferred_element_type=F32) + found.astype(F32)).astype(BF16)
        right_ref[own, :] = found
        for p in range(2):
            mine = found[p * side : (p + 1) * side]
            at = 2 * r + p * 2 * side
            left_ref[at : at + side, :] = mine
            left_ref[at + side : at + 2 * side, :WIDTH] = mine[:, WIDTH:]
            left_ref[at + side : at + 2 * side, WIDTH:] = -mine[:, :WIDTH]
    for c in range(0, blocks, 2):
        right = right_ref[c * side : (c + 2) * side, :]
        for b in range(c, blocks):
            left = left_ref[b * 2 * side : (b + 1) * 2 * side, :]
            product = lax.dot_general(left, right, NT, preferred_element_type=F32)
            for p in range(2):
                if c + p <= b:
                    tile = b * (b + 1) // 2 + c + p
                    scaled = (product[:, p * side : (p + 1) * side] * scale).astype(BF16)
                    out_ref[0, tile, 0] = scaled[:side]
                    out_ref[0, tile, 1] = scaled[side:]


def tiles(early, power, picks, parts):
    blocks = STATIONS // BLOCK
    pairs = blocks * (blocks + 1) // 2
    side = 2 * BLOCK
    rows = 2 * STATIONS
    return pl.pallas_call(
        functools.partial(tiles_kernel, len(parts)),
        out_shape=jax.ShapeDtypeStruct((OUT_DEV, pairs, 2, side, side), BF16),
        grid=(OUT_DEV,),
        in_specs=[
            pl.BlockSpec((1, rows, 2 * WIDTH), lambda o: (o, 0, 0)),
            pl.BlockSpec((1, 8, LANES), lambda o: (o, 0, 0)),
        ]
        + [pl.BlockSpec(pick.shape, lambda o: (0, 0)) for pick in picks]
        + [pl.BlockSpec((2,) + part.shape[1:], lambda o: (o, 0, 0)) for part in parts],
        out_specs=pl.BlockSpec((1, pairs, 2, side, side), lambda o: (o, 0, 0, 0, 0)),
        scratch_shapes=[
            pltpu.VMEM((2 * rows, 2 * WIDTH), BF16),
            pltpu.VMEM((rows, 2 * WIDTH), BF16),
        ],
        compiler_params=pltpu.CompilerParams(vmem_limit_bytes=40 * 2**20),
        cost_estimate=pl.CostEstimate(flops=4_500_000_000, bytes_accessed=9_000_000, transcendentals=0),
        name="tiles",
    )(early, power, *picks, *parts)


def body(voltages, taps, station_gain, station_order):
    devices = lax.axis_size("ingest")
    streams = 2 * voltages.shape[0]
    blocks = NCHAN // LANES
    outs = 2 * OUT_DEV * devices
    consts = tables(OUT_DEV * devices)
    samples = voltages.reshape(streams, 2, FRAMES * blocks, LANES).transpose(0, 2, 1, 3)
    samples = samples.reshape(streams, FRAMES, 2 * blocks, LANES)
    coeffs = taps.reshape(TAPS, blocks, LANES).transpose(1, 0, 2).reshape(TAPS * blocks, LANES)
    cut = min(streams, ROWS)
    wanted = (2 * station_order[:, None] + jnp.arange(2, dtype=jnp.int32)).reshape(-1, 1)

    def pick(start, stop, first):
        place = np.arange(devices * (stop - start), dtype=np.int32)
        source = jnp.bitwise_xor(place // (stop - start), first) * streams + start + place % (stop - start)
        return (wanted == source).astype(BF16)

    packed = spectra(samples, coeffs, station_gain, consts, outs, 0, cut)[0]
    packed = packed.reshape(devices, 2 * OUT_DEV, cut, WIDTH)
    packed, station_gain = lax.optimization_barrier((packed, station_gain))
    early = lax.all_to_all(packed, "ingest", split_axis=0, concat_axis=0, tiled=True)
    picks, late = [], []
    if cut < streams:
        sent = spectra(samples, coeffs, station_gain, consts, outs, cut, streams, devices)
        late = [sent[0]]
        for k in range(1, devices):
            ready = sent[k]
            if k > WINDOW:
                ready, late[k - WINDOW] = lax.optimization_barrier((ready, late[k - WINDOW]))
            late.append(lax.ppermute(ready, "ingest", [(i, i ^ k) for i in range(devices)]))
        picks = [pick(cut, streams, lax.axis_index("ingest"))]
    rows, power = arrange(pick(0, cut, 0), early)
    return tiles(rows, power, picks, late)


def solution(mesh):
    return jax.shard_map(
        body,
        mesh=mesh,
        in_specs=(P(("band", "ingest"), None, None, None), P(), P("ingest"), P()),
        out_specs=P(("band", "ingest"), None, None, None, None),
        check_vma=False,
    )
```

```python
import functools
import math

import jax
import jax.numpy as jnp
import ml_dtypes
import numpy as np
from jax import lax
from jax.experimental import pallas as pl
from jax.experimental.pallas import tpu as pltpu
from jax.sharding import PartitionSpec as P

STATIONS = 512
NCHAN = 4096
BLOCK = 64
TAPS = 4
SPECTRA = 8
FRAMES = SPECTRA + TAPS - 1
AVG = 32
OUT_DEV = 2
LANES = 128
WIDE = 2 * AVG
WIDTH = SPECTRA * AVG
GROUP = 2
STEP = 8
ROWS = 16
WINDOW = 5
VMEM_LIMIT = 60_000_000
BF16 = jnp.bfloat16
F32 = jnp.float32
NT = (((1,), (1,)), ((), ()))


def split(values):
    high = values.astype(ml_dtypes.bfloat16)
    low = (values - high.astype(np.float64)).astype(ml_dtypes.bfloat16)
    return high, low


def tables(all_out):
    blocks = NCHAN // LANES
    angle = 2.0 * math.pi * (np.outer(np.arange(AVG), np.arange(blocks)) % blocks) / blocks
    cos, sin = np.cos(angle), np.sin(angle)
    stage = np.zeros((2, AVG, blocks, 2))
    stage[0, :, :, 0], stage[0, :, :, 1] = cos, sin
    stage[1, :, :, 0], stage[1, :, :, 1] = -sin, cos
    stage = np.stack(split(stage), axis=1).reshape(4 * AVG, 2 * blocks)
    stage = np.concatenate([np.kron(np.eye(GROUP), stage.astype(np.float32))] * 2, axis=1).astype(ml_dtypes.bfloat16)
    angle = 2.0 * math.pi * np.outer(np.arange(AVG), np.arange(LANES)) / NCHAN
    turn = np.stack([np.cos(angle), -np.sin(angle)]).astype(np.float32)
    first = (NCHAN - all_out * AVG) // 2
    bins = first // AVG + np.arange(all_out)
    angle = 2.0 * math.pi * (np.outer(np.arange(LANES), bins) % LANES) / LANES
    cos, sin = np.cos(angle), np.sin(angle)
    last = np.zeros((2, LANES, all_out, 2))
    last[0, :, :, 0], last[0, :, :, 1] = cos, -sin
    last[1, :, :, 0], last[1, :, :, 1] = sin, cos
    beside = max(1, LANES // (2 * all_out))
    last = np.kron(np.eye(beside), last.reshape(2 * LANES, 2 * all_out))
    last = np.concatenate(split(last), axis=1)
    return stage, turn, np.concatenate([last, last])


def halves(values):
    high = values.astype(BF16)
    return high, (values - high.astype(F32)).astype(BF16)


def spectra_kernel(first_stream, partners, outs, gain_ref, *refs):
    frames, refs = refs[:FRAMES], refs[FRAMES:]
    (taps_ref, stage_ref, turn_ref, last_ref), refs = refs[:4], refs[4:]
    out_refs, refs = refs[: max(partners, 1)], refs[max(partners, 1) :]
    (coeff_ref, held_ref), refs = refs[:2], refs[2:]
    groups = STEP // GROUP
    halves_refs, turned_refs = refs[:groups], refs[groups:]
    outer, inner = pl.program_id(0), pl.program_id(1)
    size = GROUP * WIDE
    beside = last_ref.shape[0] // (4 * LANES)
    columns = beside * outs

    @pl.when((outer == 0) & (inner == 0))
    def _():
        for j in range(TAPS):
            rows = taps_ref[pl.ds(j, AVG, stride=TAPS), :]
            for ri in range(2):
                coeff_ref[j, pl.ds(ri, AVG, stride=2), :] = rows

    def filter_rows(g, u, r):
        rows = slice(r, r + 16)
        coeffs = [coeff_ref[j, rows, :] for j in range(TAPS)]
        samples = [ref[g * GROUP + u, 0, rows, :].astype(F32) for ref in frames]
        for m in range(SPECTRA):
            value = coeffs[0] * samples[m]
            for j in range(1, TAPS):
                value = value + coeffs[j] * samples[m + j]
            for part, kept in enumerate(halves(value)):
                row = part * size + u * WIDE + r
                halves_refs[g][row : row + 16, m * LANES : (m + 1) * LANES] = kept

    def first_product(g, start):
        lanes = slice(start * LANES, (start + 2) * LANES)
        return jnp.dot(stage_ref[...], halves_refs[g][:, lanes], preferred_element_type=F32)

    def first_rest(g, start, section):
        turn_real, turn_imag = turn_ref[0], turn_ref[1]
        for u in range(GROUP):
            pair, place = divmod(u, beside)
            for m in range(start, start + 2):
                at = slice((m - start) * LANES, (m - start + 1) * LANES)
                blocks = [section[(4 * u + i) * AVG : (4 * u + i + 1) * AVG, at] for i in range(4)]
                real, imag = blocks[0] + blocks[1], blocks[2] + blocks[3]
                row = pair * WIDTH + m * AVG
                for ri, value in enumerate((real * turn_real - imag * turn_imag, real * turn_imag + imag * turn_real)):
                    for part, kept in enumerate(halves(value)):
                        lane = ((part * beside + place) * 2 + ri) * LANES
                        turned_refs[g][row : row + AVG, lane : lane + LANES] = kept

    def last_product(g, pair):
        rows = slice(pair * WIDTH, (pair + 1) * WIDTH)
        return jnp.dot(turned_refs[g][rows, :], last_ref[...], preferred_element_type=F32)

    def last_rest(g, pair, product):
        found = (product[:, :columns] + product[:, columns:]).T
        for place in range(beside):
            stream = g * GROUP + pair * beside + place
            factor = gain_ref[(first_stream + outer * ROWS + inner * STEP + stream) // 2]
            factor = factor * (1.0 / (64.0 * math.sqrt(NCHAN)))
            at = pl.multiple_of((inner * STEP + stream) * outs, outs)
            mine = found[place * outs : (place + 1) * outs] * factor
            for half in range(WIDTH // LANES):
                held_ref[half, pl.ds(at, outs), :] = mine[:, half * LANES : (half + 1) * LANES]

    waiting = []
    for g in range(groups + 3):
        filters = [(g, u, r) for u in range(GROUP) for r in range(0, WIDE, 16)] if g < groups else []
        units = [(first_product, first_rest, g - 1, start) for start in range(0, SPECTRA, 2)] if 1 <= g <= groups else []
        if 3 <= g:
            units += [(last_product, last_rest, g - 3, pair) for pair in range(GROUP // beside)]
        while filters or units:
            if units:
                product, rest, *job = units.pop(0)
                waiting.append((rest, job, product(*job)))
            for job in filters[:2]:
                filter_rows(*job)
            del filters[:2]
            if len(waiting) > 1 or not units:
                for rest, job, result in waiting[:1]:
                    rest(*job, result)
                del waiting[:1]
    for rest, job, result in waiting:
        rest(*job, result)

    @pl.when(inner == ROWS // STEP - 1)
    def _():
        me = lax.axis_index("ingest") if partners else 0
        each = outs // len(out_refs)
        for k, out_ref in enumerate(out_refs):
            target = jnp.bitwise_xor(me, k) * each if partners else 0
            for q in range(each):
                for half in range(WIDTH // LANES):
                    rows = held_ref[half, pl.ds(target + q, ROWS, stride=outs), :]
                    out_ref[q, :, half * LANES : (half + 1) * LANES] = rows.astype(BF16)


def spectra(voltages, taps, station_gain, consts, outs, start, stop, partners=0):
    stage, turn, last = consts
    groups = STEP // GROUP
    inner = ROWS // STEP
    pieces = max(partners, 1)
    frame_spec = [
        pl.BlockSpec((STEP, 1, WIDE, LANES), functools.partial(lambda j, a, b: (start // STEP + a * inner + b, j, 0, 0), j))
        for j in range(FRAMES)
    ]
    whole = lambda shape: pl.BlockSpec(shape, lambda a, b: (0,) * len(shape))
    return pl.pallas_call(
        functools.partial(spectra_kernel, start, partners, outs),
        out_shape=[jax.ShapeDtypeStruct((outs // pieces, stop - start, WIDTH), BF16)] * pieces,
        grid=((stop - start) // ROWS, inner),
        in_specs=[pl.BlockSpec(memory_space=pltpu.SMEM)]
        + frame_spec
        + [whole(taps.shape), whole(stage.shape), whole(turn.shape), whole(last.shape)],
        out_specs=[pl.BlockSpec((outs // pieces, ROWS, WIDTH), lambda a, b: (0, a, 0))] * pieces,
        scratch_shapes=[
            pltpu.VMEM((TAPS, WIDE, LANES), F32),
            pltpu.VMEM((WIDTH // LANES, ROWS * outs, LANES), F32),
        ]
        + [pltpu.VMEM((2 * GROUP * WIDE, SPECTRA * LANES), BF16)] * groups
        + [pltpu.VMEM((4 * GROUP * WIDTH * LANES // last.shape[0], last.shape[0]), BF16)] * groups,
        compiler_params=pltpu.CompilerParams(vmem_limit_bytes=VMEM_LIMIT),
        cost_estimate=pl.CostEstimate(
            flops=(stop - start) * SPECTRA * 12_000_000,
            bytes_accessed=(stop - start) * FRAMES * WIDE * LANES * 4,
            transcendentals=0,
        ),
        name="spectra",
    )(station_gain, *([voltages] * FRAMES), taps, stage, turn, last)


def squares(values):
    values = values.astype(F32)
    values = jnp.sum((values * values).reshape(-1, 8, values.shape[-1]), axis=0)
    return sum(values[:, lane : lane + LANES] for lane in range(0, values.shape[-1], LANES))


def arrange_kernel(pick_ref, part_ref, out_ref, power_ref):
    rows = 2 * STATIONS
    data = jnp.concatenate([part_ref[:, ri].reshape(-1, WIDTH) for ri in range(2)], axis=1)
    power_ref[0] = squares(data)
    for r in range(0, rows, 2 * LANES):
        own = slice(r, r + 2 * LANES)
        out_ref[0, own, :] = jnp.dot(pick_ref[own, :], data, preferred_element_type=F32).astype(BF16)


def arrange(pick, part):
    devices, _, own, width = part.shape
    rows = 2 * STATIONS
    return pl.pallas_call(
        arrange_kernel,
        out_shape=(
            jax.ShapeDtypeStruct((OUT_DEV, rows, 2 * width), BF16),
            jax.ShapeDtypeStruct((OUT_DEV, 8, LANES), F32),
        ),
        grid=(OUT_DEV,),
        in_specs=[
            pl.BlockSpec(pick.shape, lambda o: (0, 0)),
            pl.BlockSpec((devices, 2, own, width), lambda o: (0, o, 0, 0)),
        ],
        out_specs=(
            pl.BlockSpec((1, rows, 2 * width), lambda o: (o, 0, 0)),
            pl.BlockSpec((1, 8, LANES), lambda o: (o, 0, 0)),
        ),
        compiler_params=pltpu.CompilerParams(vmem_limit_bytes=40 * 2**20),
        cost_estimate=pl.CostEstimate(flops=1_100_000_000, bytes_accessed=4_000_000, transcendentals=0),
        name="arrange",
    )(pick, part)


def tiles_kernel(late, early_ref, power_ref, *refs):
    (pick_refs, part_refs), refs = (refs[: min(late, 1)], refs[min(late, 1) :][:late]), refs[-3:]
    out_ref, left_ref, right_ref = refs
    rows = 2 * STATIONS
    side = 2 * BLOCK
    blocks = STATIONS // BLOCK
    total = power_ref[0]
    if late:
        data = [jnp.concatenate([part_ref[ri] for part_ref in part_refs], axis=0) for ri in range(2)]
        data = jnp.concatenate(data, axis=1)
        total = total + squares(data)
    power = jnp.sum(total) / (STATIONS * 2 * SPECTRA * AVG)
    scale = 1.0 / jnp.full((1, LANES), SPECTRA * AVG * power, F32)
    for r in range(0, rows, 2 * side):
        own = slice(r, r + 2 * side)
        found = early_ref[0, own, :]
        if late:
            found = (jnp.dot(pick_refs[0][own, :], data, preferred_element_type=F32) + found.astype(F32)).astype(BF16)
        right_ref[own, :] = found
        for p in range(2):
            mine = found[p * side : (p + 1) * side]
            at = 2 * r + p * 2 * side
            left_ref[at : at + side, :] = mine
            left_ref[at + side : at + 2 * side, :WIDTH] = mine[:, WIDTH:]
            left_ref[at + side : at + 2 * side, WIDTH:] = -mine[:, :WIDTH]
    for c in range(0, blocks, 2):
        right = right_ref[c * side : (c + 2) * side, :]
        for b in range(c, blocks):
            left = left_ref[b * 2 * side : (b + 1) * 2 * side, :]
            product = lax.dot_general(left, right, NT, preferred_element_type=F32)
            for p in range(2):
                if c + p <= b:
                    tile = b * (b + 1) // 2 + c + p
                    scaled = (product[:, p * side : (p + 1) * side] * scale).astype(BF16)
                    out_ref[0, tile, 0] = scaled[:side]
                    out_ref[0, tile, 1] = scaled[side:]


def tiles(early, power, picks, parts):
    blocks = STATIONS // BLOCK
    pairs = blocks * (blocks + 1) // 2
    side = 2 * BLOCK
    rows = 2 * STATIONS
    return pl.pallas_call(
        functools.partial(tiles_kernel, len(parts)),
        out_shape=jax.ShapeDtypeStruct((OUT_DEV, pairs, 2, side, side), BF16),
        grid=(OUT_DEV,),
        in_specs=[
            pl.BlockSpec((1, rows, 2 * WIDTH), lambda o: (o, 0, 0)),
            pl.BlockSpec((1, 8, LANES), lambda o: (o, 0, 0)),
        ]
        + [pl.BlockSpec(pick.shape, lambda o: (0, 0)) for pick in picks]
        + [pl.BlockSpec((2,) + part.shape[1:], lambda o: (o, 0, 0)) for part in parts],
        out_specs=pl.BlockSpec((1, pairs, 2, side, side), lambda o: (o, 0, 0, 0, 0)),
        scratch_shapes=[
            pltpu.VMEM((2 * rows, 2 * WIDTH), BF16),
            pltpu.VMEM((rows, 2 * WIDTH), BF16),
        ],
        compiler_params=pltpu.CompilerParams(vmem_limit_bytes=40 * 2**20),
        cost_estimate=pl.CostEstimate(flops=4_500_000_000, bytes_accessed=9_000_000, transcendentals=0),
        name="tiles",
    )(early, power, *picks, *parts)


def sending_order(devices):
    far, near = list(range(devices // 2, devices)), list(range(1, devices // 2))
    order, near = near[:4], near[4:]
    while far or near:
        order += far[:1] + near[:1]
        far, near = far[1:], near[1:]
    return order


def body(voltages, taps, station_gain, station_order):
    devices = lax.axis_size("ingest")
    streams = 2 * voltages.shape[0]
    blocks = NCHAN // LANES
    outs = 2 * OUT_DEV * devices
    consts = tables(OUT_DEV * devices)
    samples = voltages.reshape(streams, 2, FRAMES * blocks, LANES).transpose(0, 2, 1, 3)
    samples = samples.reshape(streams, FRAMES, 2 * blocks, LANES)
    coeffs = taps.reshape(TAPS, blocks, LANES).transpose(1, 0, 2).reshape(TAPS * blocks, LANES)
    cut = streams - streams // (2 * ROWS) * ROWS
    wanted = (2 * station_order[:, None] + jnp.arange(2, dtype=jnp.int32)).reshape(-1, 1)

    def pick(start, stop, first):
        place = np.arange(devices * (stop - start), dtype=np.int32)
        source = jnp.bitwise_xor(place // (stop - start), first) * streams + start + place % (stop - start)
        return (wanted == source).astype(BF16)

    packed = spectra(samples, coeffs, station_gain, consts, outs, 0, cut)[0]
    packed = packed.reshape(devices, 2 * OUT_DEV, cut, WIDTH)
    packed, station_gain = lax.optimization_barrier((packed, station_gain))
    early = lax.all_to_all(packed, "ingest", split_axis=0, concat_axis=0, tiled=True)
    picks, late = [], []
    if cut < streams:
        sent = spectra(samples, coeffs, station_gain, consts, outs, cut, streams, devices)
        received = {0: sent[0]}
        order = sending_order(devices)
        for place, k in enumerate(order):
            ready = sent[k]
            if place >= WINDOW:
                past = order[place - WINDOW]
                ready, received[past] = lax.optimization_barrier((ready, received[past]))
            received[k] = lax.ppermute(ready, "ingest", [(i, i ^ k) for i in range(devices)])
        late = [received[k] for k in range(devices)]
        picks = [pick(cut, streams, lax.axis_index("ingest"))]
    rows, power = arrange(pick(0, cut, 0), early)
    return tiles(rows, power, picks, late)


def solution(mesh):
    return jax.shard_map(
        body,
        mesh=mesh,
        in_specs=(P(("band", "ingest"), None, None, None), P(), P("ingest"), P()),
        out_specs=P(("band", "ingest"), None, None, None, None),
        check_vma=False,
    )
```

```python
import functools
import math

import jax
import jax.numpy as jnp
import ml_dtypes
import numpy as np
from jax import lax
from jax.experimental import pallas as pl
from jax.experimental.pallas import tpu as pltpu
from jax.sharding import PartitionSpec as P

STATIONS = 512
NCHAN = 4096
BLOCK = 64
TAPS = 4
SPECTRA = 8
FRAMES = SPECTRA + TAPS - 1
AVG = 32
OUT_DEV = 2
LANES = 128
WIDE = 2 * AVG
WIDTH = SPECTRA * AVG
GROUP = 2
STEP = 8
ROWS = 16
WINDOW = 5
VMEM_LIMIT = 60_000_000
BF16 = jnp.bfloat16
F32 = jnp.float32
NT = (((1,), (1,)), ((), ()))


def split(values):
    high = values.astype(ml_dtypes.bfloat16)
    low = (values - high.astype(np.float64)).astype(ml_dtypes.bfloat16)
    return high, low


def tables(all_out):
    blocks = NCHAN // LANES
    angle = 2.0 * math.pi * (np.outer(np.arange(AVG), np.arange(blocks)) % blocks) / blocks
    cos, sin = np.cos(angle), np.sin(angle)
    stage = np.zeros((2, AVG, blocks, 2))
    stage[0, :, :, 0], stage[0, :, :, 1] = cos, sin
    stage[1, :, :, 0], stage[1, :, :, 1] = -sin, cos
    stage = np.stack(split(stage), axis=1).reshape(4 * AVG, 2 * blocks)
    stage = np.concatenate([np.kron(np.eye(GROUP), stage.astype(np.float32))] * 2, axis=1).astype(ml_dtypes.bfloat16)
    angle = 2.0 * math.pi * np.outer(np.arange(AVG), np.arange(LANES)) / NCHAN
    turn = np.stack([np.cos(angle), -np.sin(angle)]).astype(np.float32)
    first = (NCHAN - all_out * AVG) // 2
    bins = first // AVG + np.arange(all_out)
    angle = 2.0 * math.pi * (np.outer(np.arange(LANES), bins) % LANES) / LANES
    cos, sin = np.cos(angle), np.sin(angle)
    last = np.zeros((2, LANES, all_out, 2))
    last[0, :, :, 0], last[0, :, :, 1] = cos, -sin
    last[1, :, :, 0], last[1, :, :, 1] = sin, cos
    beside = max(1, LANES // (2 * all_out))
    last = np.kron(np.eye(beside), last.reshape(2 * LANES, 2 * all_out))
    last = np.concatenate(split(last), axis=1)
    return stage, turn, np.concatenate([last, last])


def halves(values):
    scaled = values * 65537.0
    high = scaled - (scaled - values)
    return high.astype(BF16), (values - high).astype(BF16)


def spectra_kernel(first_stream, partners, outs, gain_ref, *refs):
    frames, refs = refs[:FRAMES], refs[FRAMES:]
    (taps_ref, stage_ref, turn_ref, last_ref), refs = refs[:4], refs[4:]
    out_refs, refs = refs[: max(partners, 1)], refs[max(partners, 1) :]
    (coeff_ref, held_ref), refs = refs[:2], refs[2:]
    groups = STEP // GROUP
    halves_refs, turned_refs = refs[:groups], refs[groups:]
    outer, inner = pl.program_id(0), pl.program_id(1)
    size = GROUP * WIDE
    beside = last_ref.shape[0] // (4 * LANES)
    columns = beside * outs

    @pl.when((outer == 0) & (inner == 0))
    def _():
        for j in range(TAPS):
            rows = taps_ref[pl.ds(j, AVG, stride=TAPS), :]
            for ri in range(2):
                coeff_ref[j, pl.ds(ri, AVG, stride=2), :] = rows

    def filter_rows(g, u, r):
        rows = slice(r, r + 16)
        coeffs = [coeff_ref[j, rows, :] for j in range(TAPS)]
        sums = {}
        for f, ref in enumerate(frames):
            sample = ref[g * GROUP + u, 0, rows, :].astype(F32)
            for m in range(max(f - TAPS + 1, 0), min(f + 1, SPECTRA)):
                term = coeffs[f - m] * sample
                sums[m] = sums[m] + term if m in sums else term
            if f >= TAPS - 1:
                m = f - TAPS + 1
                for part, kept in enumerate(halves(sums.pop(m))):
                    row = part * size + u * WIDE + r
                    halves_refs[g][row : row + 16, m * LANES : (m + 1) * LANES] = kept

    def first_product(g, start):
        lanes = slice(start * LANES, (start + 2) * LANES)
        return jnp.dot(stage_ref[...], halves_refs[g][:, lanes], preferred_element_type=F32)

    def first_rest(g, start, section):
        turn_real, turn_imag = turn_ref[0], turn_ref[1]
        for u in range(GROUP):
            pair, place = divmod(u, beside)
            for m in range(start, start + 2):
                at = slice((m - start) * LANES, (m - start + 1) * LANES)
                blocks = [section[(4 * u + i) * AVG : (4 * u + i + 1) * AVG, at] for i in range(4)]
                real, imag = blocks[0] + blocks[1], blocks[2] + blocks[3]
                row = pair * WIDTH + m * AVG
                for ri, value in enumerate((real * turn_real - imag * turn_imag, real * turn_imag + imag * turn_real)):
                    for part, kept in enumerate(halves(value)):
                        lane = ((part * beside + place) * 2 + ri) * LANES
                        turned_refs[g][row : row + AVG, lane : lane + LANES] = kept

    def last_product(g, pair):
        rows = slice(pair * WIDTH, (pair + 1) * WIDTH)
        return jnp.dot(turned_refs[g][rows, :], last_ref[...], preferred_element_type=F32)

    def last_rest(g, pair, product):
        found = (product[:, :columns] + product[:, columns:]).T
        for place in range(beside):
            stream = g * GROUP + pair * beside + place
            factor = gain_ref[(first_stream + outer * ROWS + inner * STEP + stream) // 2]
            factor = factor * (1.0 / (64.0 * math.sqrt(NCHAN)))
            at = pl.multiple_of((inner * STEP + stream) * outs, outs)
            mine = found[place * outs : (place + 1) * outs] * factor
            for half in range(WIDTH // LANES):
                held_ref[half, pl.ds(at, outs), :] = mine[:, half * LANES : (half + 1) * LANES]

    waiting = []
    for g in range(groups + 3):
        filters = [(g, u, r) for u in range(GROUP) for r in range(0, WIDE, 16)] if g < groups else []
        units = [(first_product, first_rest, g - 1, start) for start in range(0, SPECTRA, 2)] if 1 <= g <= groups else []
        if 3 <= g:
            units += [(last_product, last_rest, g - 3, pair) for pair in range(GROUP // beside)]
        while filters or units:
            if units:
                product, rest, *job = units.pop(0)
                waiting.append((rest, job, product(*job)))
            for job in filters[:2]:
                filter_rows(*job)
            del filters[:2]
            if len(waiting) > 1 or not units:
                for rest, job, result in waiting[:1]:
                    rest(*job, result)
                del waiting[:1]
    for rest, job, result in waiting:
        rest(*job, result)

    @pl.when(inner == ROWS // STEP - 1)
    def _():
        me = lax.axis_index("ingest") if partners else 0
        each = outs // len(out_refs)
        for k, out_ref in enumerate(out_refs):
            target = jnp.bitwise_xor(me, k) * each if partners else 0
            for q in range(each):
                for half in range(WIDTH // LANES):
                    rows = held_ref[half, pl.ds(target + q, ROWS, stride=outs), :]
                    out_ref[q, :, half * LANES : (half + 1) * LANES] = rows.astype(BF16)


def spectra(voltages, taps, station_gain, consts, outs, start, stop, partners=0):
    stage, turn, last = consts
    groups = STEP // GROUP
    inner = ROWS // STEP
    pieces = max(partners, 1)
    frame_spec = [
        pl.BlockSpec((STEP, 1, WIDE, LANES), functools.partial(lambda j, a, b: (start // STEP + a * inner + b, j, 0, 0), j))
        for j in range(FRAMES)
    ]
    whole = lambda shape: pl.BlockSpec(shape, lambda a, b: (0,) * len(shape))
    return pl.pallas_call(
        functools.partial(spectra_kernel, start, partners, outs),
        out_shape=[jax.ShapeDtypeStruct((outs // pieces, stop - start, WIDTH), BF16)] * pieces,
        grid=((stop - start) // ROWS, inner),
        in_specs=[pl.BlockSpec(memory_space=pltpu.SMEM)]
        + frame_spec
        + [whole(taps.shape), whole(stage.shape), whole(turn.shape), whole(last.shape)],
        out_specs=[pl.BlockSpec((outs // pieces, ROWS, WIDTH), lambda a, b: (0, a, 0))] * pieces,
        scratch_shapes=[
            pltpu.VMEM((TAPS, WIDE, LANES), F32),
            pltpu.VMEM((WIDTH // LANES, ROWS * outs, LANES), F32),
        ]
        + [pltpu.VMEM((2 * GROUP * WIDE, SPECTRA * LANES), BF16)] * groups
        + [pltpu.VMEM((4 * GROUP * WIDTH * LANES // last.shape[0], last.shape[0]), BF16)] * groups,
        compiler_params=pltpu.CompilerParams(vmem_limit_bytes=VMEM_LIMIT),
        cost_estimate=pl.CostEstimate(
            flops=(stop - start) * SPECTRA * 12_000_000,
            bytes_accessed=(stop - start) * FRAMES * WIDE * LANES * 4,
            transcendentals=0,
        ),
        name="spectra",
    )(station_gain, *([voltages] * FRAMES), taps, stage, turn, last)


def squares(values):
    values = values.astype(F32)
    values = jnp.sum((values * values).reshape(-1, 8, values.shape[-1]), axis=0)
    return sum(values[:, lane : lane + LANES] for lane in range(0, values.shape[-1], LANES))


def arrange_kernel(pick_ref, part_ref, out_ref, power_ref):
    rows = 2 * STATIONS
    data = jnp.concatenate([part_ref[:, ri].reshape(-1, WIDTH) for ri in range(2)], axis=1)
    power_ref[0] = squares(data)
    for r in range(0, rows, 2 * LANES):
        own = slice(r, r + 2 * LANES)
        out_ref[0, own, :] = jnp.dot(pick_ref[own, :], data, preferred_element_type=F32).astype(BF16)


def arrange(pick, part):
    devices, _, own, width = part.shape
    rows = 2 * STATIONS
    return pl.pallas_call(
        arrange_kernel,
        out_shape=(
            jax.ShapeDtypeStruct((OUT_DEV, rows, 2 * width), BF16),
            jax.ShapeDtypeStruct((OUT_DEV, 8, LANES), F32),
        ),
        grid=(OUT_DEV,),
        in_specs=[
            pl.BlockSpec(pick.shape, lambda o: (0, 0)),
            pl.BlockSpec((devices, 2, own, width), lambda o: (0, o, 0, 0)),
        ],
        out_specs=(
            pl.BlockSpec((1, rows, 2 * width), lambda o: (o, 0, 0)),
            pl.BlockSpec((1, 8, LANES), lambda o: (o, 0, 0)),
        ),
        compiler_params=pltpu.CompilerParams(vmem_limit_bytes=40 * 2**20),
        cost_estimate=pl.CostEstimate(flops=1_100_000_000, bytes_accessed=4_000_000, transcendentals=0),
        name="arrange",
    )(pick, part)


def tiles_kernel(late, early_ref, power_ref, *refs):
    (pick_refs, part_refs), refs = (refs[: min(late, 1)], refs[min(late, 1) :][:late]), refs[-3:]
    out_ref, left_ref, right_ref = refs
    rows = 2 * STATIONS
    side = 2 * BLOCK
    blocks = STATIONS // BLOCK
    total = power_ref[0]
    if late:
        data = [jnp.concatenate([part_ref[ri] for part_ref in part_refs], axis=0) for ri in range(2)]
        data = jnp.concatenate(data, axis=1)
        total = total + squares(data)
    power = jnp.sum(total) / (STATIONS * 2 * SPECTRA * AVG)
    scale = 1.0 / jnp.full((1, LANES), SPECTRA * AVG * power, F32)
    for r in range(0, rows, 2 * side):
        own = slice(r, r + 2 * side)
        found = early_ref[0, own, :]
        if late:
            found = (jnp.dot(pick_refs[0][own, :], data, preferred_element_type=F32) + found.astype(F32)).astype(BF16)
        right_ref[own, :] = found
        for p in range(2):
            mine = found[p * side : (p + 1) * side]
            at = 2 * r + p * 2 * side
            left_ref[at : at + side, :] = mine
            left_ref[at + side : at + 2 * side, :WIDTH] = mine[:, WIDTH:]
            left_ref[at + side : at + 2 * side, WIDTH:] = -mine[:, :WIDTH]
    for c in range(0, blocks, 2):
        right = right_ref[c * side : (c + 2) * side, :]
        for b in range(c, blocks):
            left = left_ref[b * 2 * side : (b + 1) * 2 * side, :]
            product = lax.dot_general(left, right, NT, preferred_element_type=F32)
            for p in range(2):
                if c + p <= b:
                    tile = b * (b + 1) // 2 + c + p
                    scaled = (product[:, p * side : (p + 1) * side] * scale).astype(BF16)
                    out_ref[0, tile, 0] = scaled[:side]
                    out_ref[0, tile, 1] = scaled[side:]


def tiles(early, power, picks, parts):
    blocks = STATIONS // BLOCK
    pairs = blocks * (blocks + 1) // 2
    side = 2 * BLOCK
    rows = 2 * STATIONS
    return pl.pallas_call(
        functools.partial(tiles_kernel, len(parts)),
        out_shape=jax.ShapeDtypeStruct((OUT_DEV, pairs, 2, side, side), BF16),
        grid=(OUT_DEV,),
        in_specs=[
            pl.BlockSpec((1, rows, 2 * WIDTH), lambda o: (o, 0, 0)),
            pl.BlockSpec((1, 8, LANES), lambda o: (o, 0, 0)),
        ]
        + [pl.BlockSpec(pick.shape, lambda o: (0, 0)) for pick in picks]
        + [pl.BlockSpec((2,) + part.shape[1:], lambda o: (o, 0, 0)) for part in parts],
        out_specs=pl.BlockSpec((1, pairs, 2, side, side), lambda o: (o, 0, 0, 0, 0)),
        scratch_shapes=[
            pltpu.VMEM((2 * rows, 2 * WIDTH), BF16),
            pltpu.VMEM((rows, 2 * WIDTH), BF16),
        ],
        compiler_params=pltpu.CompilerParams(vmem_limit_bytes=40 * 2**20),
        cost_estimate=pl.CostEstimate(flops=4_500_000_000, bytes_accessed=9_000_000, transcendentals=0),
        name="tiles",
    )(early, power, *picks, *parts)


def sending_order(devices):
    far, near = list(range(devices // 2, devices)), list(range(1, devices // 2))
    order, near = near[:4], near[4:]
    while far or near:
        order += far[:1] + near[:1]
        far, near = far[1:], near[1:]
    return order


def body(voltages, taps, station_gain, station_order):
    devices = lax.axis_size("ingest")
    streams = 2 * voltages.shape[0]
    blocks = NCHAN // LANES
    outs = 2 * OUT_DEV * devices
    consts = tables(OUT_DEV * devices)
    samples = voltages.reshape(streams, 2, FRAMES * blocks, LANES).transpose(0, 2, 1, 3)
    samples = samples.reshape(streams, FRAMES, 2 * blocks, LANES)
    coeffs = taps.reshape(TAPS, blocks, LANES).transpose(1, 0, 2).reshape(TAPS * blocks, LANES)
    cut = streams - streams // (2 * ROWS) * ROWS
    wanted = (2 * station_order[:, None] + jnp.arange(2, dtype=jnp.int32)).reshape(-1, 1)

    def pick(start, stop, first):
        place = np.arange(devices * (stop - start), dtype=np.int32)
        source = jnp.bitwise_xor(place // (stop - start), first) * streams + start + place % (stop - start)
        return (wanted == source).astype(BF16)

    packed = spectra(samples, coeffs, station_gain, consts, outs, 0, cut)[0]
    packed = packed.reshape(devices, 2 * OUT_DEV, cut, WIDTH)
    packed, station_gain = lax.optimization_barrier((packed, station_gain))
    early = lax.all_to_all(packed, "ingest", split_axis=0, concat_axis=0, tiled=True)
    picks, late = [], []
    if cut < streams:
        sent = spectra(samples, coeffs, station_gain, consts, outs, cut, streams, devices)
        received = {0: sent[0]}
        order = sending_order(devices)
        for place, k in enumerate(order):
            ready = sent[k]
            if place >= WINDOW:
                past = order[place - WINDOW]
                ready, received[past] = lax.optimization_barrier((ready, received[past]))
            received[k] = lax.ppermute(ready, "ingest", [(i, i ^ k) for i in range(devices)])
        late = [received[k] for k in range(devices)]
        picks = [pick(cut, streams, lax.axis_index("ingest"))]
    rows, power = arrange(pick(0, cut, 0), early)
    return tiles(rows, power, picks, late)


def solution(mesh):
    return jax.shard_map(
        body,
        mesh=mesh,
        in_specs=(P(("band", "ingest"), None, None, None), P(), P("ingest"), P()),
        out_specs=P(("band", "ingest"), None, None, None, None),
        check_vma=False,
    )
```

```python
import functools
import math

import jax
import jax.numpy as jnp
import ml_dtypes
import numpy as np
from jax import lax
from jax.experimental import pallas as pl
from jax.experimental.pallas import tpu as pltpu
from jax.sharding import PartitionSpec as P

STATIONS = 512
NCHAN = 4096
BLOCK = 64
TAPS = 4
SPECTRA = 8
FRAMES = SPECTRA + TAPS - 1
AVG = 32
OUT_DEV = 2
LANES = 128
WIDE = 2 * AVG
WIDTH = SPECTRA * AVG
GROUP = 2
STEP = 8
ROWS = 16
WINDOW = 5
VMEM_LIMIT = 60_000_000
BF16 = jnp.bfloat16
F32 = jnp.float32
NT = (((1,), (1,)), ((), ()))


def split(values):
    high = values.astype(ml_dtypes.bfloat16)
    low = (values - high.astype(np.float64)).astype(ml_dtypes.bfloat16)
    return high, low


def tables(all_out):
    blocks = NCHAN // LANES
    angle = 2.0 * math.pi * (np.outer(np.arange(AVG), np.arange(blocks)) % blocks) / blocks
    cos, sin = np.cos(angle), np.sin(angle)
    stage = np.zeros((2, AVG, blocks, 2))
    stage[0, :, :, 0], stage[0, :, :, 1] = cos, sin
    stage[1, :, :, 0], stage[1, :, :, 1] = -sin, cos
    stage = np.stack(split(stage), axis=1).reshape(4 * AVG, 2 * blocks)
    stage = np.concatenate([np.kron(np.eye(GROUP), stage.astype(np.float32))] * 2, axis=1).astype(ml_dtypes.bfloat16)
    angle = 2.0 * math.pi * np.outer(np.arange(AVG), np.arange(LANES)) / NCHAN
    turn = np.stack([np.cos(angle), -np.sin(angle)]).astype(np.float32)
    first = (NCHAN - all_out * AVG) // 2
    bins = first // AVG + np.arange(all_out)
    angle = 2.0 * math.pi * (np.outer(np.arange(LANES), bins) % LANES) / LANES
    cos, sin = np.cos(angle), np.sin(angle)
    last = np.zeros((2, LANES, all_out, 2))
    last[0, :, :, 0], last[0, :, :, 1] = cos, -sin
    last[1, :, :, 0], last[1, :, :, 1] = sin, cos
    beside = max(1, LANES // (2 * all_out))
    last = np.kron(np.eye(beside), last.reshape(2 * LANES, 2 * all_out))
    last = np.concatenate(split(last), axis=1)
    return stage.astype(np.float32), turn, np.concatenate([last, last]).astype(np.float32)


def halves(values):
    scaled = values * 65537.0
    high = scaled - (scaled - values)
    return high, values - high


def spectra_kernel(first_stream, partners, outs, gain_ref, *refs):
    frames, refs = refs[:FRAMES], refs[FRAMES:]
    (taps_ref, stage_ref, turn_ref, last_ref), refs = refs[:4], refs[4:]
    out_refs, refs = refs[: max(partners, 1)], refs[max(partners, 1) :]
    (coeff_ref, held_ref), refs = refs[:2], refs[2:]
    groups = STEP // GROUP
    halves_refs, turned_refs = refs[:groups], refs[groups:]
    outer, inner = pl.program_id(0), pl.program_id(1)
    size = GROUP * WIDE
    beside = last_ref.shape[0] // (4 * LANES)
    columns = beside * outs

    @pl.when((outer == 0) & (inner == 0))
    def _():
        for j in range(TAPS):
            rows = taps_ref[pl.ds(j, AVG, stride=TAPS), :]
            for ri in range(2):
                coeff_ref[j, pl.ds(ri, AVG, stride=2), :] = rows

    def filter_rows(g, u, r):
        rows = slice(r, r + 16)
        coeffs = [coeff_ref[j, rows, :] for j in range(TAPS)]
        samples = [ref[g * GROUP + u, 0, rows, :].astype(F32) for ref in frames]
        for m in range(SPECTRA):
            value = coeffs[0] * samples[m]
            for j in range(1, TAPS):
                value = value + coeffs[j] * samples[m + j]
            for part, kept in enumerate(halves(value)):
                row = part * size + u * WIDE + r
                halves_refs[g][row : row + 16, m * LANES : (m + 1) * LANES] = kept

    def first_product(g, start):
        lanes = slice(start * LANES, (start + 2) * LANES)
        return jnp.dot(stage_ref[...], halves_refs[g][:, lanes], preferred_element_type=F32)

    def first_rest(g, start, section):
        turn_real, turn_imag = turn_ref[0], turn_ref[1]
        for u in range(GROUP):
            pair, place = divmod(u, beside)
            for m in range(start, start + 2):
                at = slice((m - start) * LANES, (m - start + 1) * LANES)
                blocks = [section[(4 * u + i) * AVG : (4 * u + i + 1) * AVG, at] for i in range(4)]
                real, imag = blocks[0] + blocks[1], blocks[2] + blocks[3]
                row = pair * WIDTH + m * AVG
                for ri, value in enumerate((real * turn_real - imag * turn_imag, real * turn_imag + imag * turn_real)):
                    for part, kept in enumerate(halves(value)):
                        lane = ((part * beside + place) * 2 + ri) * LANES
                        turned_refs[g][row : row + AVG, lane : lane + LANES] = kept

    def last_product(g, pair):
        rows = slice(pair * WIDTH, (pair + 1) * WIDTH)
        return jnp.dot(turned_refs[g][rows, :], last_ref[...], preferred_element_type=F32)

    def last_rest(g, pair, product):
        found = (product[:, :columns] + product[:, columns:]).T
        for place in range(beside):
            stream = g * GROUP + pair * beside + place
            factor = gain_ref[(first_stream + outer * ROWS + inner * STEP + stream) // 2]
            factor = factor * (1.0 / (64.0 * math.sqrt(NCHAN)))
            at = pl.multiple_of((inner * STEP + stream) * outs, outs)
            mine = found[place * outs : (place + 1) * outs] * factor
            for half in range(WIDTH // LANES):
                held_ref[half, pl.ds(at, outs), :] = mine[:, half * LANES : (half + 1) * LANES]

    waiting = []
    for g in range(groups + 3):
        filters = [(g, u, r) for u in range(GROUP) for r in range(0, WIDE, 16)] if g < groups else []
        units = [(first_product, first_rest, g - 1, start) for start in range(0, SPECTRA, 2)] if 1 <= g <= groups else []
        if 3 <= g:
            units += [(last_product, last_rest, g - 3, pair) for pair in range(GROUP // beside)]
        while filters or units:
            if units:
                product, rest, *job = units.pop(0)
                waiting.append((rest, job, product(*job)))
            for job in filters[:2]:
                filter_rows(*job)
            del filters[:2]
            if len(waiting) > 1 or not units:
                for rest, job, result in waiting[:1]:
                    rest(*job, result)
                del waiting[:1]
    for rest, job, result in waiting:
        rest(*job, result)

    @pl.when(inner == ROWS // STEP - 1)
    def _():
        me = lax.axis_index("ingest") if partners else 0
        each = outs // len(out_refs)
        for k, out_ref in enumerate(out_refs):
            target = jnp.bitwise_xor(me, k) * each if partners else 0
            for q in range(each):
                for half in range(WIDTH // LANES):
                    rows = held_ref[half, pl.ds(target + q, ROWS, stride=outs), :]
                    out_ref[q, :, half * LANES : (half + 1) * LANES] = rows.astype(BF16)


def spectra(voltages, taps, station_gain, consts, outs, start, stop, partners=0):
    stage, turn, last = consts
    groups = STEP // GROUP
    inner = ROWS // STEP
    pieces = max(partners, 1)
    frame_spec = [
        pl.BlockSpec((STEP, 1, WIDE, LANES), functools.partial(lambda j, a, b: (start // STEP + a * inner + b, j, 0, 0), j))
        for j in range(FRAMES)
    ]
    whole = lambda shape: pl.BlockSpec(shape, lambda a, b: (0,) * len(shape))
    return pl.pallas_call(
        functools.partial(spectra_kernel, start, partners, outs),
        out_shape=[jax.ShapeDtypeStruct((outs // pieces, stop - start, WIDTH), BF16)] * pieces,
        grid=((stop - start) // ROWS, inner),
        in_specs=[pl.BlockSpec(memory_space=pltpu.SMEM)]
        + frame_spec
        + [whole(taps.shape), whole(stage.shape), whole(turn.shape), whole(last.shape)],
        out_specs=[pl.BlockSpec((outs // pieces, ROWS, WIDTH), lambda a, b: (0, a, 0))] * pieces,
        scratch_shapes=[
            pltpu.VMEM((TAPS, WIDE, LANES), F32),
            pltpu.VMEM((WIDTH // LANES, ROWS * outs, LANES), F32),
        ]
        + [pltpu.VMEM((2 * GROUP * WIDE, SPECTRA * LANES), F32)] * groups
        + [pltpu.VMEM((4 * GROUP * WIDTH * LANES // last.shape[0], last.shape[0]), F32)] * groups,
        compiler_params=pltpu.CompilerParams(vmem_limit_bytes=VMEM_LIMIT),
        cost_estimate=pl.CostEstimate(
            flops=(stop - start) * SPECTRA * 12_000_000,
            bytes_accessed=(stop - start) * FRAMES * WIDE * LANES * 4,
            transcendentals=0,
        ),
        name="spectra",
    )(station_gain, *([voltages] * FRAMES), taps, stage, turn, last)


def squares(values):
    values = values.astype(F32)
    values = jnp.sum((values * values).reshape(-1, 8, values.shape[-1]), axis=0)
    return sum(values[:, lane : lane + LANES] for lane in range(0, values.shape[-1], LANES))


def arrange_kernel(pick_ref, part_ref, out_ref, power_ref):
    rows = 2 * STATIONS
    data = jnp.concatenate([part_ref[:, ri].reshape(-1, WIDTH) for ri in range(2)], axis=1)
    power_ref[0] = squares(data)
    for r in range(0, rows, 2 * LANES):
        own = slice(r, r + 2 * LANES)
        out_ref[0, own, :] = jnp.dot(pick_ref[own, :], data, preferred_element_type=F32).astype(BF16)


def arrange(pick, part):
    devices, _, own, width = part.shape
    rows = 2 * STATIONS
    return pl.pallas_call(
        arrange_kernel,
        out_shape=(
            jax.ShapeDtypeStruct((OUT_DEV, rows, 2 * width), BF16),
            jax.ShapeDtypeStruct((OUT_DEV, 8, LANES), F32),
        ),
        grid=(OUT_DEV,),
        in_specs=[
            pl.BlockSpec(pick.shape, lambda o: (0, 0)),
            pl.BlockSpec((devices, 2, own, width), lambda o: (0, o, 0, 0)),
        ],
        out_specs=(
            pl.BlockSpec((1, rows, 2 * width), lambda o: (o, 0, 0)),
            pl.BlockSpec((1, 8, LANES), lambda o: (o, 0, 0)),
        ),
        compiler_params=pltpu.CompilerParams(vmem_limit_bytes=40 * 2**20),
        cost_estimate=pl.CostEstimate(flops=1_100_000_000, bytes_accessed=4_000_000, transcendentals=0),
        name="arrange",
    )(pick, part)


def tiles_kernel(late, early_ref, power_ref, *refs):
    (pick_refs, part_refs), refs = (refs[: min(late, 1)], refs[min(late, 1) :][:late]), refs[-3:]
    out_ref, left_ref, right_ref = refs
    rows = 2 * STATIONS
    side = 2 * BLOCK
    blocks = STATIONS // BLOCK
    total = power_ref[0]
    if late:
        data = [jnp.concatenate([part_ref[ri] for part_ref in part_refs], axis=0) for ri in range(2)]
        data = jnp.concatenate(data, axis=1)
        total = total + squares(data)
    power = jnp.sum(total) / (STATIONS * 2 * SPECTRA * AVG)
    scale = 1.0 / jnp.full((1, LANES), SPECTRA * AVG * power, F32)
    for r in range(0, rows, 2 * side):
        own = slice(r, r + 2 * side)
        found = early_ref[0, own, :]
        if late:
            found = (jnp.dot(pick_refs[0][own, :], data, preferred_element_type=F32) + found.astype(F32)).astype(BF16)
        right_ref[own, :] = found
        for p in range(2):
            mine = found[p * side : (p + 1) * side]
            at = 2 * r + p * 2 * side
            left_ref[at : at + side, :] = mine
            left_ref[at + side : at + 2 * side, :WIDTH] = mine[:, WIDTH:]
            left_ref[at + side : at + 2 * side, WIDTH:] = -mine[:, :WIDTH]
    for c in range(0, blocks, 2):
        right = right_ref[c * side : (c + 2) * side, :]
        for b in range(c, blocks):
            left = left_ref[b * 2 * side : (b + 1) * 2 * side, :]
            product = lax.dot_general(left, right, NT, preferred_element_type=F32)
            for p in range(2):
                if c + p <= b:
                    tile = b * (b + 1) // 2 + c + p
                    scaled = (product[:, p * side : (p + 1) * side] * scale).astype(BF16)
                    out_ref[0, tile, 0] = scaled[:side]
                    out_ref[0, tile, 1] = scaled[side:]


def tiles(early, power, picks, parts):
    blocks = STATIONS // BLOCK
    pairs = blocks * (blocks + 1) // 2
    side = 2 * BLOCK
    rows = 2 * STATIONS
    return pl.pallas_call(
        functools.partial(tiles_kernel, len(parts)),
        out_shape=jax.ShapeDtypeStruct((OUT_DEV, pairs, 2, side, side), BF16),
        grid=(OUT_DEV,),
        in_specs=[
            pl.BlockSpec((1, rows, 2 * WIDTH), lambda o: (o, 0, 0)),
            pl.BlockSpec((1, 8, LANES), lambda o: (o, 0, 0)),
        ]
        + [pl.BlockSpec(pick.shape, lambda o: (0, 0)) for pick in picks]
        + [pl.BlockSpec((2,) + part.shape[1:], lambda o: (o, 0, 0)) for part in parts],
        out_specs=pl.BlockSpec((1, pairs, 2, side, side), lambda o: (o, 0, 0, 0, 0)),
        scratch_shapes=[
            pltpu.VMEM((2 * rows, 2 * WIDTH), BF16),
            pltpu.VMEM((rows, 2 * WIDTH), BF16),
        ],
        compiler_params=pltpu.CompilerParams(vmem_limit_bytes=40 * 2**20),
        cost_estimate=pl.CostEstimate(flops=4_500_000_000, bytes_accessed=9_000_000, transcendentals=0),
        name="tiles",
    )(early, power, *picks, *parts)


def sending_order(devices):
    far, near = list(range(devices // 2, devices)), list(range(1, devices // 2))
    order, near = near[:4], near[4:]
    while far or near:
        order += far[:1] + near[:1]
        far, near = far[1:], near[1:]
    return order


def body(voltages, taps, station_gain, station_order):
    devices = lax.axis_size("ingest")
    streams = 2 * voltages.shape[0]
    blocks = NCHAN // LANES
    outs = 2 * OUT_DEV * devices
    consts = tables(OUT_DEV * devices)
    samples = voltages.reshape(streams, 2, FRAMES * blocks, LANES).transpose(0, 2, 1, 3)
    samples = samples.reshape(streams, FRAMES, 2 * blocks, LANES)
    coeffs = taps.reshape(TAPS, blocks, LANES).transpose(1, 0, 2).reshape(TAPS * blocks, LANES)
    cut = max(streams - ROWS, ROWS)
    wanted = (2 * station_order[:, None] + jnp.arange(2, dtype=jnp.int32)).reshape(-1, 1)

    def pick(start, stop, first):
        place = np.arange(devices * (stop - start), dtype=np.int32)
        source = jnp.bitwise_xor(place // (stop - start), first) * streams + start + place % (stop - start)
        return (wanted == source).astype(BF16)

    packed = spectra(samples, coeffs, station_gain, consts, outs, 0, cut)[0]
    packed = packed.reshape(devices, 2 * OUT_DEV, cut, WIDTH)
    packed, station_gain = lax.optimization_barrier((packed, station_gain))
    early = lax.all_to_all(packed, "ingest", split_axis=0, concat_axis=0, tiled=True)
    picks, late = [], []
    if cut < streams:
        sent = spectra(samples, coeffs, station_gain, consts, outs, cut, streams, devices)
        received = {0: sent[0]}
        order = sending_order(devices)
        for place, k in enumerate(order):
            ready = sent[k]
            if place >= WINDOW:
                past = order[place - WINDOW]
                ready, received[past] = lax.optimization_barrier((ready, received[past]))
            received[k] = lax.ppermute(ready, "ingest", [(i, i ^ k) for i in range(devices)])
        late = [received[k] for k in range(devices)]
        picks = [pick(cut, streams, lax.axis_index("ingest"))]
    rows, power = arrange(pick(0, cut, 0), early)
    return tiles(rows, power, picks, late)


def solution(mesh):
    return jax.shard_map(
        body,
        mesh=mesh,
        in_specs=(P(("band", "ingest"), None, None, None), P(), P("ingest"), P()),
        out_specs=P(("band", "ingest"), None, None, None, None),
        check_vma=False,
    )
```

```python
import functools
import math

import jax
import jax.numpy as jnp
import ml_dtypes
import numpy as np
from jax import lax
from jax.experimental import pallas as pl
from jax.experimental.pallas import tpu as pltpu
from jax.sharding import PartitionSpec as P

STATIONS = 512
NCHAN = 4096
BLOCK = 64
TAPS = 4
SPECTRA = 8
FRAMES = SPECTRA + TAPS - 1
AVG = 32
OUT_DEV = 2
LANES = 128
WIDE = 2 * AVG
WIDTH = SPECTRA * AVG
GROUP = 2
STEP = 8
ROWS = 16
WINDOW = 5
VMEM_LIMIT = 60_000_000
BF16 = jnp.bfloat16
F32 = jnp.float32
NT = (((1,), (1,)), ((), ()))


def split(values):
    high = values.astype(ml_dtypes.bfloat16)
    low = (values - high.astype(np.float64)).astype(ml_dtypes.bfloat16)
    return high, low


def tables(all_out):
    blocks = NCHAN // LANES
    angle = 2.0 * math.pi * (np.outer(np.arange(AVG), np.arange(blocks)) % blocks) / blocks
    cos, sin = np.cos(angle), np.sin(angle)
    stage = np.zeros((2, AVG, blocks, 2))
    stage[0, :, :, 0], stage[0, :, :, 1] = cos, sin
    stage[1, :, :, 0], stage[1, :, :, 1] = -sin, cos
    stage = np.stack(split(stage), axis=1).reshape(4 * AVG, 2 * blocks)
    stage = np.concatenate([np.kron(np.eye(GROUP), stage.astype(np.float32))] * 2, axis=1).astype(ml_dtypes.bfloat16)
    angle = 2.0 * math.pi * np.outer(np.arange(AVG), np.arange(LANES)) / NCHAN
    turn = np.stack([np.cos(angle), -np.sin(angle)]).astype(np.float32)
    first = (NCHAN - all_out * AVG) // 2
    bins = first // AVG + np.arange(all_out)
    angle = 2.0 * math.pi * (np.outer(np.arange(LANES), bins) % LANES) / LANES
    cos, sin = np.cos(angle), np.sin(angle)
    last = np.zeros((2, LANES, all_out, 2))
    last[0, :, :, 0], last[0, :, :, 1] = cos, -sin
    last[1, :, :, 0], last[1, :, :, 1] = sin, cos
    beside = max(1, LANES // (2 * all_out))
    last = np.kron(np.eye(beside), last.reshape(2 * LANES, 2 * all_out))
    last = np.concatenate(split(last), axis=1)
    return stage.astype(np.float32), turn, np.concatenate([last, last]).astype(np.float32)


def halves(values):
    scaled = values * 65537.0
    high = scaled - (scaled - values)
    return high, values - high


def spectra_kernel(first_stream, partners, outs, gain_ref, *refs):
    frames, refs = refs[:FRAMES], refs[FRAMES:]
    (taps_ref, stage_ref, turn_ref, last_ref), refs = refs[:4], refs[4:]
    out_refs, refs = refs[: max(partners, 1)], refs[max(partners, 1) :]
    (coeff_ref, held_ref), refs = refs[:2], refs[2:]
    groups = STEP // GROUP
    halves_refs, turned_refs = refs[:groups], refs[groups:]
    outer, inner = pl.program_id(0), pl.program_id(1)
    size = GROUP * WIDE
    beside = last_ref.shape[0] // (4 * LANES)
    columns = beside * outs

    @pl.when((outer == 0) & (inner == 0))
    def _():
        for j in range(TAPS):
            rows = taps_ref[pl.ds(j, AVG, stride=TAPS), :]
            for ri in range(2):
                coeff_ref[j, pl.ds(ri, AVG, stride=2), :] = rows

    def filter_rows(g, u, r):
        rows = slice(r, r + 16)
        coeffs = [coeff_ref[j, rows, :] for j in range(TAPS)]
        samples = [ref[g * GROUP + u, 0, rows, :].astype(F32) for ref in frames]
        for m in range(SPECTRA):
            value = coeffs[0] * samples[m]
            for j in range(1, TAPS):
                value = value + coeffs[j] * samples[m + j]
            for part, kept in enumerate(halves(value)):
                row = part * size + u * WIDE + r
                halves_refs[g][row : row + 16, m * LANES : (m + 1) * LANES] = kept

    def first_product(g, start):
        lanes = slice(start * LANES, (start + 2) * LANES)
        return jnp.dot(stage_ref[...], halves_refs[g][:, lanes], preferred_element_type=F32)

    def first_rest(g, start, section):
        turn_real, turn_imag = turn_ref[0], turn_ref[1]
        for u in range(GROUP):
            pair, place = divmod(u, beside)
            for m in range(start, start + 2):
                at = slice((m - start) * LANES, (m - start + 1) * LANES)
                blocks = [section[(4 * u + i) * AVG : (4 * u + i + 1) * AVG, at] for i in range(4)]
                real, imag = blocks[0] + blocks[1], blocks[2] + blocks[3]
                row = pair * WIDTH + m * AVG
                for ri, value in enumerate((real * turn_real - imag * turn_imag, real * turn_imag + imag * turn_real)):
                    for part, kept in enumerate(halves(value)):
                        lane = ((part * beside + place) * 2 + ri) * LANES
                        turned_refs[g][row : row + AVG, lane : lane + LANES] = kept

    def last_product(g, pair):
        rows = slice(pair * WIDTH, (pair + 1) * WIDTH)
        return jnp.dot(turned_refs[g][rows, :], last_ref[...], preferred_element_type=F32)

    def last_rest(g, pair, product):
        found = (product[:, :columns] + product[:, columns:]).T
        for place in range(beside):
            stream = g * GROUP + pair * beside + place
            factor = gain_ref[(first_stream + outer * ROWS + inner * STEP + stream) // 2]
            factor = factor * (1.0 / (64.0 * math.sqrt(NCHAN)))
            at = pl.multiple_of((inner * STEP + stream) * outs, outs)
            mine = found[place * outs : (place + 1) * outs] * factor
            for half in range(WIDTH // LANES):
                held_ref[half, pl.ds(at, outs), :] = mine[:, half * LANES : (half + 1) * LANES]

    waiting = []
    for g in range(groups + 3):
        filters = [(g, u, r) for u in range(GROUP) for r in range(0, WIDE, 16)] if g < groups else []
        units = [(first_product, first_rest, g - 1, start) for start in range(0, SPECTRA, 2)] if 1 <= g <= groups else []
        if 3 <= g:
            units += [(last_product, last_rest, g - 3, pair) for pair in range(GROUP // beside)]
        while filters or units:
            if units:
                product, rest, *job = units.pop(0)
                waiting.append((rest, job, product(*job)))
            for job in filters[:2]:
                filter_rows(*job)
            del filters[:2]
            if len(waiting) > 1 or not units:
                for rest, job, result in waiting[:1]:
                    rest(*job, result)
                del waiting[:1]
    for rest, job, result in waiting:
        rest(*job, result)

    @pl.when(inner == ROWS // STEP - 1)
    def _():
        me = lax.axis_index("ingest") if partners else 0
        each = outs // len(out_refs)
        for k, out_ref in enumerate(out_refs):
            target = jnp.bitwise_xor(me, k) * each if partners else 0
            for q in range(each):
                for half in range(WIDTH // LANES):
                    rows = held_ref[half, pl.ds(target + q, ROWS, stride=outs), :]
                    out_ref[q, :, half * LANES : (half + 1) * LANES] = rows.astype(BF16)


def spectra(voltages, taps, station_gain, consts, outs, start, stop, partners=0):
    stage, turn, last = consts
    groups = STEP // GROUP
    inner = ROWS // STEP
    pieces = max(partners, 1)
    frame_spec = [
        pl.BlockSpec((STEP, 1, WIDE, LANES), functools.partial(lambda j, a, b: (start // STEP + a * inner + b, j, 0, 0), j))
        for j in range(FRAMES)
    ]
    whole = lambda shape: pl.BlockSpec(shape, lambda a, b: (0,) * len(shape))
    return pl.pallas_call(
        functools.partial(spectra_kernel, start, partners, outs),
        out_shape=[jax.ShapeDtypeStruct((outs // pieces, stop - start, WIDTH), BF16)] * pieces,
        grid=((stop - start) // ROWS, inner),
        in_specs=[pl.BlockSpec(memory_space=pltpu.SMEM)]
        + frame_spec
        + [whole(taps.shape), whole(stage.shape), whole(turn.shape), whole(last.shape)],
        out_specs=[pl.BlockSpec((outs // pieces, ROWS, WIDTH), lambda a, b: (0, a, 0))] * pieces,
        scratch_shapes=[
            pltpu.VMEM((TAPS, WIDE, LANES), F32),
            pltpu.VMEM((WIDTH // LANES, ROWS * outs, LANES), F32),
        ]
        + [pltpu.VMEM((2 * GROUP * WIDE, SPECTRA * LANES), F32)] * groups
        + [pltpu.VMEM((4 * GROUP * WIDTH * LANES // last.shape[0], last.shape[0]), F32)] * groups,
        compiler_params=pltpu.CompilerParams(vmem_limit_bytes=VMEM_LIMIT),
        cost_estimate=pl.CostEstimate(
            flops=(stop - start) * SPECTRA * 12_000_000,
            bytes_accessed=(stop - start) * FRAMES * WIDE * LANES * 4,
            transcendentals=0,
        ),
        name="spectra",
    )(station_gain, *([voltages] * FRAMES), taps, stage, turn, last)


def squares(values):
    values = values.astype(F32)
    values = jnp.sum((values * values).reshape(-1, 8, values.shape[-1]), axis=0)
    return sum(values[:, lane : lane + LANES] for lane in range(0, values.shape[-1], LANES))


def arrange_kernel(pick_ref, part_ref, out_ref, power_ref):
    rows = 2 * STATIONS
    data = jnp.concatenate([part_ref[:, ri].reshape(-1, WIDTH) for ri in range(2)], axis=1)
    power_ref[0] = squares(data)
    for r in range(0, rows, 2 * LANES):
        own = slice(r, r + 2 * LANES)
        out_ref[0, own, :] = jnp.dot(pick_ref[own, :], data, preferred_element_type=F32).astype(BF16)


def arrange(pick, part):
    devices, _, own, width = part.shape
    rows = 2 * STATIONS
    return pl.pallas_call(
        arrange_kernel,
        out_shape=(
            jax.ShapeDtypeStruct((OUT_DEV, rows, 2 * width), BF16),
            jax.ShapeDtypeStruct((OUT_DEV, 8, LANES), F32),
        ),
        grid=(OUT_DEV,),
        in_specs=[
            pl.BlockSpec(pick.shape, lambda o: (0, 0)),
            pl.BlockSpec((devices, 2, own, width), lambda o: (0, o, 0, 0)),
        ],
        out_specs=(
            pl.BlockSpec((1, rows, 2 * width), lambda o: (o, 0, 0)),
            pl.BlockSpec((1, 8, LANES), lambda o: (o, 0, 0)),
        ),
        compiler_params=pltpu.CompilerParams(vmem_limit_bytes=40 * 2**20),
        cost_estimate=pl.CostEstimate(flops=1_100_000_000, bytes_accessed=4_000_000, transcendentals=0),
        name="arrange",
    )(pick, part)


def tiles_kernel(late, early_ref, power_ref, *refs):
    (pick_refs, part_refs), refs = (refs[: min(late, 1)], refs[min(late, 1) :][:late]), refs[-3:]
    out_ref, left_ref, right_ref = refs
    rows = 2 * STATIONS
    side = 2 * BLOCK
    blocks = STATIONS // BLOCK
    total = power_ref[0]
    if late:
        data = [jnp.concatenate([part_ref[ri] for part_ref in part_refs], axis=0) for ri in range(2)]
        data = jnp.concatenate(data, axis=1)
        total = total + squares(data)
    power = jnp.sum(total) / (STATIONS * 2 * SPECTRA * AVG)
    scale = 1.0 / jnp.full((1, LANES), SPECTRA * AVG * power, F32)
    for r in range(0, rows, 2 * side):
        own = slice(r, r + 2 * side)
        found = early_ref[0, own, :]
        if late:
            found = (jnp.dot(pick_refs[0][own, :], data, preferred_element_type=F32) + found.astype(F32)).astype(BF16)
        right_ref[own, :] = found
        for p in range(2):
            mine = found[p * side : (p + 1) * side]
            at = 2 * r + p * 2 * side
            left_ref[at : at + side, :] = mine
            left_ref[at + side : at + 2 * side, :WIDTH] = mine[:, WIDTH:]
            left_ref[at + side : at + 2 * side, WIDTH:] = -mine[:, :WIDTH]
    for c in range(0, blocks, 2):
        right = right_ref[c * side : (c + 2) * side, :]
        for b in range(c, blocks):
            left = left_ref[b * 2 * side : (b + 1) * 2 * side, :]
            product = lax.dot_general(left, right, NT, preferred_element_type=F32)
            for p in range(2):
                if c + p <= b:
                    tile = b * (b + 1) // 2 + c + p
                    scaled = (product[:, p * side : (p + 1) * side] * scale).astype(BF16)
                    out_ref[0, tile, 0] = scaled[:side]
                    out_ref[0, tile, 1] = scaled[side:]


def tiles(early, power, picks, parts):
    blocks = STATIONS // BLOCK
    pairs = blocks * (blocks + 1) // 2
    side = 2 * BLOCK
    rows = 2 * STATIONS
    return pl.pallas_call(
        functools.partial(tiles_kernel, len(parts)),
        out_shape=jax.ShapeDtypeStruct((OUT_DEV, pairs, 2, side, side), BF16),
        grid=(OUT_DEV,),
        in_specs=[
            pl.BlockSpec((1, rows, 2 * WIDTH), lambda o: (o, 0, 0)),
            pl.BlockSpec((1, 8, LANES), lambda o: (o, 0, 0)),
        ]
        + [pl.BlockSpec(pick.shape, lambda o: (0, 0)) for pick in picks]
        + [pl.BlockSpec((2,) + part.shape[1:], lambda o: (o, 0, 0)) for part in parts],
        out_specs=pl.BlockSpec((1, pairs, 2, side, side), lambda o: (o, 0, 0, 0, 0)),
        scratch_shapes=[
            pltpu.VMEM((2 * rows, 2 * WIDTH), BF16),
            pltpu.VMEM((rows, 2 * WIDTH), BF16),
        ],
        compiler_params=pltpu.CompilerParams(vmem_limit_bytes=40 * 2**20),
        cost_estimate=pl.CostEstimate(flops=4_500_000_000, bytes_accessed=9_000_000, transcendentals=0),
        name="tiles",
    )(early, power, *picks, *parts)


def body(voltages, taps, station_gain, station_order):
    devices = lax.axis_size("ingest")
    streams = 2 * voltages.shape[0]
    blocks = NCHAN // LANES
    outs = 2 * OUT_DEV * devices
    consts = tables(OUT_DEV * devices)
    samples = voltages.reshape(streams, 2, FRAMES * blocks, LANES).transpose(0, 2, 1, 3)
    samples = samples.reshape(streams, FRAMES, 2 * blocks, LANES)
    coeffs = taps.reshape(TAPS, blocks, LANES).transpose(1, 0, 2).reshape(TAPS * blocks, LANES)
    cut = streams - streams // (2 * ROWS) * ROWS
    wanted = (2 * station_order[:, None] + jnp.arange(2, dtype=jnp.int32)).reshape(-1, 1)

    def pick(start, stop, first):
        place = np.arange(devices * (stop - start), dtype=np.int32)
        source = jnp.bitwise_xor(place // (stop - start), first) * streams + start + place % (stop - start)
        return (wanted == source).astype(BF16)

    packed = spectra(samples, coeffs, station_gain, consts, outs, 0, cut)[0]
    packed = packed.reshape(devices, 2 * OUT_DEV, cut, WIDTH)
    packed, station_gain = lax.optimization_barrier((packed, station_gain))
    early = lax.all_to_all(packed, "ingest", split_axis=0, concat_axis=0, tiled=True)
    picks, late = [], []
    if cut < streams:
        sent = spectra(samples, coeffs, station_gain, consts, outs, cut, streams, devices)
        received = {0: sent[0]}
        for k in range(1, devices):
            ready = sent[k]
            if k > WINDOW:
                ready, received[k - WINDOW] = lax.optimization_barrier((ready, received[k - WINDOW]))
            received[k] = lax.ppermute(ready, "ingest", [(i, i ^ k) for i in range(devices)])
        late = [received[k] for k in range(devices)]
        picks = [pick(cut, streams, lax.axis_index("ingest"))]
    rows, power = arrange(pick(0, cut, 0), early)
    return tiles(rows, power, picks, late)


def solution(mesh):
    return jax.shard_map(
        body,
        mesh=mesh,
        in_specs=(P(("band", "ingest"), None, None, None), P(), P("ingest"), P()),
        out_specs=P(("band", "ingest"), None, None, None, None),
        check_vma=False,
    )
```

```python
import functools
import math

import jax
import jax.numpy as jnp
import ml_dtypes
import numpy as np
from jax import lax
from jax.experimental import pallas as pl
from jax.experimental.pallas import tpu as pltpu
from jax.sharding import PartitionSpec as P

STATIONS = 512
NCHAN = 4096
BLOCK = 64
TAPS = 4
SPECTRA = 8
FRAMES = SPECTRA + TAPS - 1
AVG = 32
OUT_DEV = 2
LANES = 128
WIDE = 2 * AVG
WIDTH = SPECTRA * AVG
GROUP = 2
STEP = 8
ROWS = 16
WINDOW = 5
VMEM_LIMIT = 60_000_000
BF16 = jnp.bfloat16
F32 = jnp.float32
NT = (((1,), (1,)), ((), ()))


def split(values):
    high = values.astype(ml_dtypes.bfloat16)
    low = (values - high.astype(np.float64)).astype(ml_dtypes.bfloat16)
    return high, low


def tables(all_out):
    blocks = NCHAN // LANES
    angle = 2.0 * math.pi * (np.outer(np.arange(AVG), np.arange(blocks)) % blocks) / blocks
    cos, sin = np.cos(angle), np.sin(angle)
    stage = np.zeros((2, AVG, blocks, 2))
    stage[0, :, :, 0], stage[0, :, :, 1] = cos, sin
    stage[1, :, :, 0], stage[1, :, :, 1] = -sin, cos
    stage = np.stack(split(stage), axis=1).reshape(4 * AVG, 2 * blocks)
    stage = np.concatenate([np.kron(np.eye(GROUP), stage.astype(np.float32))] * 2, axis=1).astype(ml_dtypes.bfloat16)
    angle = 2.0 * math.pi * np.outer(np.arange(AVG), np.arange(LANES)) / NCHAN
    turn = np.stack([np.cos(angle), -np.sin(angle)]).astype(np.float32)
    first = (NCHAN - all_out * AVG) // 2
    bins = first // AVG + np.arange(all_out)
    angle = 2.0 * math.pi * (np.outer(np.arange(LANES), bins) % LANES) / LANES
    cos, sin = np.cos(angle), np.sin(angle)
    last = np.zeros((2, LANES, all_out, 2))
    last[0, :, :, 0], last[0, :, :, 1] = cos, -sin
    last[1, :, :, 0], last[1, :, :, 1] = sin, cos
    beside = max(1, LANES // (2 * all_out))
    last = np.kron(np.eye(beside), last.reshape(2 * LANES, 2 * all_out))
    last = np.concatenate(split(last), axis=1)
    return stage.astype(np.float32), turn, np.concatenate([last, last]).astype(np.float32)


def halves(values):
    scaled = values * 65537.0
    high = scaled - (scaled - values)
    return high, values - high


def spectra_kernel(first_stream, partners, outs, gain_ref, *refs):
    frames, refs = refs[:FRAMES], refs[FRAMES:]
    (taps_ref, stage_ref, turn_ref, last_ref), refs = refs[:4], refs[4:]
    out_refs, refs = refs[: max(partners, 1)], refs[max(partners, 1) :]
    (coeff_ref, held_ref), refs = refs[:2], refs[2:]
    groups = STEP // GROUP
    halves_refs, turned_refs = refs[:groups], refs[groups:]
    outer, inner = pl.program_id(0), pl.program_id(1)
    size = GROUP * WIDE
    beside = last_ref.shape[0] // (4 * LANES)
    columns = beside * outs

    @pl.when((outer == 0) & (inner == 0))
    def _():
        for j in range(TAPS):
            rows = taps_ref[pl.ds(j, AVG, stride=TAPS), :]
            for ri in range(2):
                coeff_ref[j, pl.ds(ri, AVG, stride=2), :] = rows

    def filter_rows(g, u, r):
        rows = slice(r, r + 16)
        coeffs = [coeff_ref[j, rows, :] for j in range(TAPS)]
        samples = [ref[g * GROUP + u, 0, rows, :].astype(F32) for ref in frames]
        for m in range(SPECTRA):
            value = coeffs[0] * samples[m]
            for j in range(1, TAPS):
                value = value + coeffs[j] * samples[m + j]
            for part, kept in enumerate(halves(value)):
                row = part * size + u * WIDE + r
                halves_refs[g][row : row + 16, m * LANES : (m + 1) * LANES] = kept

    def first_product(g, start):
        lanes = slice(start * LANES, (start + 2) * LANES)
        return jnp.dot(stage_ref[...], halves_refs[g][:, lanes], preferred_element_type=F32)

    def first_rest(g, start, section):
        turn_real, turn_imag = turn_ref[0], turn_ref[1]
        for u in range(GROUP):
            pair, place = divmod(u, beside)
            for m in range(start, start + 2):
                at = slice((m - start) * LANES, (m - start + 1) * LANES)
                blocks = [section[(4 * u + i) * AVG : (4 * u + i + 1) * AVG, at] for i in range(4)]
                real, imag = blocks[0] + blocks[1], blocks[2] + blocks[3]
                row = pair * WIDTH + m * AVG
                for ri, value in enumerate((real * turn_real - imag * turn_imag, real * turn_imag + imag * turn_real)):
                    for part, kept in enumerate(halves(value)):
                        lane = ((part * beside + place) * 2 + ri) * LANES
                        turned_refs[g][row : row + AVG, lane : lane + LANES] = kept

    def last_product(g, pair):
        rows = slice(pair * WIDTH, (pair + 1) * WIDTH)
        return jnp.dot(turned_refs[g][rows, :], last_ref[...], preferred_element_type=F32)

    def last_rest(g, pair, product):
        found = (product[:, :columns] + product[:, columns:]).T
        for place in range(beside):
            stream = g * GROUP + pair * beside + place
            factor = gain_ref[(first_stream + outer * ROWS + inner * STEP + stream) // 2]
            factor = factor * (1.0 / (64.0 * math.sqrt(NCHAN)))
            at = pl.multiple_of((inner * STEP + stream) * outs, outs)
            mine = found[place * outs : (place + 1) * outs] * factor
            for half in range(WIDTH // LANES):
                held_ref[half, pl.ds(at, outs), :] = mine[:, half * LANES : (half + 1) * LANES]

    waiting = []
    for g in range(groups + 3):
        filters = [(g, u, r) for u in range(GROUP) for r in range(0, WIDE, 16)] if g < groups else []
        units = [(first_product, first_rest, g - 1, start) for start in range(0, SPECTRA, 2)] if 1 <= g <= groups else []
        if 3 <= g:
            units += [(last_product, last_rest, g - 3, pair) for pair in range(GROUP // beside)]
        while filters or units:
            if units:
                product, rest, *job = units.pop(0)
                waiting.append((rest, job, product(*job)))
            for job in filters[:2]:
                filter_rows(*job)
            del filters[:2]
            if len(waiting) > 1 or not units:
                for rest, job, result in waiting[:1]:
                    rest(*job, result)
                del waiting[:1]
    for rest, job, result in waiting:
        rest(*job, result)

    @pl.when(inner == ROWS // STEP - 1)
    def _():
        me = lax.axis_index("ingest") if partners else 0
        each = outs // len(out_refs)
        for k, out_ref in enumerate(out_refs):
            target = jnp.bitwise_xor(me, k) * each if partners else 0
            for q in range(each):
                for half in range(WIDTH // LANES):
                    rows = held_ref[half, pl.ds(target + q, ROWS, stride=outs), :]
                    out_ref[q, :, half * LANES : (half + 1) * LANES] = rows.astype(BF16)


def spectra(voltages, taps, station_gain, consts, outs, start, stop, partners=0):
    stage, turn, last = consts
    groups = STEP // GROUP
    inner = ROWS // STEP
    pieces = max(partners, 1)
    frame_spec = [
        pl.BlockSpec((STEP, 1, WIDE, LANES), functools.partial(lambda j, a, b: (start // STEP + a * inner + b, j, 0, 0), j))
        for j in range(FRAMES)
    ]
    whole = lambda shape: pl.BlockSpec(shape, lambda a, b: (0,) * len(shape))
    return pl.pallas_call(
        functools.partial(spectra_kernel, start, partners, outs),
        out_shape=[jax.ShapeDtypeStruct((outs // pieces, stop - start, WIDTH), BF16)] * pieces,
        grid=((stop - start) // ROWS, inner),
        in_specs=[pl.BlockSpec(memory_space=pltpu.SMEM)]
        + frame_spec
        + [whole(taps.shape), whole(stage.shape), whole(turn.shape), whole(last.shape)],
        out_specs=[pl.BlockSpec((outs // pieces, ROWS, WIDTH), lambda a, b: (0, a, 0))] * pieces,
        scratch_shapes=[
            pltpu.VMEM((TAPS, WIDE, LANES), F32),
            pltpu.VMEM((WIDTH // LANES, ROWS * outs, LANES), F32),
        ]
        + [pltpu.VMEM((2 * GROUP * WIDE, SPECTRA * LANES), F32)] * groups
        + [pltpu.VMEM((4 * GROUP * WIDTH * LANES // last.shape[0], last.shape[0]), F32)] * groups,
        compiler_params=pltpu.CompilerParams(vmem_limit_bytes=VMEM_LIMIT),
        cost_estimate=pl.CostEstimate(
            flops=(stop - start) * SPECTRA * 12_000_000,
            bytes_accessed=(stop - start) * FRAMES * WIDE * LANES * 4,
            transcendentals=0,
        ),
        name="spectra",
    )(station_gain, *([voltages] * FRAMES), taps, stage, turn, last)


def squares(values):
    values = values.astype(F32)
    values = jnp.sum((values * values).reshape(-1, 8, values.shape[-1]), axis=0)
    return sum(values[:, lane : lane + LANES] for lane in range(0, values.shape[-1], LANES))


def arrange_kernel(pick_ref, part_ref, out_ref, power_ref):
    rows = 2 * STATIONS
    data = jnp.concatenate([part_ref[:, ri].reshape(-1, WIDTH) for ri in range(2)], axis=1)
    power_ref[0] = squares(data)
    for r in range(0, rows, 2 * LANES):
        own = slice(r, r + 2 * LANES)
        out_ref[0, own, :] = jnp.dot(pick_ref[own, :], data, preferred_element_type=F32).astype(BF16)


def arrange(pick, part):
    devices, _, own, width = part.shape
    rows = 2 * STATIONS
    return pl.pallas_call(
        arrange_kernel,
        out_shape=(
            jax.ShapeDtypeStruct((OUT_DEV, rows, 2 * width), BF16),
            jax.ShapeDtypeStruct((OUT_DEV, 8, LANES), F32),
        ),
        grid=(OUT_DEV,),
        in_specs=[
            pl.BlockSpec(pick.shape, lambda o: (0, 0)),
            pl.BlockSpec((devices, 2, own, width), lambda o: (0, o, 0, 0)),
        ],
        out_specs=(
            pl.BlockSpec((1, rows, 2 * width), lambda o: (o, 0, 0)),
            pl.BlockSpec((1, 8, LANES), lambda o: (o, 0, 0)),
        ),
        compiler_params=pltpu.CompilerParams(vmem_limit_bytes=40 * 2**20),
        cost_estimate=pl.CostEstimate(flops=1_100_000_000, bytes_accessed=4_000_000, transcendentals=0),
        name="arrange",
    )(pick, part)


def tiles_kernel(late, early_ref, power_ref, *refs):
    (pick_refs, part_refs), refs = (refs[: min(late, 1)], refs[min(late, 1) :][:late]), refs[-3:]
    out_ref, left_ref, right_ref = refs
    rows = 2 * STATIONS
    side = 2 * BLOCK
    blocks = STATIONS // BLOCK
    total = power_ref[0]
    if late:
        data = [jnp.concatenate([part_ref[ri] for part_ref in part_refs], axis=0) for ri in range(2)]
        data = jnp.concatenate(data, axis=1)
        total = total + squares(data)
    power = jnp.sum(total) / (STATIONS * 2 * SPECTRA * AVG)
    scale = 1.0 / jnp.full((1, LANES), SPECTRA * AVG * power, F32)
    for r in range(0, rows, 2 * side):
        own = slice(r, r + 2 * side)
        found = early_ref[0, own, :]
        if late:
            found = (jnp.dot(pick_refs[0][own, :], data, preferred_element_type=F32) + found.astype(F32)).astype(BF16)
        right_ref[own, :] = found
        for p in range(2):
            mine = found[p * side : (p + 1) * side]
            at = 2 * r + p * 2 * side
            left_ref[at : at + side, :] = mine
            left_ref[at + side : at + 2 * side, :WIDTH] = mine[:, WIDTH:]
            left_ref[at + side : at + 2 * side, WIDTH:] = -mine[:, :WIDTH]
    for c in range(0, blocks, 2):
        right = right_ref[c * side : (c + 2) * side, :]
        for b in range(c, blocks):
            left = left_ref[b * 2 * side : (b + 1) * 2 * side, :]
            product = lax.dot_general(left, right, NT, preferred_element_type=F32)
            for p in range(2):
                if c + p <= b:
                    tile = b * (b + 1) // 2 + c + p
                    scaled = (product[:, p * side : (p + 1) * side] * scale).astype(BF16)
                    out_ref[0, tile, 0] = scaled[:side]
                    out_ref[0, tile, 1] = scaled[side:]


def tiles(early, power, picks, parts):
    blocks = STATIONS // BLOCK
    pairs = blocks * (blocks + 1) // 2
    side = 2 * BLOCK
    rows = 2 * STATIONS
    return pl.pallas_call(
        functools.partial(tiles_kernel, len(parts)),
        out_shape=jax.ShapeDtypeStruct((OUT_DEV, pairs, 2, side, side), BF16),
        grid=(OUT_DEV,),
        in_specs=[
            pl.BlockSpec((1, rows, 2 * WIDTH), lambda o: (o, 0, 0)),
            pl.BlockSpec((1, 8, LANES), lambda o: (o, 0, 0)),
        ]
        + [pl.BlockSpec(pick.shape, lambda o: (0, 0)) for pick in picks]
        + [pl.BlockSpec((2,) + part.shape[1:], lambda o: (o, 0, 0)) for part in parts],
        out_specs=pl.BlockSpec((1, pairs, 2, side, side), lambda o: (o, 0, 0, 0, 0)),
        scratch_shapes=[
            pltpu.VMEM((2 * rows, 2 * WIDTH), BF16),
            pltpu.VMEM((rows, 2 * WIDTH), BF16),
        ],
        compiler_params=pltpu.CompilerParams(vmem_limit_bytes=40 * 2**20),
        cost_estimate=pl.CostEstimate(flops=4_500_000_000, bytes_accessed=9_000_000, transcendentals=0),
        name="tiles",
    )(early, power, *picks, *parts)


def sending_order(devices):
    far, near = list(range(devices // 2, devices)), list(range(1, devices // 2))
    order = []
    while far or near:
        order += far[:1] + near[:1]
        far, near = far[1:], near[1:]
    return order


def body(voltages, taps, station_gain, station_order):
    devices = lax.axis_size("ingest")
    streams = 2 * voltages.shape[0]
    blocks = NCHAN // LANES
    outs = 2 * OUT_DEV * devices
    consts = tables(OUT_DEV * devices)
    samples = voltages.reshape(streams, 2, FRAMES * blocks, LANES).transpose(0, 2, 1, 3)
    samples = samples.reshape(streams, FRAMES, 2 * blocks, LANES)
    coeffs = taps.reshape(TAPS, blocks, LANES).transpose(1, 0, 2).reshape(TAPS * blocks, LANES)
    cut = min(streams, ROWS)
    wanted = (2 * station_order[:, None] + jnp.arange(2, dtype=jnp.int32)).reshape(-1, 1)

    def pick(start, stop, first):
        place = np.arange(devices * (stop - start), dtype=np.int32)
        source = jnp.bitwise_xor(place // (stop - start), first) * streams + start + place % (stop - start)
        return (wanted == source).astype(BF16)

    packed = spectra(samples, coeffs, station_gain, consts, outs, 0, cut)[0]
    packed = packed.reshape(devices, 2 * OUT_DEV, cut, WIDTH)
    packed, station_gain = lax.optimization_barrier((packed, station_gain))
    early = lax.all_to_all(packed, "ingest", split_axis=0, concat_axis=0, tiled=True)
    picks, late = [], []
    if cut < streams:
        sent = spectra(samples, coeffs, station_gain, consts, outs, cut, streams, devices)
        received = {0: sent[0]}
        order = sending_order(devices)
        for place, k in enumerate(order):
            ready = sent[k]
            if place >= WINDOW:
                past = order[place - WINDOW]
                ready, received[past] = lax.optimization_barrier((ready, received[past]))
            received[k] = lax.ppermute(ready, "ingest", [(i, i ^ k) for i in range(devices)])
        late = [received[k] for k in range(devices)]
        picks = [pick(cut, streams, lax.axis_index("ingest"))]
    rows, power = arrange(pick(0, cut, 0), early)
    return tiles(rows, power, picks, late)


def solution(mesh):
    return jax.shard_map(
        body,
        mesh=mesh,
        in_specs=(P(("band", "ingest"), None, None, None), P(), P("ingest"), P()),
        out_specs=P(("band", "ingest"), None, None, None, None),
        check_vma=False,
    )
```

```python
import functools
import math

import jax
import jax.numpy as jnp
import ml_dtypes
import numpy as np
from jax import lax
from jax.experimental import pallas as pl
from jax.experimental.pallas import tpu as pltpu
from jax.sharding import PartitionSpec as P

STATIONS = 512
NCHAN = 4096
BLOCK = 64
TAPS = 4
SPECTRA = 8
FRAMES = SPECTRA + TAPS - 1
AVG = 32
OUT_DEV = 2
LANES = 128
WIDE = 2 * AVG
WIDTH = SPECTRA * AVG
GROUP = 2
STEP = 8
ROWS = 16
WINDOW = 5
VMEM_LIMIT = 60_000_000
BF16 = jnp.bfloat16
F32 = jnp.float32
NT = (((1,), (1,)), ((), ()))


def split(values):
    high = values.astype(ml_dtypes.bfloat16)
    low = (values - high.astype(np.float64)).astype(ml_dtypes.bfloat16)
    return high, low


def tables(all_out):
    blocks = NCHAN // LANES
    angle = 2.0 * math.pi * (np.outer(np.arange(AVG), np.arange(blocks)) % blocks) / blocks
    cos, sin = np.cos(angle), np.sin(angle)
    stage = np.zeros((2, AVG, blocks, 2))
    stage[0, :, :, 0], stage[0, :, :, 1] = cos, sin
    stage[1, :, :, 0], stage[1, :, :, 1] = -sin, cos
    stage = np.stack(split(stage), axis=1).reshape(4 * AVG, 2 * blocks)
    stage = np.kron(np.eye(GROUP), stage.astype(np.float32))
    angle = 2.0 * math.pi * np.outer(np.arange(AVG), np.arange(LANES)) / NCHAN
    turn = np.stack([np.cos(angle), -np.sin(angle)]).astype(np.float32)
    first = (NCHAN - all_out * AVG) // 2
    bins = first // AVG + np.arange(all_out)
    angle = 2.0 * math.pi * (np.outer(np.arange(LANES), bins) % LANES) / LANES
    cos, sin = np.cos(angle), np.sin(angle)
    last = np.zeros((2, LANES, all_out, 2))
    last[0, :, :, 0], last[0, :, :, 1] = cos, -sin
    last[1, :, :, 0], last[1, :, :, 1] = sin, cos
    beside = max(1, LANES // (2 * all_out))
    last = np.kron(np.eye(beside), last.reshape(2 * LANES, 2 * all_out))
    last = np.concatenate(split(last), axis=1)
    return stage.astype(np.float32), turn, last.astype(np.float32)


def halves(values):
    scaled = values * 65537.0
    high = scaled - (scaled - values)
    return high, values - high


def spectra_kernel(first_stream, partners, outs, gain_ref, *refs):
    frames, refs = refs[:FRAMES], refs[FRAMES:]
    (taps_ref, stage_ref, turn_ref, last_ref), refs = refs[:4], refs[4:]
    out_refs, refs = refs[: max(partners, 1)], refs[max(partners, 1) :]
    (coeff_ref, held_ref), refs = refs[:2], refs[2:]
    groups = STEP // GROUP
    halves_refs, turned_refs = refs[:groups], refs[groups:]
    outer, inner = pl.program_id(0), pl.program_id(1)
    size = GROUP * WIDE
    beside = last_ref.shape[0] // (2 * LANES)
    columns = beside * outs

    @pl.when((outer == 0) & (inner == 0))
    def _():
        for j in range(TAPS):
            rows = taps_ref[pl.ds(j, AVG, stride=TAPS), :]
            for ri in range(2):
                coeff_ref[j, pl.ds(ri, AVG, stride=2), :] = rows

    def filter_rows(g, u, r):
        rows = slice(r, r + 16)
        coeffs = [coeff_ref[j, rows, :] for j in range(TAPS)]
        samples = [ref[g * GROUP + u, 0, rows, :].astype(F32) for ref in frames]
        for m in range(SPECTRA):
            value = coeffs[0] * samples[m]
            for j in range(1, TAPS):
                value = value + coeffs[j] * samples[m + j]
            for part, kept in enumerate(halves(value)):
                row = part * size + u * WIDE + r
                halves_refs[g][row : row + 16, m * LANES : (m + 1) * LANES] = kept

    def first_product(g, start):
        lanes = slice(start * LANES, (start + 2) * LANES)
        table = stage_ref[...]
        return jnp.dot(jnp.concatenate([table, table], axis=1), halves_refs[g][:, lanes], preferred_element_type=F32)

    def first_rest(g, start, section):
        turn_real, turn_imag = turn_ref[0], turn_ref[1]
        for u in range(GROUP):
            pair, place = divmod(u, beside)
            for m in range(start, start + 2):
                at = slice((m - start) * LANES, (m - start + 1) * LANES)
                blocks = [section[(4 * u + i) * AVG : (4 * u + i + 1) * AVG, at] for i in range(4)]
                real, imag = blocks[0] + blocks[1], blocks[2] + blocks[3]
                row = pair * WIDTH + m * AVG
                for ri, value in enumerate((real * turn_real - imag * turn_imag, real * turn_imag + imag * turn_real)):
                    for part, kept in enumerate(halves(value)):
                        lane = ((part * beside + place) * 2 + ri) * LANES
                        turned_refs[g][row : row + AVG, lane : lane + LANES] = kept

    def last_product(g, pair):
        rows = slice(pair * WIDTH, (pair + 1) * WIDTH)
        table = last_ref[...]
        return jnp.dot(turned_refs[g][rows, :], jnp.concatenate([table, table]), preferred_element_type=F32)

    def last_rest(g, pair, product):
        found = (product[:, :columns] + product[:, columns:]).T
        for place in range(beside):
            stream = g * GROUP + pair * beside + place
            factor = gain_ref[(first_stream + outer * ROWS + inner * STEP + stream) // 2]
            factor = factor * (1.0 / (64.0 * math.sqrt(NCHAN)))
            at = pl.multiple_of((inner * STEP + stream) * outs, outs)
            mine = found[place * outs : (place + 1) * outs] * factor
            for half in range(WIDTH // LANES):
                held_ref[half, pl.ds(at, outs), :] = mine[:, half * LANES : (half + 1) * LANES]

    waiting = []
    for g in range(groups + 3):
        filters = [(g, u, r) for u in range(GROUP) for r in range(0, WIDE, 16)] if g < groups else []
        units = [(first_product, first_rest, g - 1, start) for start in range(0, SPECTRA, 2)] if 1 <= g <= groups else []
        if 3 <= g:
            units += [(last_product, last_rest, g - 3, pair) for pair in range(GROUP // beside)]
        while filters or units:
            if units:
                product, rest, *job = units.pop(0)
                waiting.append((rest, job, product(*job)))
            for job in filters[:2]:
                filter_rows(*job)
            del filters[:2]
            if len(waiting) > 1 or not units:
                for rest, job, result in waiting[:1]:
                    rest(*job, result)
                del waiting[:1]
    for rest, job, result in waiting:
        rest(*job, result)

    @pl.when(inner == ROWS // STEP - 1)
    def _():
        me = lax.axis_index("ingest") if partners else 0
        each = outs // len(out_refs)
        for k, out_ref in enumerate(out_refs):
            target = jnp.bitwise_xor(me, k) * each if partners else 0
            for q in range(each):
                for half in range(WIDTH // LANES):
                    rows = held_ref[half, pl.ds(target + q, ROWS, stride=outs), :]
                    out_ref[q, :, half * LANES : (half + 1) * LANES] = rows.astype(BF16)


def spectra(voltages, taps, station_gain, consts, outs, start, stop, partners=0):
    stage, turn, last = consts
    groups = STEP // GROUP
    inner = ROWS // STEP
    pieces = max(partners, 1)
    frame_spec = [
        pl.BlockSpec((STEP, 1, WIDE, LANES), functools.partial(lambda j, a, b: (start // STEP + a * inner + b, j, 0, 0), j))
        for j in range(FRAMES)
    ]
    whole = lambda shape: pl.BlockSpec(shape, lambda a, b: (0,) * len(shape))
    return pl.pallas_call(
        functools.partial(spectra_kernel, start, partners, outs),
        out_shape=[jax.ShapeDtypeStruct((outs // pieces, stop - start, WIDTH), BF16)] * pieces,
        grid=((stop - start) // ROWS, inner),
        in_specs=[pl.BlockSpec(memory_space=pltpu.SMEM)]
        + frame_spec
        + [whole(taps.shape), whole(stage.shape), whole(turn.shape), whole(last.shape)],
        out_specs=[pl.BlockSpec((outs // pieces, ROWS, WIDTH), lambda a, b: (0, a, 0))] * pieces,
        scratch_shapes=[
            pltpu.VMEM((TAPS, WIDE, LANES), F32),
            pltpu.VMEM((WIDTH // LANES, ROWS * outs, LANES), F32),
        ]
        + [pltpu.VMEM((2 * GROUP * WIDE, SPECTRA * LANES), F32)] * groups
        + [pltpu.VMEM((2 * GROUP * WIDTH * LANES // last.shape[0], 2 * last.shape[0]), F32)] * groups,
        compiler_params=pltpu.CompilerParams(vmem_limit_bytes=VMEM_LIMIT),
        cost_estimate=pl.CostEstimate(
            flops=(stop - start) * SPECTRA * 12_000_000,
            bytes_accessed=(stop - start) * FRAMES * WIDE * LANES * 4,
            transcendentals=0,
        ),
        name="spectra",
    )(station_gain, *([voltages] * FRAMES), taps, stage, turn, last)


def squares(values):
    values = values.astype(F32)
    values = jnp.sum((values * values).reshape(-1, 8, values.shape[-1]), axis=0)
    return sum(values[:, lane : lane + LANES] for lane in range(0, values.shape[-1], LANES))


def arrange_kernel(pick_ref, part_ref, out_ref, power_ref):
    rows = 2 * STATIONS
    data = jnp.concatenate([part_ref[:, ri].reshape(-1, WIDTH) for ri in range(2)], axis=1)
    power_ref[0] = squares(data)
    for r in range(0, rows, 2 * LANES):
        own = slice(r, r + 2 * LANES)
        out_ref[0, own, :] = jnp.dot(pick_ref[own, :], data, preferred_element_type=F32).astype(BF16)


def arrange(pick, part):
    devices, _, own, width = part.shape
    rows = 2 * STATIONS
    return pl.pallas_call(
        arrange_kernel,
        out_shape=(
            jax.ShapeDtypeStruct((OUT_DEV, rows, 2 * width), BF16),
            jax.ShapeDtypeStruct((OUT_DEV, 8, LANES), F32),
        ),
        grid=(OUT_DEV,),
        in_specs=[
            pl.BlockSpec(pick.shape, lambda o: (0, 0)),
            pl.BlockSpec((devices, 2, own, width), lambda o: (0, o, 0, 0)),
        ],
        out_specs=(
            pl.BlockSpec((1, rows, 2 * width), lambda o: (o, 0, 0)),
            pl.BlockSpec((1, 8, LANES), lambda o: (o, 0, 0)),
        ),
        compiler_params=pltpu.CompilerParams(vmem_limit_bytes=40 * 2**20),
        cost_estimate=pl.CostEstimate(flops=1_100_000_000, bytes_accessed=4_000_000, transcendentals=0),
        name="arrange",
    )(pick, part)


def tiles_kernel(late, early_ref, power_ref, *refs):
    pick_refs, part_refs, refs = refs[: min(late, 1)], refs[min(late, 1) :][:late], refs[min(late, 1) + late :]
    out_ref, left_ref, right_ref, *refs = refs
    rows = 2 * STATIONS
    side = 2 * BLOCK
    blocks = STATIONS // BLOCK
    total = power_ref[0]
    if late:
        late_ref, sems = refs
        item = pl.program_id(0)

        def copy(o, k):
            return pltpu.make_async_copy(part_refs[k].at[pl.ds(2 * o, 2)], late_ref.at[o, k], sems.at[o, k])

        @pl.when(item == 0)
        def _():
            for o in range(OUT_DEV):
                for k in range(late):
                    copy(o, k).start()

        for o in range(OUT_DEV):

            @pl.when(item == o)
            def _():
                for k in range(late):
                    copy(o, k).wait()

        data = [late_ref[item, :, ri].reshape(-1, WIDTH) for ri in range(2)]
        data = jnp.concatenate(data, axis=1)
        total = total + squares(data)
    power = jnp.sum(total) / (STATIONS * 2 * SPECTRA * AVG)
    scale = 1.0 / jnp.full((1, LANES), SPECTRA * AVG * power, F32)
    for r in range(0, rows, 2 * side):
        own = slice(r, r + 2 * side)
        found = early_ref[0, own, :]
        if late:
            found = (jnp.dot(pick_refs[0][own, :], data, preferred_element_type=F32) + found.astype(F32)).astype(BF16)
        right_ref[own, :] = found
        for p in range(2):
            mine = found[p * side : (p + 1) * side]
            at = 2 * r + p * 2 * side
            left_ref[at : at + side, :] = mine
            left_ref[at + side : at + 2 * side, :WIDTH] = mine[:, WIDTH:]
            left_ref[at + side : at + 2 * side, WIDTH:] = -mine[:, :WIDTH]
    for c in range(0, blocks, 2):
        right = right_ref[c * side : (c + 2) * side, :]
        for b in range(c, blocks):
            left = left_ref[b * 2 * side : (b + 1) * 2 * side, :]
            product = lax.dot_general(left, right, NT, preferred_element_type=F32)
            for p in range(2):
                if c + p <= b:
                    tile = b * (b + 1) // 2 + c + p
                    scaled = (product[:, p * side : (p + 1) * side] * scale).astype(BF16)
                    out_ref[0, tile, 0] = scaled[:side]
                    out_ref[0, tile, 1] = scaled[side:]


def tiles(early, power, picks, parts):
    blocks = STATIONS // BLOCK
    pairs = blocks * (blocks + 1) // 2
    side = 2 * BLOCK
    rows = 2 * STATIONS
    return pl.pallas_call(
        functools.partial(tiles_kernel, len(parts)),
        out_shape=jax.ShapeDtypeStruct((OUT_DEV, pairs, 2, side, side), BF16),
        grid=(OUT_DEV,),
        in_specs=[
            pl.BlockSpec((1, rows, 2 * WIDTH), lambda o: (o, 0, 0)),
            pl.BlockSpec((1, 8, LANES), lambda o: (o, 0, 0)),
        ]
        + [pl.BlockSpec(pick.shape, lambda o: (0, 0)) for pick in picks]
        + [pl.BlockSpec(memory_space=pltpu.HBM)] * len(parts),
        out_specs=pl.BlockSpec((1, pairs, 2, side, side), lambda o: (o, 0, 0, 0, 0)),
        scratch_shapes=[
            pltpu.VMEM((2 * rows, 2 * WIDTH), BF16),
            pltpu.VMEM((rows, 2 * WIDTH), BF16),
        ]
        + [pltpu.VMEM((OUT_DEV, len(parts), 2) + part.shape[1:], BF16) for part in parts[:1]]
        + [pltpu.SemaphoreType.DMA((OUT_DEV, len(parts))) for _ in parts[:1]],
        compiler_params=pltpu.CompilerParams(vmem_limit_bytes=40 * 2**20),
        cost_estimate=pl.CostEstimate(flops=4_500_000_000, bytes_accessed=9_000_000, transcendentals=0),
        name="tiles",
    )(early, power, *picks, *parts)


def body(voltages, taps, station_gain, station_order):
    devices = lax.axis_size("ingest")
    streams = 2 * voltages.shape[0]
    blocks = NCHAN // LANES
    outs = 2 * OUT_DEV * devices
    consts = tables(OUT_DEV * devices)
    samples = voltages.reshape(streams, 2, FRAMES * blocks, LANES).transpose(0, 2, 1, 3)
    samples = samples.reshape(streams, FRAMES, 2 * blocks, LANES)
    coeffs = taps.reshape(TAPS, blocks, LANES).transpose(1, 0, 2).reshape(TAPS * blocks, LANES)
    cut = streams - streams // (2 * ROWS) * ROWS
    wanted = (2 * station_order[:, None] + jnp.arange(2, dtype=jnp.int32)).reshape(-1, 1)

    def pick(start, stop, first):
        place = np.arange(devices * (stop - start), dtype=np.int32)
        source = jnp.bitwise_xor(place // (stop - start), first) * streams + start + place % (stop - start)
        return (wanted == source).astype(BF16)

    packed = spectra(samples, coeffs, station_gain, consts, outs, 0, cut)[0]
    packed = packed.reshape(devices, 2 * OUT_DEV, cut, WIDTH)
    packed, station_gain = lax.optimization_barrier((packed, station_gain))
    early = lax.all_to_all(packed, "ingest", split_axis=0, concat_axis=0, tiled=True)
    picks, late = [], []
    if cut < streams:
        sent = spectra(samples, coeffs, station_gain, consts, outs, cut, streams, devices)
        received = {0: sent[0]}
        for k in range(1, devices):
            ready = sent[k]
            if k > WINDOW:
                ready, received[k - WINDOW] = lax.optimization_barrier((ready, received[k - WINDOW]))
            received[k] = lax.ppermute(ready, "ingest", [(i, i ^ k) for i in range(devices)])
        late = [received[k] for k in range(devices)]
        picks = [pick(cut, streams, lax.axis_index("ingest"))]
    rows, power = arrange(pick(0, cut, 0), early)
    return tiles(rows, power, picks, late)


def solution(mesh):
    return jax.shard_map(
        body,
        mesh=mesh,
        in_specs=(P(("band", "ingest"), None, None, None), P(), P("ingest"), P()),
        out_specs=P(("band", "ingest"), None, None, None, None),
        check_vma=False,
    )
```

```python
import functools
import math

import jax
import jax.numpy as jnp
import ml_dtypes
import numpy as np
from jax import lax
from jax.experimental import pallas as pl
from jax.experimental.pallas import tpu as pltpu
from jax.sharding import PartitionSpec as P

STATIONS = 512
NCHAN = 4096
BLOCK = 64
TAPS = 4
SPECTRA = 8
FRAMES = SPECTRA + TAPS - 1
AVG = 32
OUT_DEV = 2
LANES = 128
WIDE = 2 * AVG
WIDTH = SPECTRA * AVG
GROUP = 2
STEP = 8
ROWS = 16
WINDOW = 5
VMEM_LIMIT = 60_000_000
BF16 = jnp.bfloat16
F32 = jnp.float32
NT = (((1,), (1,)), ((), ()))


def split(values):
    high = values.astype(ml_dtypes.bfloat16)
    low = (values - high.astype(np.float64)).astype(ml_dtypes.bfloat16)
    return high, low


def tables(all_out):
    blocks = NCHAN // LANES
    angle = 2.0 * math.pi * (np.outer(np.arange(AVG), np.arange(blocks)) % blocks) / blocks
    cos, sin = np.cos(angle), np.sin(angle)
    stage = np.zeros((2, AVG, blocks, 2))
    stage[0, :, :, 0], stage[0, :, :, 1] = cos, sin
    stage[1, :, :, 0], stage[1, :, :, 1] = -sin, cos
    stage = np.concatenate(split(np.kron(np.eye(GROUP), stage.reshape(2 * AVG, 2 * blocks))))
    angle = 2.0 * math.pi * np.outer(np.arange(AVG), np.arange(LANES)) / NCHAN
    turn = np.stack([np.cos(angle), -np.sin(angle)]).astype(np.float32)
    first = (NCHAN - all_out * AVG) // 2
    bins = first // AVG + np.arange(all_out)
    angle = 2.0 * math.pi * (np.outer(np.arange(LANES), bins) % LANES) / LANES
    cos, sin = np.cos(angle), np.sin(angle)
    last = np.zeros((2, LANES, all_out, 2))
    last[0, :, :, 0], last[0, :, :, 1] = cos, -sin
    last[1, :, :, 0], last[1, :, :, 1] = sin, cos
    beside = max(1, LANES // (2 * all_out))
    last = np.kron(np.eye(beside), last.reshape(2 * LANES, 2 * all_out))
    last = np.concatenate(split(last), axis=1)
    return stage.astype(np.float32), turn, last.astype(np.float32)


def halves(values):
    scaled = values * 65537.0
    high = scaled - (scaled - values)
    return high, values - high


def spectra_kernel(first_stream, partners, outs, gain_ref, *refs):
    frames, refs = refs[:FRAMES], refs[FRAMES:]
    (taps_ref, stage_ref, turn_ref, last_ref), refs = refs[:4], refs[4:]
    out_refs, refs = refs[: max(partners, 1)], refs[max(partners, 1) :]
    (coeff_ref, held_ref), refs = refs[:2], refs[2:]
    groups = STEP // GROUP
    halves_refs, turned_refs = refs[:groups], refs[groups:]
    outer, inner = pl.program_id(0), pl.program_id(1)
    size = GROUP * WIDE
    beside = last_ref.shape[0] // (2 * LANES)
    columns = beside * outs

    @pl.when((outer == 0) & (inner == 0))
    def _():
        for j in range(TAPS):
            rows = taps_ref[pl.ds(j, AVG, stride=TAPS), :]
            for ri in range(2):
                coeff_ref[j, pl.ds(ri, AVG, stride=2), :] = rows

    def filter_rows(g, u, r):
        rows = slice(r, r + 16)
        coeffs = [coeff_ref[j, rows, :] for j in range(TAPS)]
        samples = [ref[g * GROUP + u, 0, rows, :].astype(F32) for ref in frames]
        for m in range(SPECTRA):
            value = coeffs[0] * samples[m]
            for j in range(1, TAPS):
                value = value + coeffs[j] * samples[m + j]
            for part, kept in enumerate(halves(value)):
                row = part * size + u * WIDE + r
                halves_refs[g][row : row + 16, m * LANES : (m + 1) * LANES] = kept

    def first_product(g, start):
        lanes = slice(start * LANES, (start + 2) * LANES)
        high, low = stage_ref[:size, :], stage_ref[size:, :]
        data = jnp.concatenate([halves_refs[g][:, lanes], halves_refs[g][:size, lanes]])
        return jnp.dot(jnp.concatenate([high, high, low], axis=1), data, preferred_element_type=F32)

    def first_rest(g, start, section):
        turn_real, turn_imag = turn_ref[0], turn_ref[1]
        for u in range(GROUP):
            pair, place = divmod(u, beside)
            for m in range(start, start + 2):
                at = slice((m - start) * LANES, (m - start + 1) * LANES)
                real, imag = [section[(2 * u + i) * AVG : (2 * u + i + 1) * AVG, at] for i in range(2)]
                row = pair * WIDTH + m * AVG
                for ri, value in enumerate((real * turn_real - imag * turn_imag, real * turn_imag + imag * turn_real)):
                    for part, kept in enumerate(halves(value)):
                        lane = ((part * beside + place) * 2 + ri) * LANES
                        turned_refs[g][row : row + AVG, lane : lane + LANES] = kept

    def last_product(g, pair):
        rows = slice(pair * WIDTH, (pair + 1) * WIDTH)
        table = last_ref[...]
        return jnp.dot(turned_refs[g][rows, :], jnp.concatenate([table, table]), preferred_element_type=F32)

    def last_rest(g, pair, product):
        found = (product[:, :columns] + product[:, columns:]).T
        for place in range(beside):
            stream = g * GROUP + pair * beside + place
            factor = gain_ref[(first_stream + outer * ROWS + inner * STEP + stream) // 2]
            factor = factor * (1.0 / (64.0 * math.sqrt(NCHAN)))
            at = pl.multiple_of((inner * STEP + stream) * outs, outs)
            mine = found[place * outs : (place + 1) * outs] * factor
            for half in range(WIDTH // LANES):
                held_ref[half, pl.ds(at, outs), :] = mine[:, half * LANES : (half + 1) * LANES]

    waiting = []
    for g in range(groups + 3):
        filters = [(g, u, r) for u in range(GROUP) for r in range(0, WIDE, 16)] if g < groups else []
        units = [(first_product, first_rest, g - 1, start) for start in range(0, SPECTRA, 2)] if 1 <= g <= groups else []
        if 3 <= g:
            units += [(last_product, last_rest, g - 3, pair) for pair in range(GROUP // beside)]
        while filters or units:
            if units:
                product, rest, *job = units.pop(0)
                waiting.append((rest, job, product(*job)))
            for job in filters[:2]:
                filter_rows(*job)
            del filters[:2]
            if len(waiting) > 1 or not units:
                for rest, job, result in waiting[:1]:
                    rest(*job, result)
                del waiting[:1]
    for rest, job, result in waiting:
        rest(*job, result)

    @pl.when(inner == ROWS // STEP - 1)
    def _():
        me = lax.axis_index("ingest") if partners else 0
        each = outs // len(out_refs)
        for k, out_ref in enumerate(out_refs):
            target = jnp.bitwise_xor(me, k) * each if partners else 0
            for q in range(each):
                for half in range(WIDTH // LANES):
                    rows = held_ref[half, pl.ds(target + q, ROWS, stride=outs), :]
                    out_ref[q, :, half * LANES : (half + 1) * LANES] = rows.astype(BF16)


def spectra(voltages, taps, station_gain, consts, outs, start, stop, partners=0):
    stage, turn, last = consts
    groups = STEP // GROUP
    inner = ROWS // STEP
    pieces = max(partners, 1)
    frame_spec = [
        pl.BlockSpec((STEP, 1, WIDE, LANES), functools.partial(lambda j, a, b: (start // STEP + a * inner + b, j, 0, 0), j))
        for j in range(FRAMES)
    ]
    whole = lambda shape: pl.BlockSpec(shape, lambda a, b: (0,) * len(shape))
    return pl.pallas_call(
        functools.partial(spectra_kernel, start, partners, outs),
        out_shape=[jax.ShapeDtypeStruct((outs // pieces, stop - start, WIDTH), BF16)] * pieces,
        grid=((stop - start) // ROWS, inner),
        in_specs=[pl.BlockSpec(memory_space=pltpu.SMEM)]
        + frame_spec
        + [whole(taps.shape), whole(stage.shape), whole(turn.shape), whole(last.shape)],
        out_specs=[pl.BlockSpec((outs // pieces, ROWS, WIDTH), lambda a, b: (0, a, 0))] * pieces,
        scratch_shapes=[
            pltpu.VMEM((TAPS, WIDE, LANES), F32),
            pltpu.VMEM((WIDTH // LANES, ROWS * outs, LANES), F32),
        ]
        + [pltpu.VMEM((2 * GROUP * WIDE, SPECTRA * LANES), F32)] * groups
        + [pltpu.VMEM((2 * GROUP * WIDTH * LANES // last.shape[0], 2 * last.shape[0]), F32)] * groups,
        compiler_params=pltpu.CompilerParams(vmem_limit_bytes=VMEM_LIMIT),
        cost_estimate=pl.CostEstimate(
            flops=(stop - start) * SPECTRA * 12_000_000,
            bytes_accessed=(stop - start) * FRAMES * WIDE * LANES * 4,
            transcendentals=0,
        ),
        name="spectra",
    )(station_gain, *([voltages] * FRAMES), taps, stage, turn, last)


def squares(values):
    values = values.astype(F32)
    values = jnp.sum((values * values).reshape(-1, 8, values.shape[-1]), axis=0)
    return sum(values[:, lane : lane + LANES] for lane in range(0, values.shape[-1], LANES))


def arrange_kernel(pick_ref, part_ref, out_ref, power_ref):
    rows = 2 * STATIONS
    data = jnp.concatenate([part_ref[:, ri].reshape(-1, WIDTH) for ri in range(2)], axis=1)
    power_ref[0] = squares(data)
    for r in range(0, rows, 2 * LANES):
        own = slice(r, r + 2 * LANES)
        out_ref[0, own, :] = jnp.dot(pick_ref[own, :], data, preferred_element_type=F32).astype(BF16)


def arrange(pick, part):
    devices, _, own, width = part.shape
    rows = 2 * STATIONS
    return pl.pallas_call(
        arrange_kernel,
        out_shape=(
            jax.ShapeDtypeStruct((OUT_DEV, rows, 2 * width), BF16),
            jax.ShapeDtypeStruct((OUT_DEV, 8, LANES), F32),
        ),
        grid=(OUT_DEV,),
        in_specs=[
            pl.BlockSpec(pick.shape, lambda o: (0, 0)),
            pl.BlockSpec((devices, 2, own, width), lambda o: (0, o, 0, 0)),
        ],
        out_specs=(
            pl.BlockSpec((1, rows, 2 * width), lambda o: (o, 0, 0)),
            pl.BlockSpec((1, 8, LANES), lambda o: (o, 0, 0)),
        ),
        compiler_params=pltpu.CompilerParams(vmem_limit_bytes=40 * 2**20),
        cost_estimate=pl.CostEstimate(flops=1_100_000_000, bytes_accessed=4_000_000, transcendentals=0),
        name="arrange",
    )(pick, part)


def tiles_kernel(late, early_ref, power_ref, *refs):
    (pick_refs, part_refs), refs = (refs[: min(late, 1)], refs[min(late, 1) :][:late]), refs[-3:]
    out_ref, left_ref, right_ref = refs
    rows = 2 * STATIONS
    side = 2 * BLOCK
    blocks = STATIONS // BLOCK
    total = power_ref[0]
    if late:
        data = [jnp.concatenate([part_ref[ri] for part_ref in part_refs], axis=0) for ri in range(2)]
        data = jnp.concatenate(data, axis=1)
        total = total + squares(data)
    power = jnp.sum(total) / (STATIONS * 2 * SPECTRA * AVG)
    scale = 1.0 / jnp.full((1, LANES), SPECTRA * AVG * power, F32)
    for r in range(0, rows, 2 * side):
        own = slice(r, r + 2 * side)
        found = early_ref[0, own, :]
        if late:
            found = (jnp.dot(pick_refs[0][own, :], data, preferred_element_type=F32) + found.astype(F32)).astype(BF16)
        right_ref[own, :] = found
        for p in range(2):
            mine = found[p * side : (p + 1) * side]
            at = 2 * r + p * 2 * side
            left_ref[at : at + side, :] = mine
            left_ref[at + side : at + 2 * side, :WIDTH] = mine[:, WIDTH:]
            left_ref[at + side : at + 2 * side, WIDTH:] = -mine[:, :WIDTH]
    for c in range(0, blocks, 2):
        right = right_ref[c * side : (c + 2) * side, :]
        for b in range(c, blocks):
            left = left_ref[b * 2 * side : (b + 1) * 2 * side, :]
            product = lax.dot_general(left, right, NT, preferred_element_type=F32)
            for p in range(2):
                if c + p <= b:
                    tile = b * (b + 1) // 2 + c + p
                    scaled = (product[:, p * side : (p + 1) * side] * scale).astype(BF16)
                    out_ref[0, tile, 0] = scaled[:side]
                    out_ref[0, tile, 1] = scaled[side:]


def tiles(early, power, picks, parts):
    blocks = STATIONS // BLOCK
    pairs = blocks * (blocks + 1) // 2
    side = 2 * BLOCK
    rows = 2 * STATIONS
    return pl.pallas_call(
        functools.partial(tiles_kernel, len(parts)),
        out_shape=jax.ShapeDtypeStruct((OUT_DEV, pairs, 2, side, side), BF16),
        grid=(OUT_DEV,),
        in_specs=[
            pl.BlockSpec((1, rows, 2 * WIDTH), lambda o: (o, 0, 0)),
            pl.BlockSpec((1, 8, LANES), lambda o: (o, 0, 0)),
        ]
        + [pl.BlockSpec(pick.shape, lambda o: (0, 0)) for pick in picks]
        + [pl.BlockSpec((2,) + part.shape[1:], lambda o: (o, 0, 0)) for part in parts],
        out_specs=pl.BlockSpec((1, pairs, 2, side, side), lambda o: (o, 0, 0, 0, 0)),
        scratch_shapes=[
            pltpu.VMEM((2 * rows, 2 * WIDTH), BF16),
            pltpu.VMEM((rows, 2 * WIDTH), BF16),
        ],
        compiler_params=pltpu.CompilerParams(vmem_limit_bytes=40 * 2**20),
        cost_estimate=pl.CostEstimate(flops=4_500_000_000, bytes_accessed=9_000_000, transcendentals=0),
        name="tiles",
    )(early, power, *picks, *parts)


def body(voltages, taps, station_gain, station_order):
    devices = lax.axis_size("ingest")
    streams = 2 * voltages.shape[0]
    blocks = NCHAN // LANES
    outs = 2 * OUT_DEV * devices
    consts = tables(OUT_DEV * devices)
    samples = voltages.reshape(streams, 2, FRAMES * blocks, LANES).transpose(0, 2, 1, 3)
    samples = samples.reshape(streams, FRAMES, 2 * blocks, LANES)
    coeffs = taps.reshape(TAPS, blocks, LANES).transpose(1, 0, 2).reshape(TAPS * blocks, LANES)
    cut = streams - streams // (2 * ROWS) * ROWS
    wanted = (2 * station_order[:, None] + jnp.arange(2, dtype=jnp.int32)).reshape(-1, 1)

    def pick(start, stop, first):
        place = np.arange(devices * (stop - start), dtype=np.int32)
        source = jnp.bitwise_xor(place // (stop - start), first) * streams + start + place % (stop - start)
        return (wanted == source).astype(BF16)

    packed = spectra(samples, coeffs, station_gain, consts, outs, 0, cut)[0]
    packed = packed.reshape(devices, 2 * OUT_DEV, cut, WIDTH)
    packed, station_gain = lax.optimization_barrier((packed, station_gain))
    early = lax.all_to_all(packed, "ingest", split_axis=0, concat_axis=0, tiled=True)
    picks, late = [], []
    if cut < streams:
        sent = spectra(samples, coeffs, station_gain, consts, outs, cut, streams, devices)
        received = {0: sent[0]}
        for k in range(1, devices):
            ready = sent[k]
            if k > WINDOW:
                ready, received[k - WINDOW] = lax.optimization_barrier((ready, received[k - WINDOW]))
            received[k] = lax.ppermute(ready, "ingest", [(i, i ^ k) for i in range(devices)])
        late = [received[k] for k in range(devices)]
        picks = [pick(cut, streams, lax.axis_index("ingest"))]
    rows, power = arrange(pick(0, cut, 0), early)
    return tiles(rows, power, picks, late)


def solution(mesh):
    return jax.shard_map(
        body,
        mesh=mesh,
        in_specs=(P(("band", "ingest"), None, None, None), P(), P("ingest"), P()),
        out_specs=P(("band", "ingest"), None, None, None, None),
        check_vma=False,
    )
```

```python
import functools
import math

import jax
import jax.numpy as jnp
import ml_dtypes
import numpy as np
from jax import lax
from jax.experimental import pallas as pl
from jax.experimental.pallas import tpu as pltpu
from jax.sharding import PartitionSpec as P

STATIONS = 512
NCHAN = 4096
BLOCK = 64
TAPS = 4
SPECTRA = 8
FRAMES = SPECTRA + TAPS - 1
AVG = 32
OUT_DEV = 2
LANES = 128
WIDE = 2 * AVG
WIDTH = SPECTRA * AVG
GROUP = 2
STEP = 8
ROWS = 16
WINDOW = 5
VMEM_LIMIT = 60_000_000
BF16 = jnp.bfloat16
F32 = jnp.float32
NT = (((1,), (1,)), ((), ()))


def split(values):
    high = values.astype(ml_dtypes.bfloat16)
    low = (values - high.astype(np.float64)).astype(ml_dtypes.bfloat16)
    return high, low


def tables(all_out):
    blocks = NCHAN // LANES
    angle = 2.0 * math.pi * (np.outer(np.arange(AVG), np.arange(blocks)) % blocks) / blocks
    cos, sin = np.cos(angle), np.sin(angle)
    stage = np.zeros((2, AVG, blocks, 2))
    stage[0, :, :, 0], stage[0, :, :, 1] = cos, sin
    stage[1, :, :, 0], stage[1, :, :, 1] = -sin, cos
    stage = np.stack(split(stage), axis=1).reshape(4 * AVG, 2 * blocks)
    stage = np.kron(np.eye(GROUP), stage.astype(np.float32))
    angle = 2.0 * math.pi * np.outer(np.arange(AVG), np.arange(LANES)) / NCHAN
    turn = np.stack([np.cos(angle), -np.sin(angle)]).astype(np.float32)
    first = (NCHAN - all_out * AVG) // 2
    bins = first // AVG + np.arange(all_out)
    angle = 2.0 * math.pi * (np.outer(np.arange(LANES), bins) % LANES) / LANES
    cos, sin = np.cos(angle), np.sin(angle)
    last = np.zeros((2, LANES, all_out, 2))
    last[0, :, :, 0], last[0, :, :, 1] = cos, -sin
    last[1, :, :, 0], last[1, :, :, 1] = sin, cos
    beside = max(1, LANES // (2 * all_out))
    last = np.kron(np.eye(beside), last.reshape(2 * LANES, 2 * all_out))
    last = np.concatenate(split(last), axis=1)
    return stage.astype(np.float32), turn, last.astype(np.float32)


def halves(values):
    scaled = values * 65537.0
    high = scaled - (scaled - values)
    return high, values - high


def spectra_kernel(first_stream, partners, outs, gain_ref, *refs):
    frames, refs = refs[:FRAMES], refs[FRAMES:]
    (taps_ref, stage_ref, turn_ref, last_ref), refs = refs[:4], refs[4:]
    out_refs, refs = refs[: max(partners, 1)], refs[max(partners, 1) :]
    (coeff_ref, held_ref), refs = refs[:2], refs[2:]
    groups = STEP // GROUP
    halves_refs, turned_refs = refs[:groups], refs[groups:]
    outer, inner = pl.program_id(0), pl.program_id(1)
    size = GROUP * WIDE
    beside = last_ref.shape[0] // (2 * LANES)
    columns = beside * outs

    @pl.when((outer == 0) & (inner == 0))
    def _():
        for j in range(TAPS):
            rows = taps_ref[pl.ds(j, AVG, stride=TAPS), :]
            for ri in range(2):
                coeff_ref[j, pl.ds(ri, AVG, stride=2), :] = rows

    def filter_rows(g, u, r):
        rows = slice(r, r + 16)
        coeffs = [coeff_ref[j, rows, :] for j in range(TAPS)]
        samples = [ref[g * GROUP + u, 0, rows, :].astype(F32) for ref in frames]
        for m in range(SPECTRA):
            value = coeffs[0] * samples[m]
            for j in range(1, TAPS):
                value = value + coeffs[j] * samples[m + j]
            for part, kept in enumerate(halves(value)):
                row = part * size + u * WIDE + r
                halves_refs[g][row : row + 16, m * LANES : (m + 1) * LANES] = kept

    def first_product(g, start):
        lanes = slice(start * LANES, (start + 2) * LANES)
        table = stage_ref[...]
        return jnp.dot(jnp.concatenate([table, table], axis=1), halves_refs[g][:, lanes], preferred_element_type=F32)

    def first_rest(g, start, section):
        turn_real, turn_imag = turn_ref[0], turn_ref[1]
        for u in range(GROUP):
            pair, place = divmod(u, beside)
            for m in range(start, start + 2):
                at = slice((m - start) * LANES, (m - start + 1) * LANES)
                blocks = [section[(4 * u + i) * AVG : (4 * u + i + 1) * AVG, at] for i in range(4)]
                real, imag = blocks[0] + blocks[1], blocks[2] + blocks[3]
                row = pair * WIDTH + m * AVG
                for ri, value in enumerate((real * turn_real - imag * turn_imag, real * turn_imag + imag * turn_real)):
                    for part, kept in enumerate(halves(value)):
                        lane = ((part * beside + place) * 2 + ri) * LANES
                        turned_refs[g][row : row + AVG, lane : lane + LANES] = kept

    def last_product(g):
        table = last_ref[...]
        rows = jnp.concatenate([turned_refs[g][...], turned_refs[g + 1][...]])
        return jnp.dot(rows, jnp.concatenate([table, table]), preferred_element_type=F32)

    def last_rest(g, product):
        for pair in range(2 * GROUP // beside):
            mine = product[pair * WIDTH : (pair + 1) * WIDTH]
            found = (mine[:, :columns] + mine[:, columns:]).T
            for place in range(beside):
                stream = g * GROUP + pair * beside + place
                factor = gain_ref[(first_stream + outer * ROWS + inner * STEP + stream) // 2]
                factor = factor * (1.0 / (64.0 * math.sqrt(NCHAN)))
                at = pl.multiple_of((inner * STEP + stream) * outs, outs)
                mine_out = found[place * outs : (place + 1) * outs] * factor
                for half in range(WIDTH // LANES):
                    held_ref[half, pl.ds(at, outs), :] = mine_out[:, half * LANES : (half + 1) * LANES]

    waiting = []
    for g in range(groups + 3):
        filters = [(g, u, r) for u in range(GROUP) for r in range(0, WIDE, 16)] if g < groups else []
        units = [(first_product, first_rest, g - 1, start) for start in range(0, SPECTRA, 2)] if 1 <= g <= groups else []
        if 4 <= g and g % 2 == 0:
            units.append((last_product, last_rest, g - 4))
        while filters or units:
            if units:
                product, rest, *job = units.pop(0)
                waiting.append((rest, job, product(*job)))
            for job in filters[:2]:
                filter_rows(*job)
            del filters[:2]
            if len(waiting) > 1 or not units:
                for rest, job, result in waiting[:1]:
                    rest(*job, result)
                del waiting[:1]
    for rest, job, result in waiting:
        rest(*job, result)

    @pl.when(inner == ROWS // STEP - 1)
    def _():
        me = lax.axis_index("ingest") if partners else 0
        each = outs // len(out_refs)
        for k, out_ref in enumerate(out_refs):
            target = jnp.bitwise_xor(me, k) * each if partners else 0
            for q in range(each):
                for half in range(WIDTH // LANES):
                    rows = held_ref[half, pl.ds(target + q, ROWS, stride=outs), :]
                    out_ref[q, :, half * LANES : (half + 1) * LANES] = rows.astype(BF16)


def spectra(voltages, taps, station_gain, consts, outs, start, stop, partners=0):
    stage, turn, last = consts
    groups = STEP // GROUP
    inner = ROWS // STEP
    pieces = max(partners, 1)
    frame_spec = [
        pl.BlockSpec((STEP, 1, WIDE, LANES), functools.partial(lambda j, a, b: (start // STEP + a * inner + b, j, 0, 0), j))
        for j in range(FRAMES)
    ]
    whole = lambda shape: pl.BlockSpec(shape, lambda a, b: (0,) * len(shape))
    return pl.pallas_call(
        functools.partial(spectra_kernel, start, partners, outs),
        out_shape=[jax.ShapeDtypeStruct((outs // pieces, stop - start, WIDTH), BF16)] * pieces,
        grid=((stop - start) // ROWS, inner),
        in_specs=[pl.BlockSpec(memory_space=pltpu.SMEM)]
        + frame_spec
        + [whole(taps.shape), whole(stage.shape), whole(turn.shape), whole(last.shape)],
        out_specs=[pl.BlockSpec((outs // pieces, ROWS, WIDTH), lambda a, b: (0, a, 0))] * pieces,
        scratch_shapes=[
            pltpu.VMEM((TAPS, WIDE, LANES), F32),
            pltpu.VMEM((WIDTH // LANES, ROWS * outs, LANES), F32),
        ]
        + [pltpu.VMEM((2 * GROUP * WIDE, SPECTRA * LANES), F32)] * groups
        + [pltpu.VMEM((2 * GROUP * WIDTH * LANES // last.shape[0], 2 * last.shape[0]), F32)] * groups,
        compiler_params=pltpu.CompilerParams(vmem_limit_bytes=VMEM_LIMIT),
        cost_estimate=pl.CostEstimate(
            flops=(stop - start) * SPECTRA * 12_000_000,
            bytes_accessed=(stop - start) * FRAMES * WIDE * LANES * 4,
            transcendentals=0,
        ),
        name="spectra",
    )(station_gain, *([voltages] * FRAMES), taps, stage, turn, last)


def squares(values):
    values = values.astype(F32)
    values = jnp.sum((values * values).reshape(-1, 8, values.shape[-1]), axis=0)
    return sum(values[:, lane : lane + LANES] for lane in range(0, values.shape[-1], LANES))


def arrange_kernel(pick_ref, part_ref, out_ref, power_ref):
    rows = 2 * STATIONS
    data = jnp.concatenate([part_ref[:, ri].reshape(-1, WIDTH) for ri in range(2)], axis=1)
    power_ref[0] = squares(data)
    for r in range(0, rows, 2 * LANES):
        own = slice(r, r + 2 * LANES)
        out_ref[0, own, :] = jnp.dot(pick_ref[own, :], data, preferred_element_type=F32).astype(BF16)


def arrange(pick, part):
    devices, _, own, width = part.shape
    rows = 2 * STATIONS
    return pl.pallas_call(
        arrange_kernel,
        out_shape=(
            jax.ShapeDtypeStruct((OUT_DEV, rows, 2 * width), BF16),
            jax.ShapeDtypeStruct((OUT_DEV, 8, LANES), F32),
        ),
        grid=(OUT_DEV,),
        in_specs=[
            pl.BlockSpec(pick.shape, lambda o: (0, 0)),
            pl.BlockSpec((devices, 2, own, width), lambda o: (0, o, 0, 0)),
        ],
        out_specs=(
            pl.BlockSpec((1, rows, 2 * width), lambda o: (o, 0, 0)),
            pl.BlockSpec((1, 8, LANES), lambda o: (o, 0, 0)),
        ),
        compiler_params=pltpu.CompilerParams(vmem_limit_bytes=40 * 2**20),
        cost_estimate=pl.CostEstimate(flops=1_100_000_000, bytes_accessed=4_000_000, transcendentals=0),
        name="arrange",
    )(pick, part)


def tiles_kernel(late, early_ref, power_ref, *refs):
    (pick_refs, part_refs), refs = (refs[: min(late, 1)], refs[min(late, 1) :][:late]), refs[-3:]
    out_ref, left_ref, right_ref = refs
    rows = 2 * STATIONS
    side = 2 * BLOCK
    blocks = STATIONS // BLOCK
    total = power_ref[0]
    if late:
        data = [jnp.concatenate([part_ref[ri] for part_ref in part_refs], axis=0) for ri in range(2)]
        data = jnp.concatenate(data, axis=1)
        total = total + squares(data)
    power = jnp.sum(total) / (STATIONS * 2 * SPECTRA * AVG)
    scale = 1.0 / jnp.full((1, LANES), SPECTRA * AVG * power, F32)
    for r in range(0, rows, 2 * side):
        own = slice(r, r + 2 * side)
        found = early_ref[0, own, :]
        if late:
            found = (jnp.dot(pick_refs[0][own, :], data, preferred_element_type=F32) + found.astype(F32)).astype(BF16)
        right_ref[own, :] = found
        for p in range(2):
            mine = found[p * side : (p + 1) * side]
            at = 2 * r + p * 2 * side
            left_ref[at : at + side, :] = mine
            left_ref[at + side : at + 2 * side, :WIDTH] = mine[:, WIDTH:]
            left_ref[at + side : at + 2 * side, WIDTH:] = -mine[:, :WIDTH]
    for c in range(0, blocks, 2):
        right = right_ref[c * side : (c + 2) * side, :]
        for b in range(c, blocks):
            left = left_ref[b * 2 * side : (b + 1) * 2 * side, :]
            product = lax.dot_general(left, right, NT, preferred_element_type=F32)
            for p in range(2):
                if c + p <= b:
                    tile = b * (b + 1) // 2 + c + p
                    scaled = (product[:, p * side : (p + 1) * side] * scale).astype(BF16)
                    out_ref[0, tile, 0] = scaled[:side]
                    out_ref[0, tile, 1] = scaled[side:]


def tiles(early, power, picks, parts):
    blocks = STATIONS // BLOCK
    pairs = blocks * (blocks + 1) // 2
    side = 2 * BLOCK
    rows = 2 * STATIONS
    return pl.pallas_call(
        functools.partial(tiles_kernel, len(parts)),
        out_shape=jax.ShapeDtypeStruct((OUT_DEV, pairs, 2, side, side), BF16),
        grid=(OUT_DEV,),
        in_specs=[
            pl.BlockSpec((1, rows, 2 * WIDTH), lambda o: (o, 0, 0)),
            pl.BlockSpec((1, 8, LANES), lambda o: (o, 0, 0)),
        ]
        + [pl.BlockSpec(pick.shape, lambda o: (0, 0)) for pick in picks]
        + [pl.BlockSpec((2,) + part.shape[1:], lambda o: (o, 0, 0)) for part in parts],
        out_specs=pl.BlockSpec((1, pairs, 2, side, side), lambda o: (o, 0, 0, 0, 0)),
        scratch_shapes=[
            pltpu.VMEM((2 * rows, 2 * WIDTH), BF16),
            pltpu.VMEM((rows, 2 * WIDTH), BF16),
        ],
        compiler_params=pltpu.CompilerParams(vmem_limit_bytes=40 * 2**20),
        cost_estimate=pl.CostEstimate(flops=4_500_000_000, bytes_accessed=9_000_000, transcendentals=0),
        name="tiles",
    )(early, power, *picks, *parts)


def body(voltages, taps, station_gain, station_order):
    devices = lax.axis_size("ingest")
    streams = 2 * voltages.shape[0]
    blocks = NCHAN // LANES
    outs = 2 * OUT_DEV * devices
    consts = tables(OUT_DEV * devices)
    samples = voltages.reshape(streams, 2, FRAMES * blocks, LANES).transpose(0, 2, 1, 3)
    samples = samples.reshape(streams, FRAMES, 2 * blocks, LANES)
    coeffs = taps.reshape(TAPS, blocks, LANES).transpose(1, 0, 2).reshape(TAPS * blocks, LANES)
    cut = streams - streams // (2 * ROWS) * ROWS
    wanted = (2 * station_order[:, None] + jnp.arange(2, dtype=jnp.int32)).reshape(-1, 1)

    def pick(start, stop, first):
        place = np.arange(devices * (stop - start), dtype=np.int32)
        source = jnp.bitwise_xor(place // (stop - start), first) * streams + start + place % (stop - start)
        return (wanted == source).astype(BF16)

    packed = spectra(samples, coeffs, station_gain, consts, outs, 0, cut)[0]
    packed = packed.reshape(devices, 2 * OUT_DEV, cut, WIDTH)
    packed, station_gain = lax.optimization_barrier((packed, station_gain))
    early = lax.all_to_all(packed, "ingest", split_axis=0, concat_axis=0, tiled=True)
    picks, late = [], []
    if cut < streams:
        sent = spectra(samples, coeffs, station_gain, consts, outs, cut, streams, devices)
        received = {0: sent[0]}
        for k in range(1, devices):
            ready = sent[k]
            if k > WINDOW:
                ready, received[k - WINDOW] = lax.optimization_barrier((ready, received[k - WINDOW]))
            received[k] = lax.ppermute(ready, "ingest", [(i, i ^ k) for i in range(devices)])
        late = [received[k] for k in range(devices)]
        picks = [pick(cut, streams, lax.axis_index("ingest"))]
    rows, power = arrange(pick(0, cut, 0), early)
    return tiles(rows, power, picks, late)


def solution(mesh):
    return jax.shard_map(
        body,
        mesh=mesh,
        in_specs=(P(("band", "ingest"), None, None, None), P(), P("ingest"), P()),
        out_specs=P(("band", "ingest"), None, None, None, None),
        check_vma=False,
    )
```

```python
import functools
import math

import jax
import jax.numpy as jnp
import ml_dtypes
import numpy as np
from jax import lax
from jax.experimental import pallas as pl
from jax.experimental.pallas import tpu as pltpu
from jax.sharding import PartitionSpec as P

STATIONS = 512
NCHAN = 4096
BLOCK = 64
TAPS = 4
SPECTRA = 8
FRAMES = SPECTRA + TAPS - 1
AVG = 32
OUT_DEV = 2
LANES = 128
WIDE = 2 * AVG
WIDTH = SPECTRA * AVG
GROUP = 2
STEP = 8
ROWS = 16
WINDOW = 5
VMEM_LIMIT = 60_000_000
BF16 = jnp.bfloat16
F32 = jnp.float32
NT = (((1,), (1,)), ((), ()))


def split(values):
    high = values.astype(ml_dtypes.bfloat16)
    low = (values - high.astype(np.float64)).astype(ml_dtypes.bfloat16)
    return high, low


def tables(all_out):
    blocks = NCHAN // LANES
    angle = 2.0 * math.pi * (np.outer(np.arange(AVG), np.arange(blocks)) % blocks) / blocks
    cos, sin = np.cos(angle), np.sin(angle)
    stage = np.zeros((2, AVG, blocks, 2))
    stage[0, :, :, 0], stage[0, :, :, 1] = cos, sin
    stage[1, :, :, 0], stage[1, :, :, 1] = -sin, cos
    stage = np.stack(split(stage), axis=1).reshape(4 * AVG, 2 * blocks)
    stage = np.kron(np.eye(GROUP), stage.astype(np.float32))
    angle = 2.0 * math.pi * np.outer(np.arange(AVG), np.arange(LANES)) / NCHAN
    turn = np.stack([np.cos(angle), -np.sin(angle)]).astype(np.float32)
    first = (NCHAN - all_out * AVG) // 2
    bins = first // AVG + np.arange(all_out)
    angle = 2.0 * math.pi * (np.outer(np.arange(LANES), bins) % LANES) / LANES
    cos, sin = np.cos(angle), np.sin(angle)
    last = np.zeros((2, LANES, all_out, 2))
    last[0, :, :, 0], last[0, :, :, 1] = cos, -sin
    last[1, :, :, 0], last[1, :, :, 1] = sin, cos
    beside = max(1, LANES // (2 * all_out))
    last = np.kron(np.eye(beside), last.reshape(2 * LANES, 2 * all_out))
    last = np.concatenate(split(last), axis=1)
    return stage.astype(np.float32), turn, last.astype(np.float32)


def halves(values):
    scaled = values * 65537.0
    high = scaled - (scaled - values)
    return high, values - high


def spectra_kernel(first_stream, partners, outs, gain_ref, *refs):
    frames, refs = refs[:FRAMES], refs[FRAMES:]
    (taps_ref, stage_ref, turn_ref, last_ref), refs = refs[:4], refs[4:]
    out_refs, refs = refs[: max(partners, 1)], refs[max(partners, 1) :]
    (coeff_ref, held_ref), refs = refs[:2], refs[2:]
    groups = STEP // GROUP
    halves_refs, turned_refs = refs[:groups], refs[groups:]
    outer, inner = pl.program_id(0), pl.program_id(1)
    size = GROUP * WIDE
    beside = last_ref.shape[0] // (2 * LANES)
    columns = beside * outs

    @pl.when((outer == 0) & (inner == 0))
    def _():
        for j in range(TAPS):
            rows = taps_ref[pl.ds(j, AVG, stride=TAPS), :]
            for ri in range(2):
                coeff_ref[j, pl.ds(ri, AVG, stride=2), :] = rows

    def filter_rows(g, u, r):
        rows = slice(r, r + 16)
        coeffs = [coeff_ref[j, rows, :] for j in range(TAPS)]
        samples = [ref[g * GROUP + u, 0, rows, :].astype(F32) for ref in frames]
        for m in range(SPECTRA):
            value = coeffs[0] * samples[m]
            for j in range(1, TAPS):
                value = value + coeffs[j] * samples[m + j]
            for part, kept in enumerate(halves(value)):
                row = part * size + u * WIDE + r
                halves_refs[g][row : row + 16, m * LANES : (m + 1) * LANES] = kept

    def first_product(g, start):
        lanes = slice(start * LANES, (start + 2) * LANES)
        table = stage_ref[...]
        return jnp.dot(jnp.concatenate([table, table], axis=1), halves_refs[g][:, lanes], preferred_element_type=F32)

    def first_rest(g, start, section):
        turn_real, turn_imag = turn_ref[0], turn_ref[1]
        for u in range(GROUP):
            pair, place = divmod(u, beside)
            for m in range(start, start + 2):
                at = slice((m - start) * LANES, (m - start + 1) * LANES)
                blocks = [section[(4 * u + i) * AVG : (4 * u + i + 1) * AVG, at] for i in range(4)]
                real, imag = blocks[0] + blocks[1], blocks[2] + blocks[3]
                row = pair * WIDTH + m * AVG
                for ri, value in enumerate((real * turn_real - imag * turn_imag, real * turn_imag + imag * turn_real)):
                    for part, kept in enumerate(halves(value)):
                        lane = ((part * beside + place) * 2 + ri) * LANES
                        turned_refs[g][row : row + AVG, lane : lane + LANES] = kept

    def last_product(g, pair):
        rows = slice(pair * WIDTH, (pair + 1) * WIDTH)
        table = last_ref[...]
        return jnp.dot(turned_refs[g][rows, :], jnp.concatenate([table, table]), preferred_element_type=F32)

    def last_rest(g, pair, product):
        found = (product[:, :columns] + product[:, columns:]).T
        for place in range(beside):
            stream = g * GROUP + pair * beside + place
            factor = gain_ref[(first_stream + outer * ROWS + inner * STEP + stream) // 2]
            factor = factor * (1.0 / (64.0 * math.sqrt(NCHAN)))
            at = pl.multiple_of((inner * STEP + stream) * outs, outs)
            mine = found[place * outs : (place + 1) * outs] * factor
            for half in range(WIDTH // LANES):
                held_ref[half, pl.ds(at, outs), :] = mine[:, half * LANES : (half + 1) * LANES]

    waiting = []
    for g in range(groups + 3):
        filters = [(g, u, r) for u in range(GROUP) for r in range(0, WIDE, 16)] if g < groups else []
        units = [(first_product, first_rest, g - 1, start) for start in range(0, SPECTRA, 2)] if 1 <= g <= groups else []
        if 3 <= g:
            units += [(last_product, last_rest, g - 3, pair) for pair in range(GROUP // beside)]
        while filters or units:
            if units:
                product, rest, *job = units.pop(0)
                waiting.append((rest, job, product(*job)))
            for job in filters[:2]:
                filter_rows(*job)
            del filters[:2]
            if len(waiting) > 1 or not units:
                for rest, job, result in waiting[:1]:
                    rest(*job, result)
                del waiting[:1]
    for rest, job, result in waiting:
        rest(*job, result)

    @pl.when(inner == ROWS // STEP - 1)
    def _():
        me = lax.axis_index("ingest") if partners else 0
        each = outs // len(out_refs)
        for k, out_ref in enumerate(out_refs):
            target = jnp.bitwise_xor(me, k) * each if partners else 0
            for q in range(each):
                for half in range(WIDTH // LANES):
                    rows = held_ref[half, pl.ds(target + q, ROWS, stride=outs), :]
                    out_ref[q, :, half * LANES : (half + 1) * LANES] = rows.astype(BF16)


def spectra(voltages, taps, station_gain, consts, outs, start, stop, partners=0):
    stage, turn, last = consts
    groups = STEP // GROUP
    inner = ROWS // STEP
    pieces = max(partners, 1)
    frame_spec = [
        pl.BlockSpec((STEP, 1, WIDE, LANES), functools.partial(lambda j, a, b: (start // STEP + a * inner + b, j, 0, 0), j))
        for j in range(FRAMES)
    ]
    whole = lambda shape: pl.BlockSpec(shape, lambda a, b: (0,) * len(shape))
    return pl.pallas_call(
        functools.partial(spectra_kernel, start, partners, outs),
        out_shape=[jax.ShapeDtypeStruct((outs // pieces, stop - start, WIDTH), BF16)] * pieces,
        grid=((stop - start) // ROWS, inner),
        in_specs=[pl.BlockSpec(memory_space=pltpu.SMEM)]
        + frame_spec
        + [whole(taps.shape), whole(stage.shape), whole(turn.shape), whole(last.shape)],
        out_specs=[pl.BlockSpec((outs // pieces, ROWS, WIDTH), lambda a, b: (0, a, 0))] * pieces,
        scratch_shapes=[
            pltpu.VMEM((TAPS, WIDE, LANES), F32),
            pltpu.VMEM((WIDTH // LANES, ROWS * outs, LANES), F32),
        ]
        + [pltpu.VMEM((2 * GROUP * WIDE, SPECTRA * LANES), F32)] * groups
        + [pltpu.VMEM((2 * GROUP * WIDTH * LANES // last.shape[0], 2 * last.shape[0]), F32)] * groups,
        compiler_params=pltpu.CompilerParams(vmem_limit_bytes=VMEM_LIMIT),
        cost_estimate=pl.CostEstimate(
            flops=(stop - start) * SPECTRA * 12_000_000,
            bytes_accessed=(stop - start) * FRAMES * WIDE * LANES * 4,
            transcendentals=0,
        ),
        name="spectra",
    )(station_gain, *([voltages] * FRAMES), taps, stage, turn, last)


def squares(values):
    values = values.astype(F32)
    values = jnp.sum((values * values).reshape(-1, 8, values.shape[-1]), axis=0)
    return sum(values[:, lane : lane + LANES] for lane in range(0, values.shape[-1], LANES))


def arrange_kernel(pick_ref, part_ref, out_ref, power_ref):
    rows = 2 * STATIONS
    data = jnp.concatenate([part_ref[:, ri].reshape(-1, WIDTH) for ri in range(2)], axis=1)
    power_ref[0] = squares(data)
    for r in range(0, rows, 2 * LANES):
        own = slice(r, r + 2 * LANES)
        out_ref[0, own, :] = jnp.dot(pick_ref[own, :], data, preferred_element_type=F32).astype(BF16)


def arrange(pick, part):
    devices, _, own, width = part.shape
    rows = 2 * STATIONS
    return pl.pallas_call(
        arrange_kernel,
        out_shape=(
            jax.ShapeDtypeStruct((OUT_DEV, rows, 2 * width), BF16),
            jax.ShapeDtypeStruct((OUT_DEV, 8, LANES), F32),
        ),
        grid=(OUT_DEV,),
        in_specs=[
            pl.BlockSpec(pick.shape, lambda o: (0, 0)),
            pl.BlockSpec((devices, 2, own, width), lambda o: (0, o, 0, 0)),
        ],
        out_specs=(
            pl.BlockSpec((1, rows, 2 * width), lambda o: (o, 0, 0)),
            pl.BlockSpec((1, 8, LANES), lambda o: (o, 0, 0)),
        ),
        compiler_params=pltpu.CompilerParams(vmem_limit_bytes=40 * 2**20),
        cost_estimate=pl.CostEstimate(flops=1_100_000_000, bytes_accessed=4_000_000, transcendentals=0),
        name="arrange",
    )(pick, part)


def tiles_kernel(late, early_ref, power_ref, *refs):
    (pick_refs, part_refs), refs = (refs[: min(late, 1)], refs[min(late, 1) :][:late]), refs[-3:]
    out_ref, left_ref, right_ref = refs
    rows = 2 * STATIONS
    side = 2 * BLOCK
    blocks = STATIONS // BLOCK
    total = power_ref[0]
    if late:
        data = [jnp.concatenate([part_ref[ri] for part_ref in part_refs], axis=0) for ri in range(2)]
        data = jnp.concatenate(data, axis=1)
        total = total + squares(data)
    power = jnp.sum(total) / (STATIONS * 2 * SPECTRA * AVG)
    scale = 1.0 / jnp.full((1, LANES), SPECTRA * AVG * power, F32)
    for r in range(0, rows, 2 * side):
        own = slice(r, r + 2 * side)
        found = early_ref[0, own, :]
        if late:
            found = (jnp.dot(pick_refs[0][own, :], data, preferred_element_type=F32) + found.astype(F32)).astype(BF16)
        right_ref[own, :] = found
        for p in range(2):
            mine = found[p * side : (p + 1) * side]
            at = 2 * r + p * 2 * side
            left_ref[at : at + side, :] = mine
            left_ref[at + side : at + 2 * side, :WIDTH] = mine[:, WIDTH:]
            left_ref[at + side : at + 2 * side, WIDTH:] = -mine[:, :WIDTH]
    for c in range(0, blocks, 2):
        right = right_ref[c * side : (c + 2) * side, :]
        for b in range(c, blocks):
            left = left_ref[b * 2 * side : (b + 1) * 2 * side, :]
            product = lax.dot_general(left, right, NT, preferred_element_type=F32)
            for p in range(2):
                if c + p <= b:
                    tile = b * (b + 1) // 2 + c + p
                    scaled = (product[:, p * side : (p + 1) * side] * scale).astype(BF16)
                    out_ref[0, tile, 0] = scaled[:side]
                    out_ref[0, tile, 1] = scaled[side:]


def tiles(early, power, picks, parts):
    blocks = STATIONS // BLOCK
    pairs = blocks * (blocks + 1) // 2
    side = 2 * BLOCK
    rows = 2 * STATIONS
    return pl.pallas_call(
        functools.partial(tiles_kernel, len(parts)),
        out_shape=jax.ShapeDtypeStruct((OUT_DEV, pairs, 2, side, side), BF16),
        grid=(OUT_DEV,),
        in_specs=[
            pl.BlockSpec((1, rows, 2 * WIDTH), lambda o: (o, 0, 0)),
            pl.BlockSpec((1, 8, LANES), lambda o: (o, 0, 0)),
        ]
        + [pl.BlockSpec(pick.shape, lambda o: (0, 0)) for pick in picks]
        + [pl.BlockSpec((2,) + part.shape[1:], lambda o: (o, 0, 0)) for part in parts],
        out_specs=pl.BlockSpec((1, pairs, 2, side, side), lambda o: (o, 0, 0, 0, 0)),
        scratch_shapes=[
            pltpu.VMEM((2 * rows, 2 * WIDTH), BF16),
            pltpu.VMEM((rows, 2 * WIDTH), BF16),
        ],
        compiler_params=pltpu.CompilerParams(vmem_limit_bytes=40 * 2**20),
        cost_estimate=pl.CostEstimate(flops=4_500_000_000, bytes_accessed=9_000_000, transcendentals=0),
        name="tiles",
    )(early, power, *picks, *parts)


def body(voltages, taps, station_gain, station_order):
    devices = lax.axis_size("ingest")
    streams = 2 * voltages.shape[0]
    blocks = NCHAN // LANES
    outs = 2 * OUT_DEV * devices
    consts = tables(OUT_DEV * devices)
    samples = voltages.reshape(streams, 2, FRAMES * blocks, LANES).transpose(0, 2, 1, 3)
    samples = samples.reshape(streams, FRAMES, 2 * blocks, LANES)
    coeffs = taps.reshape(TAPS, blocks, LANES).transpose(1, 0, 2).reshape(TAPS * blocks, LANES)
    cut = streams - streams // (2 * ROWS) * ROWS
    wanted = (2 * station_order[:, None] + jnp.arange(2, dtype=jnp.int32)).reshape(-1, 1)

    def pick(start, stop, first):
        place = np.arange(devices * (stop - start), dtype=np.int32)
        source = jnp.bitwise_xor(place // (stop - start), first) * streams + start + place % (stop - start)
        return (wanted == source).astype(BF16)

    packed = spectra(samples, coeffs, station_gain, consts, outs, 0, cut)[0]
    packed = packed.reshape(devices, 2 * OUT_DEV, cut, WIDTH)
    packed, station_gain = lax.optimization_barrier((packed, station_gain))
    early = lax.all_to_all(packed, "ingest", split_axis=0, concat_axis=0, tiled=True)
    picks, late = [], []
    if cut < streams:
        sent = spectra(samples, coeffs, station_gain, consts, outs, cut, streams, devices)
        received = {0: sent[0]}
        for k in range(1, devices):
            ready = sent[k]
            if k > WINDOW:
                ready, received[k - WINDOW] = lax.optimization_barrier((ready, received[k - WINDOW]))
            received[k] = lax.ppermute(ready, "ingest", [(i, i ^ k) for i in range(devices)])
        late = [received[k] for k in range(devices)]
        picks = [pick(cut, streams, lax.axis_index("ingest"))]
    rows, power = arrange(pick(0, cut, 0), early)
    return tiles(rows, power, picks, late)


def solution(mesh):
    return jax.shard_map(
        body,
        mesh=mesh,
        in_specs=(P(("band", "ingest"), None, None, None), P(), P("ingest"), P()),
        out_specs=P(("band", "ingest"), None, None, None, None),
        check_vma=False,
    )
```
